32 devices in a mesh: dp: 8 (over y, x, core), tensor: 4 (over z).
Axes of the slice: x: 2, y: 2, z: 4, core: 2. Of those that a mesh axis runs over, the one named last changes fastest.
Arguments:
- x_tokens: bfloat16 [512, 8192], P('dp', 'tensor'), may hold values from -6 to 6
- sign_bits: int32 [8192], P('tensor'), may hold values from 0 to 1
- weight: bfloat16 [8192, 28672], P('tensor', 'dp'), may hold values from -0.0625 to 0.0625
- upstream: bfloat16 [512, 28672], P('tensor', 'dp'), may hold values from -0.25 to 0.25
Outputs:
- projected: bfloat16 [512, 28672], P('tensor', 'dp')
- weight_grad: float32 [8192, 28672], P('tensor', 'dp')
The draws below stay inside these ranges and needn't reach their ends.
All inputs are finite; a program needn't handle non-finite values.
Results may differ from the reference program's by a relative error of at most 0.028.
Values may be sent and summed in bfloat16 or wider, within the bound.
No kernel may reach another device: no remote copies, remote signals or barrier semaphores. Data moves between devices by JAX's collectives and lax.ppermute only.
A program may use at most 128 MiB of HBM per device.

```python
import math
import jax
import jax.numpy as jnp
from jax import lax

D = 8192
FFW = 28672
TOKENS = 512
N_TENSOR = 4


def plant(values, stream_key, smallest, top_value):
    longest = values.shape.index(max(values.shape))
    spots = []
    for shift in (0, 1):
        where = [jax.random.randint(jax.random.fold_in(stream_key, axis), (), 0, length) for axis, length in enumerate(values.shape)]
        where[longest] = (where[longest] + shift) % values.shape[longest]
        spots.append(tuple(where))
    return values.at[spots[0]].set(smallest).at[spots[1]].set(top_value)


def levels(stream_key, shape, pieces, low, top_value):
    def one(axis_at, parts):
        heights = jax.random.uniform(jax.random.fold_in(jax.random.fold_in(stream_key, 6), axis_at), (parts,), jnp.float32, low / len(pieces), top_value / len(pieces))
        return jnp.repeat(jnp.exp(heights), shape[axis_at] // parts).reshape((-1,) + (1,) * (len(shape) - axis_at - 1))

    gain = one(*pieces[0])
    for cut in pieces[1:]:
        gain = gain * one(*cut)
    return gain


def noise(rng, extent, width, bound, split=(), held_as=jnp.bfloat16):
    values = width * jax.random.normal(rng, extent, jnp.float32)
    if split:
        values = values * levels(rng, extent, split, -0.22, 0.18)
    return jnp.clip(values, -bound, bound).astype(held_as)


def setup_inputs(seed: int = 0) -> dict:
    key_of = jax.random.split(jax.random.key(seed), 5)
    return {
        "x_tokens": noise(key_of[0], (TOKENS, D), 1.0, 6.0, ((0, 8), (1, 4))),
        "sign_bits": plant(jax.random.randint(key_of[1], (D,), 0, 2), jax.random.fold_in(key_of[1], 1), 0, 1).astype(jnp.int32),
        "weight": noise(key_of[2], (D, FFW), D ** -0.5, 0.0625, ((0, 4), (1, 8))),
        "upstream": noise(key_of[3], (TOKENS, FFW), TOKENS ** -0.5, 0.25, ((0, 4), (1, 8))),
    }


def hadamard(order):
    row_ids = jnp.arange(order, dtype=jnp.int32)[:, None]
    col_ids = jnp.arange(order, dtype=jnp.int32)[None, :]
    common = row_ids & col_ids
    parity = jnp.zeros((order, order), jnp.int32)
    for section_bit in range(max(order.bit_length() - 1, 0)):
        parity = parity + (common >> section_bit & 1)
    return (1 - 2 * (parity % 2)).astype(jnp.float32)

def reference(x_tokens, sign_bits, weight, upstream):
    groups = N_TENSOR
    panel_width = D // N_TENSOR
    column_sign = (1 - 2 * sign_bits).astype(jnp.float32)
    signed = x_tokens.astype(jnp.float32) * column_sign[None, :]
    blocks = signed.reshape(TOKENS, groups, panel_width)
    inner = jnp.einsum('rtd,de->rte', blocks, hadamard(panel_width), precision=lax.Precision.HIGHEST)
    outer = jnp.einsum('rtd,st->rsd', inner, hadamard(groups), precision=lax.Precision.HIGHEST)
    factor = 1.0 / math.sqrt(D)
    quantized = (outer.reshape(TOKENS, D) * factor).astype(jnp.bfloat16)
    q_blocks = quantized.reshape(TOKENS, groups, panel_width).transpose(1, 0, 2)
    w_blocks = weight.reshape(groups, panel_width, FFW)

    def add_group(running, pair):
        partial_value = jnp.dot(pair[0], pair[1], preferred_element_type=jnp.float32).astype(jnp.bfloat16)
        partial_value = lax.optimization_barrier(partial_value)
        return (running + partial_value.astype(jnp.float32), None)
    summed, _ = lax.scan(add_group, jnp.zeros((TOKENS, FFW), jnp.float32), (q_blocks, w_blocks))
    projected = summed.astype(jnp.bfloat16)
    weight_grad = lax.dot_general(quantized, upstream, (((0,), (0,)), ((), ())), preferred_element_type=jnp.float32)
    return (projected, weight_grad)
```

```python
import functools
import math

import jax
import jax.numpy as jnp
from jax import lax
from jax.experimental import pallas as pl
from jax.experimental.pallas import tpu as pltpu
from jax.sharding import PartitionSpec as P

MIB = 1 << 20


def parity_sign(bits):
    folded = bits ^ (bits >> 4)
    folded = folded ^ (folded >> 2)
    folded = folded ^ (folded >> 1)
    return (1 - 2 * (folded & 1)).astype(jnp.float32)


def hadamard(order):
    row_ids = jnp.arange(order, dtype=jnp.int32)[:, None]
    col_ids = jnp.arange(order, dtype=jnp.int32)[None, :]
    common = row_ids & col_ids
    parity = jnp.zeros((order, order), jnp.int32)
    for section_bit in range(max(order.bit_length() - 1, 0)):
        parity = parity + (common >> section_bit & 1)
    return (1 - 2 * (parity % 2)).astype(jnp.bfloat16)


def butterfly(parts):
    stride = 1
    parts = list(parts)
    while stride < len(parts):
        for low in range(len(parts)):
            if not low & stride:
                a, b = parts[low], parts[low | stride]
                parts[low], parts[low | stride] = a + b, a - b
        stride *= 2
    return parts


def rotate_kernel(groups, core_order, factor, z_ref, h_ref, *refs):
    pieces, outs = refs[:groups], refs[groups:]
    z = z_ref[0]
    width = pieces[0].shape[1]
    h = h_ref[...]
    rotated = []
    for i, piece in enumerate(pieces):
        sign = parity_sign(z & i)
        chunks = [
            jnp.dot(
                piece[:, j * core_order : (j + 1) * core_order],
                h,
                preferred_element_type=jnp.float32,
            )
            * sign
            for j in range(width // core_order)
        ]
        rotated.append(butterfly(chunks))
    for j in range(width // core_order):
        panel = butterfly([r[j] for r in rotated])
        for m in range(groups):
            scale = parity_sign((z ^ m) & z) * factor
            outs[m][:, j * core_order : (j + 1) * core_order] = (panel[m] * scale).astype(
                jnp.bfloat16
            )


def rotate(z, pieces):
    groups = len(pieces)
    rows, width = pieces[0].shape
    core_order = min(256, width)
    vmem = pl.BlockSpec(memory_space=pltpu.VMEM)
    return pl.pallas_call(
        functools.partial(
            rotate_kernel, groups, core_order, 1.0 / math.sqrt(width * groups)
        ),
        out_shape=[jax.ShapeDtypeStruct((rows, width), jnp.bfloat16)] * groups,
        in_specs=[pl.BlockSpec(memory_space=pltpu.SMEM)] + [vmem] * (groups + 1),
        out_specs=[vmem] * groups,
        name="rotate",
    )(z.reshape(1), hadamard(core_order), *pieces)


def place_kernel(span, group_rows, where_ref, *refs):
    pieces, out = refs[:-1], refs[-1]
    for n, piece in enumerate(pieces):
        for i in range(piece.shape[0] // group_rows):
            start = pl.multiple_of(where_ref[n, i], group_rows)
            out[pl.ds(start, group_rows), :] = piece[i * group_rows : (i + 1) * group_rows, :]


def place(pieces, starts, group_rows):
    total = sum(p.shape[0] for p in pieces)
    width = pieces[0].shape[1]
    if group_rows % 16:
        groups = total // group_rows
        stacked = jnp.concatenate(pieces).reshape(groups, group_rows, width)
        order = jnp.zeros((groups,), jnp.int32).at[starts.reshape(-1) // group_rows].set(
            jnp.arange(groups, dtype=jnp.int32)
        )
        return jnp.take(stacked, order, axis=0).reshape(total, width)
    vmem = pl.BlockSpec(memory_space=pltpu.VMEM)
    return pl.pallas_call(
        functools.partial(place_kernel, total, group_rows),
        out_shape=jax.ShapeDtypeStruct((total, width), jnp.bfloat16),
        in_specs=[pl.BlockSpec(memory_space=pltpu.SMEM)] + [vmem] * len(pieces),
        out_specs=vmem,
        compiler_params=pltpu.CompilerParams(vmem_limit_bytes=32 * MIB),
        name="place",
    )(starts, *pieces)


def project_kernel(q_ref, w_ref, out_ref):
    out_ref[...] = jnp.dot(
        q_ref[...], w_ref[...], preferred_element_type=jnp.float32
    ).astype(out_ref.dtype)


def project(q, weight, first, width):
    tile = next((t for t in (512, 256, 128) if width % t == 0 and first % t == 0), width)
    tokens, depth = q.shape
    return pl.pallas_call(
        project_kernel,
        out_shape=jax.ShapeDtypeStruct((tokens, width), jnp.bfloat16),
        grid=(width // tile,),
        in_specs=[
            pl.BlockSpec((tokens, depth), lambda n: (0, 0)),
            pl.BlockSpec((depth, tile), lambda n: (0, n + first // tile)),
        ],
        out_specs=pl.BlockSpec((tokens, tile), lambda n: (0, n)),
        compiler_params=pltpu.CompilerParams(vmem_limit_bytes=48 * MIB),
        cost_estimate=pl.CostEstimate(
            flops=2 * tokens * depth * width,
            bytes_accessed=2 * (tokens * depth + depth * width + tokens * width),
            transcendentals=0,
        ),
        name="project",
    )(q, weight)


def swap(block, axis, mask):
    count = lax.axis_size(axis)
    return lax.ppermute(block, axis, [(i, i ^ mask) for i in range(count)])


def gather_rows(block, axis, orders):
    step = block.shape[0] // len(orders)
    held = []
    for part, order in enumerate(orders):
        have = [(0, part, block[part * step : (part + 1) * step])]
        for bit in order:
            have += [(mask | bit, part, swap(array, axis, bit)) for mask, part, array in have]
        held += have
    return held


def shift(block, axis, pairs):
    return lax.ppermute(block, axis, pairs)


def scatter_sum(partial, z, groups):
    rows = partial.shape[0] // groups

    def block(index):
        return lax.dynamic_slice_in_dim(
            partial, jnp.clip(index, 0, groups - 1) * rows, rows, axis=0
        ).astype(jnp.float32)

    up = down = None
    for s in range(1, groups):
        send_up, send_down = block(z + groups - s), block(z - groups + s)
        if s > 1:
            send_up, send_down = send_up + up, send_down + down
        up = shift(
            send_up.astype(jnp.bfloat16), "tensor", [(i, i + 1) for i in range(s)]
        ).astype(jnp.float32)
        down = shift(
            send_down.astype(jnp.bfloat16),
            "tensor",
            [(i, i - 1) for i in range(groups - s, groups)],
        ).astype(jnp.float32)
    return (block(z) + up + down).astype(jnp.bfloat16)


def per_device(x_tokens, sign_bits, weight, upstream):
    groups = lax.axis_size("tensor")
    ways = lax.axis_size("dp")
    z = lax.axis_index("tensor")
    d = lax.axis_index("dp")
    rows, panel = x_tokens.shape
    hidden = weight.shape[1]
    group_rows = rows // groups

    all_up = lax.all_gather(upstream, "tensor", axis=0, tiled=True)

    column_sign = (1 - 2 * sign_bits).astype(jnp.bfloat16)
    signed = x_tokens * column_sign[None, :]
    pieces = []
    for m in range(groups):
        piece = lax.dynamic_slice_in_dim(signed, (z ^ m) * group_rows, group_rows, axis=0)
        pieces.append(swap(piece, "tensor", m) if m else piece)
    turned = rotate(z, pieces)
    back = [swap(t, "tensor", m) if m else t for m, t in enumerate(turned)]

    bits = [1 << b for b in range(1, ways.bit_length() - 1)]
    half = len(bits) // 2
    orders = [bits + [1], bits[half:] + bits[:half] + [1]]
    own = jnp.concatenate(back)
    held = gather_rows(own, "dp", orders)
    per_part = groups // len(orders)
    starts = jnp.stack(
        [
            jnp.stack(
                [(d ^ mask) * rows + (z ^ (part * per_part + i)) * group_rows for i in range(per_part)]
            )
            for mask, part, _ in held
        ]
    ).astype(jnp.int32)
    q = place([array for _, _, array in held], starts, group_rows)

    cuts = 2 if hidden % 512 == 0 else 1
    width = hidden // cuts
    projected = jnp.concatenate(
        [
            scatter_sum(project(q, weight, c * width, width), z, groups)
            for c in range(cuts)
        ],
        axis=1,
    )
    weight_grad = lax.dot_general(
        q, all_up, (((0,), (0,)), ((), ())), preferred_element_type=jnp.float32
    )
    return (projected, weight_grad)


def solution(mesh):
    in_specs = (P("dp", "tensor"), P("tensor"), P("tensor", "dp"), P("tensor", "dp"))
    out_specs = (P("tensor", "dp"), P("tensor", "dp"))
    return jax.shard_map(
        per_device, mesh=mesh, in_specs=in_specs, out_specs=out_specs, check_vma=False
    )
```

```python
import functools
import math

import jax
import jax.numpy as jnp
from jax import lax
from jax.experimental import pallas as pl
from jax.experimental.pallas import tpu as pltpu
from jax.sharding import PartitionSpec as P

MIB = 1 << 20


def parity_sign(bits):
    folded = bits ^ (bits >> 4)
    folded = folded ^ (folded >> 2)
    folded = folded ^ (folded >> 1)
    return (1 - 2 * (folded & 1)).astype(jnp.float32)


def hadamard(order):
    row_ids = jnp.arange(order, dtype=jnp.int32)[:, None]
    col_ids = jnp.arange(order, dtype=jnp.int32)[None, :]
    common = row_ids & col_ids
    parity = jnp.zeros((order, order), jnp.int32)
    for section_bit in range(max(order.bit_length() - 1, 0)):
        parity = parity + (common >> section_bit & 1)
    return (1 - 2 * (parity % 2)).astype(jnp.bfloat16)


def butterfly(parts):
    stride = 1
    parts = list(parts)
    while stride < len(parts):
        for low in range(len(parts)):
            if not low & stride:
                a, b = parts[low], parts[low | stride]
                parts[low], parts[low | stride] = a + b, a - b
        stride *= 2
    return parts


def sign_kernel(groups, x_ref, bits_ref, *outs):
    z = lax.axis_index("tensor")
    rows = x_ref.shape[0] // groups
    sign = (1 - 2 * bits_ref[...]).astype(jnp.float32)
    for m in range(groups):
        first = (z ^ m) * rows
        if rows % 8 == 0:
            first = pl.multiple_of(first, rows)
        piece = x_ref[pl.ds(first, rows), :]
        outs[m][...] = (piece.astype(jnp.float32) * sign).astype(jnp.bfloat16)


def whole(shape):
    return pl.BlockSpec(shape, lambda n: (0,) * len(shape))


def signed_pieces(x, sign_bits, z, groups):
    rows, width = x.shape
    part = rows // groups
    if part % 16:
        signed = x * (1 - 2 * sign_bits).astype(jnp.bfloat16)[None, :]
        return [
            lax.dynamic_slice_in_dim(signed, (z ^ m) * part, part, axis=0) for m in range(groups)
        ]
    return pl.pallas_call(
        functools.partial(sign_kernel, groups),
        out_shape=[jax.ShapeDtypeStruct((part, width), jnp.bfloat16)] * groups,
        grid=(1,),
        in_specs=[whole((rows, width)), whole((1, width))],
        out_specs=[whole((part, width))] * groups,
        name="signed_pieces",
    )(x, sign_bits.reshape(1, width))


def rotate_kernel(groups, core_order, factor, h_ref, *refs):
    pieces, outs = refs[:groups], refs[groups:]
    z = lax.axis_index("tensor")
    rows, width = pieces[0].shape
    chunks = width // core_order
    h = h_ref[...]
    cut = [
        [piece[:, j * core_order : (j + 1) * core_order] for j in range(chunks)]
        for piece in pieces
    ]
    if rows % 16 == 0:
        stacked = jnp.concatenate([c for row in cut for c in row], axis=0)
        product = jnp.dot(stacked, h, preferred_element_type=jnp.float32)
        cut = [
            [product[(i * chunks + j) * rows : (i * chunks + j + 1) * rows] for j in range(chunks)]
            for i in range(groups)
        ]
    else:
        cut = [
            [jnp.dot(c, h, preferred_element_type=jnp.float32) for c in row] for row in cut
        ]
    signs = [parity_sign(z & i) for i in range(groups)]
    scales = [parity_sign((z ^ m) & z) * factor for m in range(groups)]
    rotated = [butterfly([c * signs[i] for c in row]) for i, row in enumerate(cut)]
    for j in range(chunks):
        panel = butterfly([r[j] for r in rotated])
        for m in range(groups):
            outs[m][:, j * core_order : (j + 1) * core_order] = (panel[m] * scales[m]).astype(
                jnp.bfloat16
            )


def rotate(pieces):
    groups = len(pieces)
    rows, width = pieces[0].shape
    core_order = min(256, width)
    return pl.pallas_call(
        functools.partial(
            rotate_kernel, groups, core_order, 1.0 / math.sqrt(width * groups)
        ),
        out_shape=[jax.ShapeDtypeStruct((rows, width), jnp.bfloat16)] * groups,
        grid=(1,),
        in_specs=[whole((core_order, core_order))] + [whole((rows, width))] * groups,
        out_specs=[whole((rows, width))] * groups,
        name="rotate",
    )(hadamard(core_order), *pieces)


def place_rows(pieces, masks, rows):
    groups = lax.axis_size("tensor")
    z, d = lax.axis_index("tensor"), lax.axis_index("dp")
    group_rows = rows // groups
    starts = jnp.stack([(d ^ mask) * rows + (z ^ i) * group_rows for mask in masks for i in range(groups)])
    total = rows * len(masks)
    starts = (starts + (groups - z) * (total // groups)) % total
    stacked = jnp.concatenate(pieces).reshape(-1, group_rows, pieces[0].shape[1])
    order = jnp.zeros((total // group_rows,), jnp.int32).at[starts // group_rows].set(
        jnp.arange(total // group_rows, dtype=jnp.int32)
    )
    return jnp.take(stacked, order, axis=0).reshape(total, -1)


def first_kernel(masks, groups, group_rows, rows, *refs):
    count = len(masks)
    pieces, (w_ref, q_ref, *out_refs, sems) = refs[:count], refs[count:]
    total = rows * count

    @pl.when(pl.program_id(0) == 0)
    def _():
        z, d = lax.axis_index("tensor"), lax.axis_index("dp")
        copies = []
        for n, mask in enumerate(masks):
            for i in range(groups):
                start = (d ^ mask) * rows + (z ^ i) * group_rows + (groups - z) * (total // groups)
                start = pl.multiple_of(lax.rem(start, total), group_rows)
                copies.append(
                    pltpu.make_async_copy(
                        pieces[n].at[pl.ds(i * group_rows, group_rows), :],
                        q_ref.at[pl.ds(start, group_rows), :],
                        sems.at[n * groups + i],
                    )
                )
        for copy in copies:
            copy.start()
        for copy in copies:
            copy.wait()

    project_kernel(q_ref, w_ref, *out_refs)


def project_kernel(q_ref, w_ref, *out_refs):
    product = jnp.dot(q_ref[...], w_ref[...], preferred_element_type=jnp.float32)
    step = out_refs[0].shape[0]
    for k, out_ref in enumerate(out_refs):
        out_ref[...] = product[k * step : (k + 1) * step].astype(out_ref.dtype)


def tile_of(width, first=0):
    return next((t for t in (512, 256, 128) if width % t == 0 and first % t == 0), width)


def project_first(pieces, masks, rows, weight, width):
    groups = lax.axis_size("tensor")
    depth = weight.shape[0]
    tokens = rows * len(masks)
    if (rows // groups) % 16:
        q = place_rows(pieces, masks, rows)
        return q, project(q, weight, 0, width, groups)
    tile = tile_of(width)
    block = tokens // groups
    q, *blocks = pl.pallas_call(
        functools.partial(first_kernel, masks, groups, rows // groups, rows),
        out_shape=[
            jax.ShapeDtypeStruct((tokens, depth), jnp.bfloat16),
            *[jax.ShapeDtypeStruct((block, width), jnp.bfloat16)] * groups,
        ],
        grid=(width // tile,),
        in_specs=[pl.BlockSpec(memory_space=pl.ANY)] * len(masks)
        + [pl.BlockSpec((depth, tile), lambda n: (0, n))],
        out_specs=[whole((tokens, depth))]
        + [pl.BlockSpec((block, tile), lambda n: (0, n))] * groups,
        scratch_shapes=[pltpu.SemaphoreType.DMA((len(masks) * groups,))],
        compiler_params=pltpu.CompilerParams(vmem_limit_bytes=48 * MIB),
        cost_estimate=pl.CostEstimate(
            flops=2 * tokens * depth * width,
            bytes_accessed=2 * (2 * tokens * depth + depth * width + tokens * width),
            transcendentals=0,
        ),
        name="project_first",
    )(*pieces, weight)
    return q, blocks


def project(q, weight, first, width, groups):
    tile = tile_of(width, first)
    tokens, depth = q.shape
    block = tokens // groups
    return pl.pallas_call(
        project_kernel,
        out_shape=[jax.ShapeDtypeStruct((block, width), jnp.bfloat16)] * groups,
        grid=(width // tile,),
        in_specs=[
            whole((tokens, depth)),
            pl.BlockSpec((depth, tile), lambda n: (0, n + first // tile)),
        ],
        out_specs=[pl.BlockSpec((block, tile), lambda n: (0, n))] * groups,
        compiler_params=pltpu.CompilerParams(vmem_limit_bytes=48 * MIB),
        cost_estimate=pl.CostEstimate(
            flops=2 * tokens * depth * width,
            bytes_accessed=2 * (tokens * depth + depth * width + tokens * width),
            transcendentals=0,
        ),
        name="project",
    )(q, weight)


def grad_kernel(groups, tile, q_ref, own_ref, *refs):
    lefts, rights = refs[: groups - 1], refs[groups - 1 : 2 * (groups - 1)]
    out_ref, q_t, up_all, sems = refs[2 * (groups - 1) :]
    z = lax.axis_index("tensor")
    rows = own_ref.shape[0]

    @pl.when(pl.program_id(0) == 0)
    def _():
        def copy(source, k):
            return pltpu.make_async_copy(
                source, up_all.at[k * rows : (k + 1) * rows, :], sems.at[k]
            )

        copy(own_ref, 0).start()
        for k in range(1, groups):

            @pl.when(z + k < groups)
            def _():
                copy(rights[k - 1], k).start()

            @pl.when(z + k >= groups)
            def _():
                copy(lefts[groups - k - 1], k).start()

        q_t[...] = q_ref[...].T
        for k in range(groups):
            copy(own_ref, k).wait()

    first = pl.multiple_of(pl.program_id(0) * tile, tile)
    out_ref[...] = jnp.dot(
        q_t[...], up_all[:, pl.ds(first, tile)], preferred_element_type=jnp.float32
    )


def weight_gradient(q, own, lefts, rights):
    groups = len(lefts) + 1
    tokens, depth = q.shape
    width = own.shape[1]
    tile = tile_of(width)
    anywhere = pl.BlockSpec(memory_space=pl.ANY)
    return pl.pallas_call(
        functools.partial(grad_kernel, groups, tile),
        out_shape=jax.ShapeDtypeStruct((depth, width), jnp.float32),
        grid=(width // tile,),
        in_specs=[whole((tokens, depth))] + [anywhere] * (2 * groups - 1),
        out_specs=pl.BlockSpec((depth, tile), lambda n: (0, n)),
        scratch_shapes=[
            pltpu.VMEM((depth, tokens), jnp.bfloat16),
            pltpu.VMEM((tokens, width), jnp.bfloat16),
            pltpu.SemaphoreType.DMA((groups,)),
        ],
        compiler_params=pltpu.CompilerParams(vmem_limit_bytes=48 * MIB),
        cost_estimate=pl.CostEstimate(
            flops=2 * tokens * depth * width,
            bytes_accessed=2 * tokens * (depth + width) + 4 * depth * width,
            transcendentals=0,
        ),
        name="weight_gradient",
    )(q, own, *lefts, *rights)


def after(arrays, *earlier):
    arrays = list(arrays)
    return list(lax.optimization_barrier(tuple(arrays) + tuple(earlier))[: len(arrays)])


def swap(block, axis, mask):
    count = lax.axis_size(axis)
    return lax.ppermute(block, axis, [(i, i ^ mask) for i in range(count)])


def gather_rows(own, d):
    ways = lax.axis_size("dp")
    if ways != 8:
        held = {0: own}
        for bit in [1 << b for b in range(1, ways.bit_length() - 1)] + [1]:
            held.update({mask | bit: swap(array, "dp", bit) for mask, array in held.items()})
        return held
    x, y, core = swap(own, "dp", 2), swap(own, "dp", 4), swap(own, "dp", 1)
    x, y = after([x, y])
    through = jnp.where(d & 1 == 0, x, y)
    diagonal = lax.ppermute(
        through, "dp", [(i, i ^ (4 if i & 1 == 0 else 2)) for i in range(ways)]
    )
    held = {0: own, 1: core, 2: x, 3: swap(x, "dp", 1), 4: y, 5: swap(y, "dp", 1)}
    held[6] = diagonal
    held[7] = swap(diagonal, "dp", 1)
    return held


def step_right(block, step, groups):
    return lax.ppermute(block, "tensor", [(i, i + 1) for i in range(step)])


def step_left(block, step, groups):
    return lax.ppermute(block, "tensor", [(i, i - 1) for i in range(groups - step, groups)])


def total(*blocks):
    return sum(b.astype(jnp.float32) for b in blocks).astype(jnp.bfloat16)


def sends(blocks, step, groups, arrived=None):
    right, left = blocks[groups - step], blocks[step]
    if arrived is None:
        return right, left
    return total(right, arrived[0]), total(left, arrived[1])


def move(pair, step, groups):
    return after([step_right(pair[0], step, groups), step_left(pair[1], step, groups)])


def per_device(x_tokens, sign_bits, weight, upstream):
    groups = lax.axis_size("tensor")
    ways = lax.axis_size("dp")
    z = lax.axis_index("tensor")
    d = lax.axis_index("dp")
    rows = x_tokens.shape[0]
    hidden = weight.shape[1]
    far_first = sorted(range(1, groups), reverse=True)

    pieces = list(signed_pieces(x_tokens, sign_bits, z, groups))
    for m in far_first:
        pieces[m] = swap(pieces[m], "tensor", m)
    turned = list(rotate(pieces))
    (up_first,) = after([upstream], turned[0])
    back = [swap(t, "tensor", m) if m else t for m, t in enumerate(turned)]

    lefts, rights = [], []

    def pass_on(left, right):
        step = len(lefts) + 1
        lefts.append(lax.ppermute(left, "tensor", [(i, i + 1) for i in range(step - 1, groups - 1)]))
        rights.append(lax.ppermute(right, "tensor", [(i, i - 1) for i in range(1, groups - step + 1)]))

    pass_on(up_first, up_first)

    own = jnp.concatenate(back)
    held = gather_rows(own, d)
    masks = tuple(sorted(held))
    gathered = [held[m] for m in masks]
    *gathered, lefts[0], rights[0] = after([*gathered, lefts[0], rights[0]])
    pass_on(lefts[0], rights[0])

    half = hidden // 2 if hidden % 512 == 0 else hidden
    q, blocks = project_first(gathered, masks, rows, weight, half)
    parts = [blocks]
    if half < hidden:
        parts.append(project(q, weight, half, hidden - half, groups))

    arrived = [[] for _ in parts]
    for step in range(1, groups):
        for c, blocks in enumerate(parts):
            last = arrived[c][-1] if step > 1 else None
            if step == 2 and c == 0:
                *last, lefts[-1], rights[-1] = after([*last, lefts[-1], rights[-1]])
                while len(lefts) < groups - 1:
                    pass_on(lefts[-1], rights[-1])
            if step == groups - 1 and c == len(parts) - 1:
                ready = arrived[0][groups - 3] + arrived[c][max(groups - 4, 0)]
                (q_late,) = after([q], *ready)
                weight_grad = weight_gradient(q_late, upstream, lefts, rights)
                *last, weight_grad = after([*last, weight_grad])
            arrived[c].append(move(sends(blocks, step, groups, last), step, groups))
    projected = jnp.concatenate(
        [total(blocks[0], *a[-1]) for blocks, a in zip(parts, arrived)], axis=1
    )
    return (projected, weight_grad)


def solution(mesh):
    in_specs = (P("dp", "tensor"), P("tensor"), P("tensor", "dp"), P("tensor", "dp"))
    out_specs = (P("tensor", "dp"), P("tensor", "dp"))
    return jax.shard_map(
        per_device, mesh=mesh, in_specs=in_specs, out_specs=out_specs, check_vma=False
    )
```

```python
import functools
import math

import jax
import jax.numpy as jnp
from jax import lax
from jax.experimental import pallas as pl
from jax.experimental.pallas import tpu as pltpu
from jax.sharding import PartitionSpec as P

MIB = 1 << 20


def hadamard(order):
    row_ids = jnp.arange(order, dtype=jnp.int32)[:, None]
    col_ids = jnp.arange(order, dtype=jnp.int32)[None, :]
    common = row_ids & col_ids
    parity = jnp.zeros((order, order), jnp.int32)
    for section_bit in range(max(order.bit_length() - 1, 0)):
        parity = parity + (common >> section_bit & 1)
    return (1 - 2 * (parity % 2)).astype(jnp.bfloat16)


def swap(block, axis, mask):
    count = lax.axis_size(axis)
    return lax.ppermute(
        block, axis, [(i, i ^ mask) for i in range(count) if i ^ mask < count]
    )


def plain(x_tokens, sign_bits, weight, upstream):
    panel_width = x_tokens.shape[1]
    groups = lax.axis_size("tensor")
    factor = 1.0 / math.sqrt(panel_width * groups)
    column_sign = (1 - 2 * sign_bits).astype(jnp.bfloat16)
    current = jnp.dot(
        x_tokens * column_sign[None, :],
        hadamard(panel_width),
        preferred_element_type=jnp.float32,
    )
    position = lax.axis_index("tensor")
    for section_bit in range(groups.bit_length() - 1):
        partner = swap(current.astype(jnp.bfloat16), "tensor", 1 << section_bit).astype(
            current.dtype
        )
        upper_half = position >> section_bit & 1 == 1
        current = jnp.where(upper_half, partner - current, current + partner)
    quantized = (current * factor).astype(jnp.bfloat16)
    gathered = lax.all_gather(quantized, "dp", axis=0, tiled=True)
    projected = lax.psum_scatter(
        jnp.dot(gathered, weight, preferred_element_type=jnp.float32).astype(jnp.bfloat16),
        "tensor",
        scatter_dimension=0,
        tiled=True,
    )
    weight_grad = lax.dot_general(
        gathered,
        lax.all_gather(upstream, "tensor", axis=0, tiled=True),
        (((0,), (0,)), ((), ())),
        preferred_element_type=jnp.float32,
    )
    return (projected, weight_grad)


def parity_sign(bits):
    return (1 - 2 * ((bits ^ bits >> 1) & 1)).astype(jnp.float32)


def butterfly(parts):
    stride = 1
    parts = list(parts)
    while stride < len(parts):
        for low in range(len(parts)):
            if not low & stride:
                a, b = parts[low], parts[low | stride]
                parts[low], parts[low | stride] = a + b, a - b
        stride *= 2
    return parts


def whole(shape):
    return pl.BlockSpec(shape, lambda n: (0,) * len(shape))


def tile_of(width, first=0):
    return next((t for t in (512, 256, 128) if width % t == 0 and first % t == 0), width)


def after(arrays, *earlier):
    arrays = list(arrays)
    return list(lax.optimization_barrier(tuple(arrays) + tuple(earlier))[: len(arrays)])


def sign_kernel(x_ref, bits_ref, *outs):
    z = lax.axis_index("tensor")
    rows = outs[0].shape[0]
    sign = (1 - 2 * bits_ref[...]).astype(jnp.float32)
    for m, out in enumerate(outs):
        first = pl.multiple_of((z ^ m) * rows, rows)
        out[...] = (x_ref[pl.ds(first, rows), :].astype(jnp.float32) * sign).astype(out.dtype)


def signed_pieces(x, sign_bits, groups):
    rows, width = x.shape
    part = rows // groups
    return pl.pallas_call(
        sign_kernel,
        out_shape=[jax.ShapeDtypeStruct((part, width), jnp.bfloat16)] * groups,
        grid=(1,),
        in_specs=[whole((rows, width)), whole((1, width))],
        out_specs=[whole((part, width))] * groups,
        name="signed_pieces",
    )(x, sign_bits.reshape(1, width))


def rotate_kernel(groups, order, factor, h_ref, *refs):
    pieces, outs = refs[:groups], refs[groups:]
    z = lax.axis_index("tensor")
    rows, width = pieces[0].shape
    chunks = width // order
    stacked = jnp.concatenate(
        [piece[:, j * order : (j + 1) * order] for piece in pieces for j in range(chunks)], axis=0
    )
    product = jnp.dot(stacked, h_ref[...], preferred_element_type=jnp.float32)
    rotated = []
    for i in range(groups):
        sign = parity_sign(z & i)
        rotated.append(
            butterfly(
                [
                    product[(i * chunks + j) * rows : (i * chunks + j + 1) * rows] * sign
                    for j in range(chunks)
                ]
            )
        )
    for j in range(chunks):
        panel = butterfly([r[j] for r in rotated])
        for m in range(groups):
            scale = parity_sign((z ^ m) & z) * factor
            outs[m][:, j * order : (j + 1) * order] = (panel[m] * scale).astype(jnp.bfloat16)


def rotate(pieces):
    groups = len(pieces)
    rows, width = pieces[0].shape
    order = min(256, width)
    return pl.pallas_call(
        functools.partial(rotate_kernel, groups, order, 1.0 / math.sqrt(width * groups)),
        out_shape=[jax.ShapeDtypeStruct((rows, width), jnp.bfloat16)] * groups,
        grid=(1,),
        in_specs=[whole((order, order))] + [whole((rows, width))] * groups,
        out_specs=[whole((rows, width))] * groups,
        name="rotate",
    )(hadamard(order), *pieces)


def gather_rows(own, d):
    x, y, core = swap(own, "dp", 2), swap(own, "dp", 4), swap(own, "dp", 1)
    x, y = after([x, y])
    through = jnp.where(d & 1 == 0, x, y)
    diagonal = lax.ppermute(
        through, "dp", [(i, i ^ (4 if i & 1 == 0 else 2)) for i in range(8)]
    )
    return [
        own,
        core,
        x,
        swap(x, "dp", 1),
        y,
        swap(y, "dp", 1),
        diagonal,
        swap(diagonal, "dp", 1),
    ]


def first_kernel(*refs):
    pieces, (w_ref, q_ref, *out_refs, sems) = refs[:8], refs[8:]
    rows = pieces[0].shape[0]

    @pl.when(pl.program_id(0) == 0)
    def _():
        z, d = lax.axis_index("tensor"), lax.axis_index("dp")
        copies = []
        for mask, piece in enumerate(pieces):
            start = (((d ^ mask) >> 1) ^ z) * (2 * rows) + ((d ^ mask) & 1) * rows
            copies.append(
                pltpu.make_async_copy(
                    piece, q_ref.at[pl.ds(pl.multiple_of(start, rows), rows), :], sems.at[mask]
                )
            )
        for copy in copies:
            copy.start()
        for copy in copies:
            copy.wait()

    project_kernel(q_ref, w_ref, *out_refs)


def project_kernel(q_ref, w_ref, *out_refs):
    product = jnp.dot(q_ref[...], w_ref[...], preferred_element_type=jnp.float32)
    step = out_refs[0].shape[0]
    for m, out_ref in enumerate(out_refs):
        out_ref[...] = product[m * step : (m + 1) * step].astype(out_ref.dtype)


def project_first(pieces, weight, width, groups):
    depth = weight.shape[0]
    tokens = pieces[0].shape[0] * len(pieces)
    block = tokens // groups
    tile = tile_of(width)
    q, *blocks = pl.pallas_call(
        first_kernel,
        out_shape=[
            jax.ShapeDtypeStruct((tokens, depth), jnp.bfloat16),
            *[jax.ShapeDtypeStruct((block, width), jnp.bfloat16)] * groups,
        ],
        grid=(width // tile,),
        in_specs=[pl.BlockSpec(memory_space=pl.ANY)] * len(pieces)
        + [pl.BlockSpec((depth, tile), lambda n: (0, n))],
        out_specs=[whole((tokens, depth))]
        + [pl.BlockSpec((block, tile), lambda n: (0, n))] * groups,
        scratch_shapes=[pltpu.SemaphoreType.DMA((len(pieces),))],
        compiler_params=pltpu.CompilerParams(vmem_limit_bytes=48 * MIB),
        cost_estimate=pl.CostEstimate(flops=1, bytes_accessed=1, transcendentals=0),
        name="project_first",
    )(*pieces, weight)
    return q, blocks


def project(q, weight, first, width, groups):
    tile = tile_of(width, first)
    tokens, depth = q.shape
    block = tokens // groups
    return pl.pallas_call(
        project_kernel,
        out_shape=[jax.ShapeDtypeStruct((block, width), jnp.bfloat16)] * groups,
        grid=(width // tile,),
        in_specs=[
            whole((tokens, depth)),
            pl.BlockSpec((depth, tile), lambda n: (0, n + first // tile)),
        ],
        out_specs=[pl.BlockSpec((block, tile), lambda n: (0, n))] * groups,
        compiler_params=pltpu.CompilerParams(vmem_limit_bytes=48 * MIB),
        cost_estimate=pl.CostEstimate(
            flops=2 * tokens * depth * width,
            bytes_accessed=2 * (tokens * depth + depth * width + tokens * width),
            transcendentals=0,
        ),
        name="project",
    )(q, weight)


def grad_kernel(tile, q_ref, own_ref, e1, o1, o2, e2, e3, out_ref, q_t, up_all, sems):
    z = lax.axis_index("tensor")
    rows = own_ref.shape[0]

    @pl.when(pl.program_id(0) == 0)
    def _():
        def copy(source, m):
            return pltpu.make_async_copy(
                source, up_all.at[m * rows : (m + 1) * rows, :], sems.at[m]
            )

        copy(own_ref, 0).start()
        copy(e1, 1).start()
        inner = jnp.logical_or(z == 1, z == 2)

        @pl.when(inner)
        def _():
            copy(o2, 2).start()
            copy(o1, 3).start()

        @pl.when(jnp.logical_not(inner))
        def _():
            copy(e2, 2).start()
            copy(e3, 3).start()

        q_t[...] = q_ref[...].T
        for m in range(4):
            copy(own_ref, m).wait()

    first = pl.multiple_of(pl.program_id(0) * tile, tile)
    out_ref[...] = jnp.dot(
        q_t[...], up_all[:, pl.ds(first, tile)], preferred_element_type=jnp.float32
    )


def weight_gradient(q, own, moved):
    tokens, depth = q.shape
    width = own.shape[1]
    tile = tile_of(width)
    anywhere = pl.BlockSpec(memory_space=pl.ANY)
    return pl.pallas_call(
        functools.partial(grad_kernel, tile),
        out_shape=jax.ShapeDtypeStruct((depth, width), jnp.float32),
        grid=(width // tile,),
        in_specs=[whole((tokens, depth))] + [anywhere] * 6,
        out_specs=pl.BlockSpec((depth, tile), lambda n: (0, n)),
        scratch_shapes=[
            pltpu.VMEM((depth, tokens), jnp.bfloat16),
            pltpu.VMEM((tokens, width), jnp.bfloat16),
            pltpu.SemaphoreType.DMA((4,)),
        ],
        compiler_params=pltpu.CompilerParams(vmem_limit_bytes=48 * MIB),
        cost_estimate=pl.CostEstimate(
            flops=2 * tokens * depth * width,
            bytes_accessed=2 * tokens * (depth + width) + 4 * depth * width,
            transcendentals=0,
        ),
        name="weight_gradient",
    )(q, own, *moved)


def total(*blocks):
    return sum(b.astype(jnp.float32) for b in blocks).astype(jnp.bfloat16)


def move(block, *pairs):
    return lax.ppermute(block, "tensor", pairs)


INWARD = ((0, 1), (3, 2))
MIDDLE = ((1, 2), (2, 1))
OUTWARD = ((1, 0), (2, 3))


def lined(x_tokens, sign_bits, weight, upstream):
    groups = lax.axis_size("tensor")
    z = lax.axis_index("tensor")
    d = lax.axis_index("dp")
    hidden = weight.shape[1]

    pieces = list(signed_pieces(x_tokens, sign_bits, groups))
    for m in (3, 2, 1):
        pieces[m] = swap(pieces[m], "tensor", m)
    turned = list(rotate(pieces))
    (up,) = after([upstream], turned[0])
    for m in (3, 2, 1):
        turned[m] = swap(turned[m], "tensor", m)
    own = jnp.concatenate(
        [lax.select_n(z, *[turned[g ^ k] for k in range(groups)]) for g in range(groups)]
    )

    e1 = swap(up, "tensor", 1)
    o1 = move(up, *MIDDLE)

    gathered = gather_rows(own, d)
    cut = 3 * hidden // 7 // 512 * 512
    q, first = project_first(gathered, weight, cut, groups)
    o2_from, e2_from = after([e1, o1], first[0])
    o2 = move(o2_from, *MIDDLE)
    e2 = move(e2_from, *OUTWARD)
    e3 = move(o2, *OUTWARD)
    second = project(q, weight, cut, hidden - cut, groups)

    far_a, far_b = move(first[3], *INWARD), move(second[3], *INWARD)
    (near_a,) = after([first[2]], far_a)
    near_a = move(near_a, *INWARD)
    across_a = move(total(first[2], far_a), *MIDDLE)
    (near_b,) = after([second[2]], far_b)
    near_b = move(near_b, *INWARD)
    across_b = move(total(second[2], far_b), *MIDDLE)

    near_a, across_a = after([near_a, across_a])
    back_a = move(total(first[3], near_a), *MIDDLE)
    pair_a = swap(total(first[1], across_a), "tensor", 1)

    (q_late,) = after([q], near_a, across_a)
    weight_grad = weight_gradient(q_late, upstream, (e1, o1, o2, e2, e3))

    near_b, across_b, weight_grad = after([near_b, across_b, weight_grad])
    back_b = move(total(second[3], near_b), *MIDDLE)
    pair_b = swap(total(second[1], across_b), "tensor", 1)
    projected = jnp.concatenate(
        [total(first[0], pair_a, back_a), total(second[0], pair_b, back_b)], axis=1
    )
    return (projected, weight_grad)


def per_device(x_tokens, sign_bits, weight, upstream):
    rows, width = x_tokens.shape
    hidden = weight.shape[1]
    fits = rows % 64 == 0 and width % 256 == 0 and hidden % 512 == 0 and hidden >= 1536
    if (lax.axis_size("dp"), lax.axis_size("tensor")) == (8, 4) and fits:
        return lined(x_tokens, sign_bits, weight, upstream)
    return plain(x_tokens, sign_bits, weight, upstream)


def solution(mesh):
    in_specs = (P("dp", "tensor"), P("tensor"), P("tensor", "dp"), P("tensor", "dp"))
    out_specs = (P("tensor", "dp"), P("tensor", "dp"))
    return jax.shard_map(
        per_device, mesh=mesh, in_specs=in_specs, out_specs=out_specs, check_vma=False
    )
```

```python
import functools
import math

import jax
import jax.numpy as jnp
from jax import lax
from jax.experimental import pallas as pl
from jax.experimental.pallas import tpu as pltpu
from jax.sharding import PartitionSpec as P

MIB = 1 << 20


def hadamard(order):
    row_ids = jnp.arange(order, dtype=jnp.int32)[:, None]
    col_ids = jnp.arange(order, dtype=jnp.int32)[None, :]
    common = row_ids & col_ids
    parity = jnp.zeros((order, order), jnp.int32)
    for section_bit in range(max(order.bit_length() - 1, 0)):
        parity = parity + (common >> section_bit & 1)
    return (1 - 2 * (parity % 2)).astype(jnp.bfloat16)


def swap(block, axis, mask):
    count = lax.axis_size(axis)
    return lax.ppermute(
        block, axis, [(i, i ^ mask) for i in range(count) if i ^ mask < count]
    )


def plain(x_tokens, sign_bits, weight, upstream):
    panel_width = x_tokens.shape[1]
    groups = lax.axis_size("tensor")
    factor = 1.0 / math.sqrt(panel_width * groups)
    column_sign = (1 - 2 * sign_bits).astype(jnp.bfloat16)
    current = jnp.dot(
        x_tokens * column_sign[None, :],
        hadamard(panel_width),
        preferred_element_type=jnp.float32,
    )
    position = lax.axis_index("tensor")
    for section_bit in range(groups.bit_length() - 1):
        partner = swap(current.astype(jnp.bfloat16), "tensor", 1 << section_bit).astype(
            current.dtype
        )
        upper_half = position >> section_bit & 1 == 1
        current = jnp.where(upper_half, partner - current, current + partner)
    quantized = (current * factor).astype(jnp.bfloat16)
    gathered = lax.all_gather(quantized, "dp", axis=0, tiled=True)
    projected = lax.psum_scatter(
        jnp.dot(gathered, weight, preferred_element_type=jnp.float32).astype(jnp.bfloat16),
        "tensor",
        scatter_dimension=0,
        tiled=True,
    )
    weight_grad = lax.dot_general(
        gathered,
        lax.all_gather(upstream, "tensor", axis=0, tiled=True),
        (((0,), (0,)), ((), ())),
        preferred_element_type=jnp.float32,
    )
    return (projected, weight_grad)


def parity_sign(bits):
    return (1 - 2 * ((bits ^ bits >> 1) & 1)).astype(jnp.float32)


def butterfly(parts):
    stride = 1
    parts = list(parts)
    while stride < len(parts):
        for low in range(len(parts)):
            if not low & stride:
                a, b = parts[low], parts[low | stride]
                parts[low], parts[low | stride] = a + b, a - b
        stride *= 2
    return parts


def whole(shape):
    return pl.BlockSpec(shape, lambda n: (0,) * len(shape))


def tile_of(width, first=0):
    return next((t for t in (512, 256, 128) if width % t == 0 and first % t == 0), width)


def after(arrays, *earlier):
    arrays = list(arrays)
    return list(lax.optimization_barrier(tuple(arrays) + tuple(earlier))[: len(arrays)])


def sign_kernel(x_ref, bits_ref, *outs):
    z = lax.axis_index("tensor")
    rows = outs[0].shape[0]
    sign = (1 - 2 * bits_ref[...]).astype(jnp.float32)
    for m, out in enumerate(outs):
        first = pl.multiple_of((z ^ m) * rows, rows)
        out[...] = (x_ref[pl.ds(first, rows), :].astype(jnp.float32) * sign).astype(out.dtype)


def signed_pieces(x, sign_bits, groups):
    rows, width = x.shape
    part = rows // groups
    return pl.pallas_call(
        sign_kernel,
        out_shape=[jax.ShapeDtypeStruct((part, width), jnp.bfloat16)] * groups,
        grid=(1,),
        in_specs=[whole((rows, width)), whole((1, width))],
        out_specs=[whole((part, width))] * groups,
        name="signed_pieces",
    )(x, sign_bits.reshape(1, width))


def rotate_kernel(groups, order, factor, h_ref, *refs):
    pieces, outs = refs[:groups], refs[groups:]
    z = lax.axis_index("tensor")
    rows, width = pieces[0].shape
    chunks = width // order
    stacked = jnp.concatenate(
        [piece[:, j * order : (j + 1) * order] for piece in pieces for j in range(chunks)], axis=0
    )
    product = jnp.dot(stacked, h_ref[...], preferred_element_type=jnp.float32)
    rotated = []
    for i in range(groups):
        sign = parity_sign(z & i)
        rotated.append(
            butterfly(
                [
                    product[(i * chunks + j) * rows : (i * chunks + j + 1) * rows] * sign
                    for j in range(chunks)
                ]
            )
        )
    for j in range(chunks):
        panel = butterfly([r[j] for r in rotated])
        for m in range(groups):
            scale = parity_sign((z ^ m) & z) * factor
            outs[m][:, j * order : (j + 1) * order] = (panel[m] * scale).astype(jnp.bfloat16)


def rotate(pieces):
    groups = len(pieces)
    rows, width = pieces[0].shape
    order = min(256, width)
    return pl.pallas_call(
        functools.partial(rotate_kernel, groups, order, 1.0 / math.sqrt(width * groups)),
        out_shape=[jax.ShapeDtypeStruct((rows, width), jnp.bfloat16)] * groups,
        grid=(1,),
        in_specs=[whole((order, order))] + [whole((rows, width))] * groups,
        out_specs=[whole((rows, width))] * groups,
        name="rotate",
    )(hadamard(order), *pieces)


def gather_rows(own, d, *earlier):
    x, y, core = swap(own, "dp", 2), swap(own, "dp", 4), swap(own, "dp", 1)
    x, y, *earlier = after([x, y, *earlier])
    through = jnp.where(d & 1 == 0, x, y)
    diagonal = lax.ppermute(
        through, "dp", [(i, i ^ (4 if i & 1 == 0 else 2)) for i in range(8)]
    )
    rows = [own, core, x, swap(x, "dp", 1), y, swap(y, "dp", 1)]
    return rows + [diagonal, swap(diagonal, "dp", 1)], earlier


def first_kernel(*refs):
    pieces, (w_ref, q_ref, *out_refs, sems) = refs[:8], refs[8:]
    rows = pieces[0].shape[0]

    @pl.when(pl.program_id(0) == 0)
    def _():
        z, d = lax.axis_index("tensor"), lax.axis_index("dp")
        copies = []
        for mask, piece in enumerate(pieces):
            start = (((d ^ mask) >> 1) ^ z) * (2 * rows) + ((d ^ mask) & 1) * rows
            copies.append(
                pltpu.make_async_copy(
                    piece, q_ref.at[pl.ds(pl.multiple_of(start, rows), rows), :], sems.at[mask]
                )
            )
        for copy in copies:
            copy.start()
        for copy in copies:
            copy.wait()

    project_kernel(q_ref, w_ref, *out_refs)


def project_kernel(q_ref, w_ref, *out_refs):
    product = jnp.dot(q_ref[...], w_ref[...], preferred_element_type=jnp.float32)
    step = out_refs[0].shape[0]
    for m, out_ref in enumerate(out_refs):
        out_ref[...] = product[m * step : (m + 1) * step].astype(out_ref.dtype)


def project_first(pieces, weight, width, groups):
    depth = weight.shape[0]
    tokens = pieces[0].shape[0] * len(pieces)
    block = tokens // groups
    tile = tile_of(width)
    q, *blocks = pl.pallas_call(
        first_kernel,
        out_shape=[
            jax.ShapeDtypeStruct((tokens, depth), jnp.bfloat16),
            *[jax.ShapeDtypeStruct((block, width), jnp.bfloat16)] * groups,
        ],
        grid=(width // tile,),
        in_specs=[pl.BlockSpec(memory_space=pl.ANY)] * len(pieces)
        + [pl.BlockSpec((depth, tile), lambda n: (0, n))],
        out_specs=[whole((tokens, depth))]
        + [pl.BlockSpec((block, tile), lambda n: (0, n))] * groups,
        scratch_shapes=[pltpu.SemaphoreType.DMA((len(pieces),))],
        compiler_params=pltpu.CompilerParams(vmem_limit_bytes=48 * MIB),
        cost_estimate=pl.CostEstimate(flops=1, bytes_accessed=1, transcendentals=0),
        name="project_first",
    )(*pieces, weight)
    return q, blocks


def project(q, weight, first, width, groups):
    tile = tile_of(width, first)
    tokens, depth = q.shape
    block = tokens // groups
    return pl.pallas_call(
        project_kernel,
        out_shape=[jax.ShapeDtypeStruct((block, width), jnp.bfloat16)] * groups,
        grid=(width // tile,),
        in_specs=[
            whole((tokens, depth)),
            pl.BlockSpec((depth, tile), lambda n: (0, n + first // tile)),
        ],
        out_specs=[pl.BlockSpec((block, tile), lambda n: (0, n))] * groups,
        compiler_params=pltpu.CompilerParams(vmem_limit_bytes=48 * MIB),
        cost_estimate=pl.CostEstimate(
            flops=2 * tokens * depth * width,
            bytes_accessed=2 * (tokens * depth + depth * width + tokens * width),
            transcendentals=0,
        ),
        name="project",
    )(q, weight)


def grad_kernel(tile, start, q_ref, own_ref, e1, o1, o2, e2, e3, *refs):
    out_ref, q_t, up_all, sems = refs[-4:]
    z = lax.axis_index("tensor")
    rows, width = own_ref.shape[0], up_all.shape[1]

    @pl.when(pl.program_id(0) == 0)
    def _():
        def copy(source, m):
            return pltpu.make_async_copy(
                source, up_all.at[m * rows : (m + 1) * rows, :], sems.at[m]
            )

        copy(own_ref.at[:, start : start + width], 0).start()
        copy(e1, 1).start()
        inner = jnp.logical_or(z == 1, z == 2)

        @pl.when(inner)
        def _():
            copy(o2, 2).start()
            copy(o1, 3).start()

        @pl.when(jnp.logical_not(inner))
        def _():
            copy(e2, 2).start()
            copy(e3, 3).start()

        q_t[...] = q_ref[...].T
        for m in range(4):
            copy(e1, m).wait()

    first = pl.multiple_of(pl.program_id(0) * tile, tile)
    out_ref[...] = jnp.dot(
        q_t[...], up_all[:, pl.ds(first, tile)], preferred_element_type=jnp.float32
    )


def weight_gradient(q, own, moved, start, width, done=None):
    tokens, depth = q.shape
    hidden = own.shape[1]
    tile = tile_of(width, start)
    before = [] if done is None else [done]
    anywhere = pl.BlockSpec(memory_space=pl.ANY)
    return pl.pallas_call(
        functools.partial(grad_kernel, tile, start),
        out_shape=jax.ShapeDtypeStruct((depth, hidden), jnp.float32),
        grid=(width // tile,),
        in_specs=[whole((tokens, depth))] + [anywhere] * (6 + len(before)),
        out_specs=pl.BlockSpec((depth, tile), lambda n: (0, n + start // tile)),
        input_output_aliases={7: 0} if before else {},
        scratch_shapes=[
            pltpu.VMEM((depth, tokens), jnp.bfloat16),
            pltpu.VMEM((tokens, width), jnp.bfloat16),
            pltpu.SemaphoreType.DMA((4,)),
        ],
        compiler_params=pltpu.CompilerParams(vmem_limit_bytes=48 * MIB),
        cost_estimate=pl.CostEstimate(
            flops=2 * tokens * depth * width,
            bytes_accessed=2 * tokens * (depth + width) + 4 * depth * width,
            transcendentals=0,
        ),
        name="weight_gradient",
    )(q, own, *moved, *before)


def total(*blocks):
    return sum(b.astype(jnp.float32) for b in blocks).astype(jnp.bfloat16)


def move(block, *pairs):
    return lax.ppermute(block, "tensor", pairs)


INWARD = ((0, 1), (3, 2))
MIDDLE = ((1, 2), (2, 1))
OUTWARD = ((1, 0), (2, 3))


def lined(x_tokens, sign_bits, weight, upstream):
    groups = lax.axis_size("tensor")
    z = lax.axis_index("tensor")
    d = lax.axis_index("dp")
    hidden = weight.shape[1]

    pieces = list(signed_pieces(x_tokens, sign_bits, groups))
    for m in (3, 2, 1):
        pieces[m] = swap(pieces[m], "tensor", m)
    turned = list(rotate(pieces))
    for m in (3, 2, 1):
        turned[m] = swap(turned[m], "tensor", m)
    some = (hidden // 512 + 1) // 2 * 512
    up_a, up_b = upstream[:, :some], upstream[:, some:]
    e1_a, o1_a = swap(up_a, "tensor", 1), move(up_a, *MIDDLE)
    *turned, e1_a, o1_a = after([*turned, e1_a, o1_a])
    e1_b, o1_b = swap(up_b, "tensor", 1), move(up_b, *MIDDLE)
    o2_a, e2_a = move(e1_a, *MIDDLE), move(o1_a, *OUTWARD)

    own = jnp.concatenate(
        [lax.select_n(z, *[turned[g ^ k] for k in range(groups)]) for g in range(groups)]
    )

    gathered, (e1_b, o1_b) = gather_rows(own, d, e1_b, o1_b)
    o2_b, e2_b = move(e1_b, *MIDDLE), move(o1_b, *OUTWARD)

    cut = 3 * hidden // 7 // 512 * 512
    q, first = project_first(gathered, weight, cut, groups)
    q, o2_a, e2_a = after([q, o2_a, e2_a])
    e3_a = move(o2_a, *OUTWARD)
    second = project(q, weight, cut, hidden - cut, groups)

    far_a, far_b = move(first[3], *INWARD), move(second[3], *INWARD)
    far_a, o2_b, e2_b = after([far_a, o2_b, e2_b])
    e3_b = move(o2_b, *OUTWARD)
    (near_a,) = after([first[2]], far_a)
    near_a = move(near_a, *INWARD)
    across_a = move(total(first[2], far_a), *MIDDLE)
    (near_b,) = after([second[2]], far_b)
    near_b = move(near_b, *INWARD)
    across_b = move(total(second[2], far_b), *MIDDLE)

    near_a, across_a, e3_a = after([near_a, across_a, e3_a])
    back_a = move(total(first[3], near_a), *MIDDLE)
    pair_a = swap(total(first[1], across_a), "tensor", 1)

    (q_late,) = after([q], near_a, across_a)
    grad = weight_gradient(q_late, upstream, (e1_a, o1_a, o2_a, e2_a, e3_a), 0, some)

    near_b, across_b, grad = after([near_b, across_b, grad])
    back_b = move(total(second[3], near_b), *MIDDLE)
    pair_b = swap(total(second[1], across_b), "tensor", 1)
    (q_late,) = after([q], near_b, across_b)
    weight_grad = weight_gradient(
        q_late, upstream, (e1_b, o1_b, o2_b, e2_b, e3_b), some, hidden - some, grad
    )
    projected = jnp.concatenate(
        [total(first[0], pair_a, back_a), total(second[0], pair_b, back_b)], axis=1
    )
    return (projected, weight_grad)


def per_device(x_tokens, sign_bits, weight, upstream):
    rows, width = x_tokens.shape
    hidden = weight.shape[1]
    fits = rows % 64 == 0 and width % 256 == 0 and hidden % 512 == 0 and hidden >= 1536
    if (lax.axis_size("dp"), lax.axis_size("tensor")) == (8, 4) and fits:
        return lined(x_tokens, sign_bits, weight, upstream)
    return plain(x_tokens, sign_bits, weight, upstream)


def solution(mesh):
    in_specs = (P("dp", "tensor"), P("tensor"), P("tensor", "dp"), P("tensor", "dp"))
    out_specs = (P("tensor", "dp"), P("tensor", "dp"))
    return jax.shard_map(
        per_device, mesh=mesh, in_specs=in_specs, out_specs=out_specs, check_vma=False
    )
```

```python
import functools
import math

import jax
import jax.numpy as jnp
from jax import lax
from jax.experimental import pallas as pl
from jax.experimental.pallas import tpu as pltpu
from jax.sharding import PartitionSpec as P

MIB = 1 << 20
VMEM = pl.BlockSpec(memory_space=pltpu.VMEM)


def hadamard(order):
    row_ids = jnp.arange(order, dtype=jnp.int32)[:, None]
    col_ids = jnp.arange(order, dtype=jnp.int32)[None, :]
    common = row_ids & col_ids
    parity = jnp.zeros((order, order), jnp.int32)
    for section_bit in range(max(order.bit_length() - 1, 0)):
        parity = parity + (common >> section_bit & 1)
    return (1 - 2 * (parity % 2)).astype(jnp.bfloat16)


def swap(block, axis, mask):
    count = lax.axis_size(axis)
    return lax.ppermute(
        block, axis, [(i, i ^ mask) for i in range(count) if i ^ mask < count]
    )


def plain(x_tokens, sign_bits, weight, upstream):
    panel_width = x_tokens.shape[1]
    groups = lax.axis_size("tensor")
    factor = 1.0 / math.sqrt(panel_width * groups)
    column_sign = (1 - 2 * sign_bits).astype(jnp.bfloat16)
    current = jnp.dot(
        x_tokens * column_sign[None, :],
        hadamard(panel_width),
        preferred_element_type=jnp.float32,
    )
    position = lax.axis_index("tensor")
    for section_bit in range(groups.bit_length() - 1):
        partner = swap(current.astype(jnp.bfloat16), "tensor", 1 << section_bit).astype(
            current.dtype
        )
        upper_half = position >> section_bit & 1 == 1
        current = jnp.where(upper_half, partner - current, current + partner)
    quantized = (current * factor).astype(jnp.bfloat16)
    gathered = lax.all_gather(quantized, "dp", axis=0, tiled=True)
    projected = lax.psum_scatter(
        jnp.dot(gathered, weight, preferred_element_type=jnp.float32).astype(jnp.bfloat16),
        "tensor",
        scatter_dimension=0,
        tiled=True,
    )
    weight_grad = lax.dot_general(
        gathered,
        lax.all_gather(upstream, "tensor", axis=0, tiled=True),
        (((0,), (0,)), ((), ())),
        preferred_element_type=jnp.float32,
    )
    return (projected, weight_grad)


def parity_sign(bits):
    return (1 - 2 * ((bits ^ bits >> 1) & 1)).astype(jnp.float32)


def butterfly(parts):
    stride = 1
    parts = list(parts)
    while stride < len(parts):
        for low in range(len(parts)):
            if not low & stride:
                a, b = parts[low], parts[low | stride]
                parts[low], parts[low | stride] = a + b, a - b
        stride *= 2
    return parts


def whole(shape):
    return pl.BlockSpec(shape, lambda n: (0,) * len(shape))


def tile_of(width, first=0):
    return next((t for t in (512, 256, 128) if width % t == 0 and first % t == 0), width)


def after(arrays, *earlier):
    arrays = list(arrays)
    return list(lax.optimization_barrier(tuple(arrays) + tuple(earlier))[: len(arrays)])


def sign_kernel(x_ref, bits_ref, *outs):
    z = lax.axis_index("tensor")
    rows = outs[0].shape[0]
    sign = (1 - 2 * bits_ref[...]).astype(jnp.float32)
    for m, out in enumerate(outs):
        first = pl.multiple_of((z ^ m) * rows, rows)
        out[...] = (x_ref[pl.ds(first, rows), :].astype(jnp.float32) * sign).astype(out.dtype)


def signed_pieces(x, sign_bits, groups):
    rows, width = x.shape
    part = rows // groups
    return pl.pallas_call(
        sign_kernel,
        out_shape=[jax.ShapeDtypeStruct((part, width), jnp.bfloat16)] * groups,
        in_specs=[VMEM] * 2,
        out_specs=[VMEM] * groups,
        compiler_params=pltpu.CompilerParams(vmem_limit_bytes=8 * MIB),
        name="signed_pieces",
    )(x, sign_bits.reshape(1, width))


def rotate_kernel(groups, order, factor, h_ref, *refs):
    pieces, outs = refs[:groups], refs[groups:]
    z = lax.axis_index("tensor")
    rows, width = pieces[0].shape
    chunks = width // order
    stacked = jnp.concatenate(
        [piece[:, j * order : (j + 1) * order] for piece in pieces for j in range(chunks)], axis=0
    )
    product = jnp.dot(stacked, h_ref[...], preferred_element_type=jnp.float32)
    rotated = []
    for i in range(groups):
        sign = parity_sign(z & i)
        rotated.append(
            butterfly(
                [
                    product[(i * chunks + j) * rows : (i * chunks + j + 1) * rows] * sign
                    for j in range(chunks)
                ]
            )
        )
    for j in range(chunks):
        panel = butterfly([r[j] for r in rotated])
        for m in range(groups):
            scale = parity_sign((z ^ m) & z) * factor
            outs[m][:, j * order : (j + 1) * order] = (panel[m] * scale).astype(jnp.bfloat16)


def rotate(pieces):
    groups = len(pieces)
    rows, width = pieces[0].shape
    order = min(256, width)
    return pl.pallas_call(
        functools.partial(rotate_kernel, groups, order, 1.0 / math.sqrt(width * groups)),
        out_shape=[jax.ShapeDtypeStruct((rows, width), jnp.bfloat16)] * groups,
        in_specs=[VMEM] * (1 + groups),
        out_specs=[VMEM] * groups,
        compiler_params=pltpu.CompilerParams(vmem_limit_bytes=8 * MIB),
        name="rotate",
    )(hadamard(order), *pieces)


def gather_rows(own, d):
    x, y, core = swap(own, "dp", 2), swap(own, "dp", 4), swap(own, "dp", 1)
    x, y = after([x, y])
    through = jnp.where(d & 1 == 0, x, y)
    diagonal = lax.ppermute(
        through, "dp", [(i, i ^ (4 if i & 1 == 0 else 2)) for i in range(8)]
    )
    return [
        own,
        core,
        x,
        swap(x, "dp", 1),
        y,
        swap(y, "dp", 1),
        diagonal,
        swap(diagonal, "dp", 1),
    ]


def first_kernel(*refs):
    pieces, (w_ref, q_ref, *out_refs, sems) = refs[:8], refs[8:]
    rows = pieces[0].shape[0]

    @pl.when(pl.program_id(0) == 0)
    def _():
        z, d = lax.axis_index("tensor"), lax.axis_index("dp")
        copies = []
        for mask, piece in enumerate(pieces):
            start = (((d ^ mask) >> 1) ^ z) * (2 * rows) + ((d ^ mask) & 1) * rows
            copies.append(
                pltpu.make_async_copy(
                    piece, q_ref.at[pl.ds(pl.multiple_of(start, rows), rows), :], sems.at[mask]
                )
            )
        for copy in copies:
            copy.start()
        for copy in copies:
            copy.wait()

    project_kernel(q_ref, w_ref, *out_refs)


def project_kernel(q_ref, w_ref, *out_refs):
    product = jnp.dot(q_ref[...], w_ref[...], preferred_element_type=jnp.float32)
    step = out_refs[0].shape[0]
    for m, out_ref in enumerate(out_refs):
        out_ref[...] = product[m * step : (m + 1) * step].astype(out_ref.dtype)


def project_first(pieces, weight, width, groups):
    depth = weight.shape[0]
    tokens = pieces[0].shape[0] * len(pieces)
    block = tokens // groups
    tile = tile_of(width)
    q, *blocks = pl.pallas_call(
        first_kernel,
        out_shape=[
            jax.ShapeDtypeStruct((tokens, depth), jnp.bfloat16),
            *[jax.ShapeDtypeStruct((block, width), jnp.bfloat16)] * groups,
        ],
        grid=(width // tile,),
        in_specs=[pl.BlockSpec(memory_space=pl.ANY)] * len(pieces)
        + [pl.BlockSpec((depth, tile), lambda n: (0, n))],
        out_specs=[whole((tokens, depth))]
        + [pl.BlockSpec((block, tile), lambda n: (0, n))] * groups,
        scratch_shapes=[pltpu.SemaphoreType.DMA((len(pieces),))],
        compiler_params=pltpu.CompilerParams(vmem_limit_bytes=48 * MIB),
        cost_estimate=pl.CostEstimate(flops=1, bytes_accessed=1, transcendentals=0),
        name="project_first",
    )(*pieces, weight)
    return q, blocks


def project(q, weight, first, width, groups):
    tile = tile_of(width, first)
    tokens, depth = q.shape
    block = tokens // groups
    return pl.pallas_call(
        project_kernel,
        out_shape=[jax.ShapeDtypeStruct((block, width), jnp.bfloat16)] * groups,
        grid=(width // tile,),
        in_specs=[
            whole((tokens, depth)),
            pl.BlockSpec((depth, tile), lambda n: (0, n + first // tile)),
        ],
        out_specs=[pl.BlockSpec((block, tile), lambda n: (0, n))] * groups,
        compiler_params=pltpu.CompilerParams(vmem_limit_bytes=48 * MIB),
        cost_estimate=pl.CostEstimate(
            flops=2 * tokens * depth * width,
            bytes_accessed=2 * (tokens * depth + depth * width + tokens * width),
            transcendentals=0,
        ),
        name="project",
    )(q, weight)


def grad_kernel(tile, start, q_ref, own_ref, e1, o1, o2, e2, e3, *refs):
    out_ref, q_t, up_all, sems = refs[-4:]
    z = lax.axis_index("tensor")
    rows, width = own_ref.shape[0], up_all.shape[1]

    @pl.when(pl.program_id(0) == 0)
    def _():
        def copy(source, m):
            return pltpu.make_async_copy(
                source.at[:, start : start + width],
                up_all.at[m * rows : (m + 1) * rows, :],
                sems.at[m],
            )

        copy(own_ref, 0).start()
        copy(e1, 1).start()
        inner = jnp.logical_or(z == 1, z == 2)

        @pl.when(inner)
        def _():
            copy(o2, 2).start()
            copy(o1, 3).start()

        @pl.when(jnp.logical_not(inner))
        def _():
            copy(e2, 2).start()
            copy(e3, 3).start()

        q_t[...] = q_ref[...].T
        for m in range(4):
            copy(own_ref, m).wait()

    first = pl.multiple_of(pl.program_id(0) * tile, tile)
    out_ref[...] = jnp.dot(
        q_t[...], up_all[:, pl.ds(first, tile)], preferred_element_type=jnp.float32
    )


def weight_gradient(q, own, moved, start, width, done=None):
    tokens, depth = q.shape
    hidden = own.shape[1]
    tile = tile_of(width, start)
    before = [] if done is None else [done]
    anywhere = pl.BlockSpec(memory_space=pl.ANY)
    return pl.pallas_call(
        functools.partial(grad_kernel, tile, start),
        out_shape=jax.ShapeDtypeStruct((depth, hidden), jnp.float32),
        grid=(width // tile,),
        in_specs=[whole((tokens, depth))] + [anywhere] * (6 + len(before)),
        out_specs=pl.BlockSpec((depth, tile), lambda n: (0, n + start // tile)),
        input_output_aliases={7: 0} if before else {},
        scratch_shapes=[
            pltpu.VMEM((depth, tokens), jnp.bfloat16),
            pltpu.VMEM((tokens, width), jnp.bfloat16),
            pltpu.SemaphoreType.DMA((4,)),
        ],
        compiler_params=pltpu.CompilerParams(vmem_limit_bytes=48 * MIB),
        cost_estimate=pl.CostEstimate(
            flops=2 * tokens * depth * width,
            bytes_accessed=2 * tokens * (depth + width) + 4 * depth * width,
            transcendentals=0,
        ),
        name="weight_gradient",
    )(q, own, *moved, *before)


def total(*blocks):
    return sum(b.astype(jnp.float32) for b in blocks).astype(jnp.bfloat16)


def move(block, *pairs):
    return lax.ppermute(block, "tensor", pairs)


INWARD = ((0, 1), (3, 2))
MIDDLE = ((1, 2), (2, 1))
OUTWARD = ((1, 0), (2, 3))


def lined(x_tokens, sign_bits, weight, upstream):
    groups = lax.axis_size("tensor")
    z = lax.axis_index("tensor")
    d = lax.axis_index("dp")
    hidden = weight.shape[1]

    pieces = list(signed_pieces(x_tokens, sign_bits, groups))
    for m in (3, 2, 1):
        pieces[m] = swap(pieces[m], "tensor", m)
    turned = list(rotate(pieces))
    (up,) = after([upstream], turned[0])
    for m in (3, 2, 1):
        turned[m] = swap(turned[m], "tensor", m)
    own = jnp.concatenate(
        [lax.select_n(z, *[turned[g ^ k] for k in range(groups)]) for g in range(groups)]
    )

    e1 = swap(up, "tensor", 1)
    o1 = move(up, *MIDDLE)

    gathered = gather_rows(own, d)
    cut = 3 * hidden // 7 // 512 * 512
    q, first = project_first(gathered, weight, cut, groups)
    q, e1, o1 = after([q, e1, o1])
    o2 = move(e1, *MIDDLE)
    e2 = move(o1, *OUTWARD)
    second = project(q, weight, cut, hidden - cut, groups)

    far_a, near_a = move(first[3], *INWARD), move(first[2], *INWARD)
    *second, far_a = after([*second, far_a])
    far_b = move(second[3], *INWARD)
    across_a = move(total(first[2], far_a), *MIDDLE)
    near_a, o2, e2, near_b = after([near_a, o2, e2, second[2]])
    near_b = move(near_b, *INWARD)
    back_a = move(total(first[3], near_a), *MIDDLE)
    e3 = move(o2, *OUTWARD)
    near_b, e3 = after([near_b, e3])
    across_b = move(total(second[2], far_b), *MIDDLE)
    pair_a = swap(total(first[1], across_a), "tensor", 1)
    back_b = move(total(second[3], near_b), *MIDDLE)

    moved = (e1, o1, o2, e2, e3)
    some = hidden // 2 // 512 * 512
    (q_late,) = after([q], across_a, near_b)
    grad = weight_gradient(q_late, upstream, moved, 0, some)
    across_b, grad = after([across_b, grad])
    pair_b = swap(total(second[1], across_b), "tensor", 1)
    (q_late,) = after([q], across_b)
    weight_grad = weight_gradient(q_late, upstream, moved, some, hidden - some, grad)
    projected = jnp.concatenate(
        [total(first[0], pair_a, back_a), total(second[0], pair_b, back_b)], axis=1
    )
    return (projected, weight_grad)


def per_device(x_tokens, sign_bits, weight, upstream):
    rows, width = x_tokens.shape
    hidden = weight.shape[1]
    fits = rows % 64 == 0 and width % 256 == 0 and hidden % 512 == 0 and hidden >= 1536
    if (lax.axis_size("dp"), lax.axis_size("tensor")) == (8, 4) and fits:
        return lined(x_tokens, sign_bits, weight, upstream)
    return plain(x_tokens, sign_bits, weight, upstream)


def solution(mesh):
    in_specs = (P("dp", "tensor"), P("tensor"), P("tensor", "dp"), P("tensor", "dp"))
    out_specs = (P("tensor", "dp"), P("tensor", "dp"))
    return jax.shard_map(
        per_device, mesh=mesh, in_specs=in_specs, out_specs=out_specs, check_vma=False
    )
```

```python
import functools
import math

import jax
import jax.numpy as jnp
from jax import lax
from jax.experimental import pallas as pl
from jax.experimental.pallas import tpu as pltpu
from jax.sharding import PartitionSpec as P

MIB = 1 << 20
VMEM = pl.BlockSpec(memory_space=pltpu.VMEM)


def hadamard(order):
    row_ids = jnp.arange(order, dtype=jnp.int32)[:, None]
    col_ids = jnp.arange(order, dtype=jnp.int32)[None, :]
    common = row_ids & col_ids
    parity = jnp.zeros((order, order), jnp.int32)
    for section_bit in range(max(order.bit_length() - 1, 0)):
        parity = parity + (common >> section_bit & 1)
    return (1 - 2 * (parity % 2)).astype(jnp.bfloat16)


def swap(block, axis, mask):
    count = lax.axis_size(axis)
    return lax.ppermute(
        block, axis, [(i, i ^ mask) for i in range(count) if i ^ mask < count]
    )


def plain(x_tokens, sign_bits, weight, upstream):
    panel_width = x_tokens.shape[1]
    groups = lax.axis_size("tensor")
    factor = 1.0 / math.sqrt(panel_width * groups)
    column_sign = (1 - 2 * sign_bits).astype(jnp.bfloat16)
    current = jnp.dot(
        x_tokens * column_sign[None, :],
        hadamard(panel_width),
        preferred_element_type=jnp.float32,
    )
    position = lax.axis_index("tensor")
    for section_bit in range(groups.bit_length() - 1):
        partner = swap(current.astype(jnp.bfloat16), "tensor", 1 << section_bit).astype(
            current.dtype
        )
        upper_half = position >> section_bit & 1 == 1
        current = jnp.where(upper_half, partner - current, current + partner)
    quantized = (current * factor).astype(jnp.bfloat16)
    gathered = lax.all_gather(quantized, "dp", axis=0, tiled=True)
    projected = lax.psum_scatter(
        jnp.dot(gathered, weight, preferred_element_type=jnp.float32).astype(jnp.bfloat16),
        "tensor",
        scatter_dimension=0,
        tiled=True,
    )
    weight_grad = lax.dot_general(
        gathered,
        lax.all_gather(upstream, "tensor", axis=0, tiled=True),
        (((0,), (0,)), ((), ())),
        preferred_element_type=jnp.float32,
    )
    return (projected, weight_grad)


def parity_sign(bits):
    return (1 - 2 * ((bits ^ bits >> 1) & 1)).astype(jnp.float32)


def butterfly(parts):
    stride = 1
    parts = list(parts)
    while stride < len(parts):
        for low in range(len(parts)):
            if not low & stride:
                a, b = parts[low], parts[low | stride]
                parts[low], parts[low | stride] = a + b, a - b
        stride *= 2
    return parts


def whole(shape):
    return pl.BlockSpec(shape, lambda n: (0,) * len(shape))


def tile_of(width, first=0):
    return next((t for t in (512, 256, 128) if width % t == 0 and first % t == 0), width)


def after(arrays, *earlier):
    arrays = list(arrays)
    return list(lax.optimization_barrier(tuple(arrays) + tuple(earlier))[: len(arrays)])


def sign_kernel(x_ref, bits_ref, *outs):
    z = lax.axis_index("tensor")
    rows = outs[0].shape[0]
    sign = (1 - 2 * bits_ref[...]).astype(jnp.float32)
    for m, out in enumerate(outs):
        first = pl.multiple_of((z ^ m) * rows, rows)
        out[...] = (x_ref[pl.ds(first, rows), :].astype(jnp.float32) * sign).astype(out.dtype)


def signed_pieces(x, sign_bits, groups):
    rows, width = x.shape
    part = rows // groups
    return pl.pallas_call(
        sign_kernel,
        out_shape=[jax.ShapeDtypeStruct((part, width), jnp.bfloat16)] * groups,
        in_specs=[VMEM] * 2,
        out_specs=[VMEM] * groups,
        compiler_params=pltpu.CompilerParams(vmem_limit_bytes=8 * MIB),
        name="signed_pieces",
    )(x, sign_bits.reshape(1, width))


def rotate_kernel(groups, order, factor, h_ref, *refs):
    pieces, outs = refs[:groups], refs[groups:]
    z = lax.axis_index("tensor")
    rows, width = pieces[0].shape
    chunks = width // order
    stacked = jnp.concatenate(
        [piece[:, j * order : (j + 1) * order] for piece in pieces for j in range(chunks)], axis=0
    )
    product = jnp.dot(stacked, h_ref[...], preferred_element_type=jnp.float32)
    rotated = []
    for i in range(groups):
        sign = parity_sign(z & i)
        rotated.append(
            butterfly(
                [
                    product[(i * chunks + j) * rows : (i * chunks + j + 1) * rows] * sign
                    for j in range(chunks)
                ]
            )
        )
    for j in range(chunks):
        panel = butterfly([r[j] for r in rotated])
        for m in range(groups):
            scale = parity_sign((z ^ m) & z) * factor
            outs[m][:, j * order : (j + 1) * order] = (panel[m] * scale).astype(jnp.bfloat16)


def rotate(pieces):
    groups = len(pieces)
    rows, width = pieces[0].shape
    order = min(256, width)
    return pl.pallas_call(
        functools.partial(rotate_kernel, groups, order, 1.0 / math.sqrt(width * groups)),
        out_shape=[jax.ShapeDtypeStruct((rows, width), jnp.bfloat16)] * groups,
        in_specs=[VMEM] * (1 + groups),
        out_specs=[VMEM] * groups,
        compiler_params=pltpu.CompilerParams(vmem_limit_bytes=8 * MIB),
        name="rotate",
    )(hadamard(order), *pieces)


def gather_rows(own, d):
    x, y, core = swap(own, "dp", 2), swap(own, "dp", 4), swap(own, "dp", 1)
    x, y = after([x, y])
    through = jnp.where(d & 1 == 0, x, y)
    diagonal = lax.ppermute(
        through, "dp", [(i, i ^ (4 if i & 1 == 0 else 2)) for i in range(8)]
    )
    return [
        own,
        core,
        x,
        swap(x, "dp", 1),
        y,
        swap(y, "dp", 1),
        diagonal,
        swap(diagonal, "dp", 1),
    ]


def is_outer(z):
    return 1 - ((z ^ z >> 1) & 1)


def slot(m, z):
    return m ^ (m >> 1 & is_outer(z))


def first_kernel(*refs):
    pieces, (w_ref, q_ref, *out_refs, sems) = refs[:8], refs[8:]
    rows = pieces[0].shape[0]

    @pl.when(pl.program_id(0) == 0)
    def _():
        z, d = lax.axis_index("tensor"), lax.axis_index("dp")
        copies = []
        for mask, piece in enumerate(pieces):
            start = slot(((d ^ mask) >> 1) ^ z, z) * (2 * rows) + ((d ^ mask) & 1) * rows
            copies.append(
                pltpu.make_async_copy(
                    piece, q_ref.at[pl.ds(pl.multiple_of(start, rows), rows), :], sems.at[mask]
                )
            )
        for copy in copies:
            copy.start()
        for copy in copies:
            copy.wait()

    project_kernel(q_ref, w_ref, *out_refs)


def project_kernel(q_ref, w_ref, *out_refs):
    product = jnp.dot(q_ref[...], w_ref[...], preferred_element_type=jnp.float32)
    first = 0
    for out_ref in out_refs:
        rows = out_ref.shape[0]
        out_ref[...] = product[first : first + rows].astype(out_ref.dtype)
        first += rows


def project_first(pieces, weight, width, blocks):
    depth = weight.shape[0]
    tokens = sum(blocks)
    tile = tile_of(width)
    q, *products = pl.pallas_call(
        first_kernel,
        out_shape=[
            jax.ShapeDtypeStruct((tokens, depth), jnp.bfloat16),
            *[jax.ShapeDtypeStruct((block, width), jnp.bfloat16) for block in blocks],
        ],
        grid=(width // tile,),
        in_specs=[pl.BlockSpec(memory_space=pl.ANY)] * len(pieces)
        + [pl.BlockSpec((depth, tile), lambda n: (0, n))],
        out_specs=[whole((tokens, depth))]
        + [pl.BlockSpec((block, tile), lambda n: (0, n)) for block in blocks],
        scratch_shapes=[pltpu.SemaphoreType.DMA((len(pieces),))],
        compiler_params=pltpu.CompilerParams(vmem_limit_bytes=48 * MIB),
        cost_estimate=pl.CostEstimate(flops=1, bytes_accessed=1, transcendentals=0),
        name="project_first",
    )(*pieces, weight)
    return q, products


def project(q, weight, first, width, blocks):
    tile = tile_of(width, first)
    tokens, depth = q.shape
    return pl.pallas_call(
        project_kernel,
        out_shape=[jax.ShapeDtypeStruct((block, width), jnp.bfloat16) for block in blocks],
        grid=(width // tile,),
        in_specs=[
            whole((tokens, depth)),
            pl.BlockSpec((depth, tile), lambda n: (0, n + first // tile)),
        ],
        out_specs=[pl.BlockSpec((block, tile), lambda n: (0, n)) for block in blocks],
        compiler_params=pltpu.CompilerParams(vmem_limit_bytes=48 * MIB),
        cost_estimate=pl.CostEstimate(
            flops=2 * tokens * depth * width,
            bytes_accessed=2 * (tokens * depth + depth * width + tokens * width),
            transcendentals=0,
        ),
        name="project",
    )(q, weight)


def transpose_kernel(q_ref, out_ref):
    out_ref[...] = q_ref[...].T


def transposed(q):
    tokens, depth = q.shape
    return pl.pallas_call(
        transpose_kernel,
        out_shape=jax.ShapeDtypeStruct((depth, tokens), jnp.bfloat16),
        in_specs=[VMEM],
        out_specs=VMEM,
        compiler_params=pltpu.CompilerParams(vmem_limit_bytes=16 * MIB),
        name="transposed",
    )(q)


def grad_kernel(tile, start, q_t, own_ref, e1, o1, o2, e2, e3, *refs):
    out_ref, up_all, sems = refs[-3:]
    z = lax.axis_index("tensor")
    rows, width = own_ref.shape[0], up_all.shape[1]

    @pl.when(pl.program_id(0) == 0)
    def _():
        def copy(source, m):
            return pltpu.make_async_copy(
                source.at[:, start : start + width],
                up_all.at[m * rows : (m + 1) * rows, :],
                sems.at[m],
            )

        copy(own_ref, 0).start()
        copy(e1, 1).start()

        @pl.when(is_outer(z) == 0)
        def _():
            copy(o2, 2).start()
            copy(o1, 3).start()

        @pl.when(is_outer(z) == 1)
        def _():
            copy(e3, 2).start()
            copy(e2, 3).start()

        for m in range(4):
            copy(own_ref, m).wait()

    first = pl.multiple_of(pl.program_id(0) * tile, tile)
    out_ref[...] = jnp.dot(
        q_t[...], up_all[:, pl.ds(first, tile)], preferred_element_type=jnp.float32
    )


def weight_gradient(q_t, own, moved, start, width, done=None):
    depth, tokens = q_t.shape
    hidden = own.shape[1]
    tile = tile_of(width, start)
    before = [] if done is None else [done]
    anywhere = pl.BlockSpec(memory_space=pl.ANY)
    return pl.pallas_call(
        functools.partial(grad_kernel, tile, start),
        out_shape=jax.ShapeDtypeStruct((depth, hidden), jnp.float32),
        grid=(width // tile,),
        in_specs=[whole((depth, tokens))] + [anywhere] * (6 + len(before)),
        out_specs=pl.BlockSpec((depth, tile), lambda n: (0, n + start // tile)),
        input_output_aliases={7: 0} if before else {},
        scratch_shapes=[
            pltpu.VMEM((tokens, width), jnp.bfloat16),
            pltpu.SemaphoreType.DMA((4,)),
        ],
        compiler_params=pltpu.CompilerParams(vmem_limit_bytes=48 * MIB),
        cost_estimate=pl.CostEstimate(
            flops=2 * tokens * depth * width,
            bytes_accessed=2 * tokens * (depth + width) + 4 * depth * width,
            transcendentals=0,
        ),
        name="weight_gradient",
    )(q_t, own, *moved, *before)


def total(*blocks):
    return sum(b.astype(jnp.float32) for b in blocks).astype(jnp.bfloat16)


def move(block, *pairs):
    return lax.ppermute(block, "tensor", pairs)


INWARD = ((0, 1), (3, 2))
MIDDLE = ((1, 2), (2, 1))
OUTWARD = ((1, 0), (2, 3))


def lined(x_tokens, sign_bits, weight, upstream):
    groups = lax.axis_size("tensor")
    z = lax.axis_index("tensor")
    d = lax.axis_index("dp")
    rows = x_tokens.shape[0]
    hidden = weight.shape[1]

    pieces = list(signed_pieces(x_tokens, sign_bits, groups))
    for m in (3, 2, 1):
        pieces[m] = swap(pieces[m], "tensor", m)
    turned = list(rotate(pieces))
    (up,) = after([upstream], turned[0])
    for m in (3, 2, 1):
        turned[m] = swap(turned[m], "tensor", m)
    own = jnp.concatenate(
        [lax.select_n(z, *[turned[g ^ k] for k in range(groups)]) for g in range(groups)]
    )

    e1 = swap(up, "tensor", 1)
    o1 = move(up, *MIDDLE)

    gathered = gather_rows(own, d)
    cut = 3 * hidden // 7 // 512 * 512
    block = rows * len(gathered) // groups
    q, *first = project_first(gathered, weight, cut, (block, block, 2 * block))
    own_a, pair_a, beyond_a = first[0]
    q, e1, o1 = after([q, e1, o1])
    o2 = move(e1, *MIDDLE)
    e2 = move(o1, *OUTWARD)
    own_b, pair_b, far_b, near_b = project(q, weight, cut, hidden - cut, (block,) * 4)

    inward_a = move(beyond_a, *INWARD)
    inward_far = move(far_b, *INWARD)
    (inward_near,) = after([near_b], inward_a)
    inward_near = move(inward_near, *INWARD)
    across_a = move(total(beyond_a, inward_a), *MIDDLE)
    e3 = move(o2, *OUTWARD)
    across_far = move(total(far_b, inward_far), *MIDDLE)
    inward_near, e3 = after([inward_near, e3])
    across_near = move(total(near_b, inward_near), *MIDDLE)

    across_a, inward_near = after([across_a, inward_near])
    out_a = swap(total(pair_a, across_a[:block]), "tensor", 1)

    (late,) = after([q], inward_far)
    q_t = transposed(late)
    moved = (e1, o1, o2, e2, e3)
    some = hidden // 3 // 512 * 512
    (late,) = after([q_t], across_a, inward_near)
    grad = weight_gradient(late, upstream, moved, 0, some)
    across_far, grad, out_a = after([across_far, grad, out_a])
    out_b = swap(total(pair_b, across_far), "tensor", 1)
    (late,) = after([q_t], across_far)
    weight_grad = weight_gradient(late, upstream, moved, some, hidden - some, grad)
    projected = jnp.concatenate(
        [total(own_a, out_a, across_a[block:]), total(own_b, out_b, across_near)], axis=1
    )
    return (projected, weight_grad)


def per_device(x_tokens, sign_bits, weight, upstream):
    rows, width = x_tokens.shape
    hidden = weight.shape[1]
    fits = rows % 64 == 0 and width % 256 == 0 and hidden % 512 == 0 and hidden >= 1536
    if (lax.axis_size("dp"), lax.axis_size("tensor")) == (8, 4) and fits:
        return lined(x_tokens, sign_bits, weight, upstream)
    return plain(x_tokens, sign_bits, weight, upstream)


def solution(mesh):
    in_specs = (P("dp", "tensor"), P("tensor"), P("tensor", "dp"), P("tensor", "dp"))
    out_specs = (P("tensor", "dp"), P("tensor", "dp"))
    return jax.shard_map(
        per_device, mesh=mesh, in_specs=in_specs, out_specs=out_specs, check_vma=False
    )
```

```python
import functools
import math

import jax
import jax.numpy as jnp
from jax import lax
from jax.experimental import pallas as pl
from jax.experimental.pallas import tpu as pltpu
from jax.sharding import PartitionSpec as P

MIB = 1 << 20
VMEM = pl.BlockSpec(memory_space=pltpu.VMEM)


def hadamard(order):
    row_ids = jnp.arange(order, dtype=jnp.int32)[:, None]
    col_ids = jnp.arange(order, dtype=jnp.int32)[None, :]
    common = row_ids & col_ids
    parity = jnp.zeros((order, order), jnp.int32)
    for section_bit in range(max(order.bit_length() - 1, 0)):
        parity = parity + (common >> section_bit & 1)
    return (1 - 2 * (parity % 2)).astype(jnp.bfloat16)


def swap(block, axis, mask):
    count = lax.axis_size(axis)
    return lax.ppermute(
        block, axis, [(i, i ^ mask) for i in range(count) if i ^ mask < count]
    )


def plain(x_tokens, sign_bits, weight, upstream):
    panel_width = x_tokens.shape[1]
    groups = lax.axis_size("tensor")
    factor = 1.0 / math.sqrt(panel_width * groups)
    column_sign = (1 - 2 * sign_bits).astype(jnp.bfloat16)
    current = jnp.dot(
        x_tokens * column_sign[None, :],
        hadamard(panel_width),
        preferred_element_type=jnp.float32,
    )
    position = lax.axis_index("tensor")
    for section_bit in range(groups.bit_length() - 1):
        partner = swap(current.astype(jnp.bfloat16), "tensor", 1 << section_bit).astype(
            current.dtype
        )
        upper_half = position >> section_bit & 1 == 1
        current = jnp.where(upper_half, partner - current, current + partner)
    quantized = (current * factor).astype(jnp.bfloat16)
    gathered = lax.all_gather(quantized, "dp", axis=0, tiled=True)
    projected = lax.psum_scatter(
        jnp.dot(gathered, weight, preferred_element_type=jnp.float32).astype(jnp.bfloat16),
        "tensor",
        scatter_dimension=0,
        tiled=True,
    )
    weight_grad = lax.dot_general(
        gathered,
        lax.all_gather(upstream, "tensor", axis=0, tiled=True),
        (((0,), (0,)), ((), ())),
        preferred_element_type=jnp.float32,
    )
    return (projected, weight_grad)


def parity_sign(bits):
    return (1 - 2 * ((bits ^ bits >> 1) & 1)).astype(jnp.float32)


def butterfly(parts):
    stride = 1
    parts = list(parts)
    while stride < len(parts):
        for low in range(len(parts)):
            if not low & stride:
                a, b = parts[low], parts[low | stride]
                parts[low], parts[low | stride] = a + b, a - b
        stride *= 2
    return parts


def whole(shape):
    return pl.BlockSpec(shape, lambda n: (0,) * len(shape))


def tile_of(width, first=0):
    return next((t for t in (512, 256, 128) if width % t == 0 and first % t == 0), width)


def after(arrays, *earlier):
    arrays = list(arrays)
    return list(lax.optimization_barrier(tuple(arrays) + tuple(earlier))[: len(arrays)])


def sign_kernel(x_ref, bits_ref, *outs):
    z = lax.axis_index("tensor")
    rows = outs[0].shape[0]
    sign = (1 - 2 * bits_ref[...]).astype(jnp.float32)
    for m, out in enumerate(outs):
        first = pl.multiple_of((z ^ m) * rows, rows)
        out[...] = (x_ref[pl.ds(first, rows), :].astype(jnp.float32) * sign).astype(out.dtype)


def signed_pieces(x, sign_bits, groups):
    rows, width = x.shape
    part = rows // groups
    return pl.pallas_call(
        sign_kernel,
        out_shape=[jax.ShapeDtypeStruct((part, width), jnp.bfloat16)] * groups,
        in_specs=[VMEM] * 2,
        out_specs=[VMEM] * groups,
        compiler_params=pltpu.CompilerParams(vmem_limit_bytes=8 * MIB),
        name="signed_pieces",
    )(x, sign_bits.reshape(1, width))


def rotate_kernel(groups, order, factor, h_ref, *refs):
    pieces, outs = refs[:groups], refs[groups:]
    z = lax.axis_index("tensor")
    rows, width = pieces[0].shape
    chunks = width // order
    stacked = jnp.concatenate(
        [piece[:, j * order : (j + 1) * order] for piece in pieces for j in range(chunks)], axis=0
    )
    product = jnp.dot(stacked, h_ref[...], preferred_element_type=jnp.float32)
    rotated = []
    for i in range(groups):
        sign = parity_sign(z & i)
        rotated.append(
            butterfly(
                [
                    product[(i * chunks + j) * rows : (i * chunks + j + 1) * rows] * sign
                    for j in range(chunks)
                ]
            )
        )
    for j in range(chunks):
        panel = butterfly([r[j] for r in rotated])
        for m in range(groups):
            scale = parity_sign((z ^ m) & z) * factor
            outs[m][:, j * order : (j + 1) * order] = (panel[m] * scale).astype(jnp.bfloat16)


def rotate(pieces):
    groups = len(pieces)
    rows, width = pieces[0].shape
    order = min(256, width)
    return pl.pallas_call(
        functools.partial(rotate_kernel, groups, order, 1.0 / math.sqrt(width * groups)),
        out_shape=[jax.ShapeDtypeStruct((rows, width), jnp.bfloat16)] * groups,
        in_specs=[VMEM] * (1 + groups),
        out_specs=[VMEM] * groups,
        compiler_params=pltpu.CompilerParams(vmem_limit_bytes=8 * MIB),
        name="rotate",
    )(hadamard(order), *pieces)


def gather_rows(own, d):
    x, y, core = swap(own, "dp", 2), swap(own, "dp", 4), swap(own, "dp", 1)
    x, y = after([x, y])
    through = jnp.where(d & 1 == 0, x, y)
    diagonal = lax.ppermute(
        through, "dp", [(i, i ^ (4 if i & 1 == 0 else 2)) for i in range(8)]
    )
    return [
        own,
        core,
        x,
        swap(x, "dp", 1),
        y,
        swap(y, "dp", 1),
        diagonal,
        swap(diagonal, "dp", 1),
    ]


def is_outer(z):
    return 1 - ((z ^ z >> 1) & 1)


def slot(m, z):
    return m ^ (m >> 1 & is_outer(z))


def first_kernel(*refs):
    pieces, (w_ref, q_ref, *out_refs, sems) = refs[:8], refs[8:]
    rows = pieces[0].shape[0]

    @pl.when(pl.program_id(0) == 0)
    def _():
        z, d = lax.axis_index("tensor"), lax.axis_index("dp")
        copies = []
        for mask, piece in enumerate(pieces):
            start = slot(((d ^ mask) >> 1) ^ z, z) * (2 * rows) + ((d ^ mask) & 1) * rows
            copies.append(
                pltpu.make_async_copy(
                    piece, q_ref.at[pl.ds(pl.multiple_of(start, rows), rows), :], sems.at[mask]
                )
            )
        for copy in copies:
            copy.start()
        for copy in copies:
            copy.wait()

    project_kernel(q_ref, w_ref, *out_refs)


def project_kernel(q_ref, w_ref, *out_refs):
    product = jnp.dot(q_ref[...], w_ref[...], preferred_element_type=jnp.float32)
    first = 0
    for out_ref in out_refs:
        rows = out_ref.shape[0]
        out_ref[...] = product[first : first + rows].astype(out_ref.dtype)
        first += rows


def project_first(pieces, weight, width, blocks):
    depth = weight.shape[0]
    tokens = sum(blocks)
    tile = tile_of(width)
    q, *products = pl.pallas_call(
        first_kernel,
        out_shape=[
            jax.ShapeDtypeStruct((tokens, depth), jnp.bfloat16),
            *[jax.ShapeDtypeStruct((block, width), jnp.bfloat16) for block in blocks],
        ],
        grid=(width // tile,),
        in_specs=[pl.BlockSpec(memory_space=pl.ANY)] * len(pieces)
        + [pl.BlockSpec((depth, tile), lambda n: (0, n))],
        out_specs=[whole((tokens, depth))]
        + [pl.BlockSpec((block, tile), lambda n: (0, n)) for block in blocks],
        scratch_shapes=[pltpu.SemaphoreType.DMA((len(pieces),))],
        compiler_params=pltpu.CompilerParams(vmem_limit_bytes=48 * MIB),
        cost_estimate=pl.CostEstimate(flops=1, bytes_accessed=1, transcendentals=0),
        name="project_first",
    )(*pieces, weight)
    return q, products


def project(q, weight, first, width, blocks):
    tile = tile_of(width, first)
    tokens, depth = q.shape
    return pl.pallas_call(
        project_kernel,
        out_shape=[jax.ShapeDtypeStruct((block, width), jnp.bfloat16) for block in blocks],
        grid=(width // tile,),
        in_specs=[
            whole((tokens, depth)),
            pl.BlockSpec((depth, tile), lambda n: (0, n + first // tile)),
        ],
        out_specs=[pl.BlockSpec((block, tile), lambda n: (0, n)) for block in blocks],
        compiler_params=pltpu.CompilerParams(vmem_limit_bytes=48 * MIB),
        cost_estimate=pl.CostEstimate(
            flops=2 * tokens * depth * width,
            bytes_accessed=2 * (tokens * depth + depth * width + tokens * width),
            transcendentals=0,
        ),
        name="project",
    )(q, weight)


def transpose_kernel(q_ref, out_ref):
    out_ref[...] = q_ref[...].T


def transposed(q):
    tokens, depth = q.shape
    return pl.pallas_call(
        transpose_kernel,
        out_shape=jax.ShapeDtypeStruct((depth, tokens), jnp.bfloat16),
        in_specs=[VMEM],
        out_specs=VMEM,
        compiler_params=pltpu.CompilerParams(vmem_limit_bytes=16 * MIB),
        name="transposed",
    )(q)


def grad_kernel(tile, start, q_t, own_ref, e1, o1, o2, e2, e3, *refs):
    out_ref, up_all, sems = refs[-3:]
    z = lax.axis_index("tensor")
    rows, width = own_ref.shape[0], up_all.shape[1]

    @pl.when(pl.program_id(0) == 0)
    def _():
        def copy(source, m):
            return pltpu.make_async_copy(
                source.at[:, start : start + width],
                up_all.at[m * rows : (m + 1) * rows, :],
                sems.at[m],
            )

        copy(own_ref, 0).start()
        copy(e1, 1).start()

        @pl.when(is_outer(z) == 0)
        def _():
            copy(o2, 2).start()
            copy(o1, 3).start()

        @pl.when(is_outer(z) == 1)
        def _():
            copy(e3, 2).start()
            copy(e2, 3).start()

        for m in range(4):
            copy(own_ref, m).wait()

    first = pl.multiple_of(pl.program_id(0) * tile, tile)
    out_ref[...] = jnp.dot(
        q_t[...], up_all[:, pl.ds(first, tile)], preferred_element_type=jnp.float32
    )


def weight_gradient(q_t, own, moved, start, width, done=None):
    depth, tokens = q_t.shape
    hidden = own.shape[1]
    tile = tile_of(width, start)
    before = [] if done is None else [done]
    anywhere = pl.BlockSpec(memory_space=pl.ANY)
    return pl.pallas_call(
        functools.partial(grad_kernel, tile, start),
        out_shape=jax.ShapeDtypeStruct((depth, hidden), jnp.float32),
        grid=(width // tile,),
        in_specs=[whole((depth, tokens))] + [anywhere] * (6 + len(before)),
        out_specs=pl.BlockSpec((depth, tile), lambda n: (0, n + start // tile)),
        input_output_aliases={7: 0} if before else {},
        scratch_shapes=[
            pltpu.VMEM((tokens, width), jnp.bfloat16),
            pltpu.SemaphoreType.DMA((4,)),
        ],
        compiler_params=pltpu.CompilerParams(vmem_limit_bytes=48 * MIB),
        cost_estimate=pl.CostEstimate(
            flops=2 * tokens * depth * width,
            bytes_accessed=2 * tokens * (depth + width) + 4 * depth * width,
            transcendentals=0,
        ),
        name="weight_gradient",
    )(q_t, own, *moved, *before)


def total(*blocks):
    return sum(b.astype(jnp.float32) for b in blocks).astype(jnp.bfloat16)


def move(block, *pairs):
    return lax.ppermute(block, "tensor", pairs)


INWARD = ((0, 1), (3, 2))
MIDDLE = ((1, 2), (2, 1))
OUTWARD = ((1, 0), (2, 3))


def lined(x_tokens, sign_bits, weight, upstream):
    groups = lax.axis_size("tensor")
    z = lax.axis_index("tensor")
    d = lax.axis_index("dp")
    rows = x_tokens.shape[0]
    hidden = weight.shape[1]

    pieces = list(signed_pieces(x_tokens, sign_bits, groups))
    for m in (3, 2, 1):
        pieces[m] = swap(pieces[m], "tensor", m)
    turned = list(rotate(pieces))
    (up,) = after([upstream], turned[0])
    for m in (3, 2, 1):
        turned[m] = swap(turned[m], "tensor", m)
    own = jnp.concatenate(
        [lax.select_n(z, *[turned[g ^ k] for k in range(groups)]) for g in range(groups)]
    )

    e1 = swap(up, "tensor", 1)
    o1 = move(up, *MIDDLE)

    gathered = gather_rows(own, d)
    cut = 3 * hidden // 7 // 512 * 512
    block = rows * len(gathered) // groups
    q, *first = project_first(gathered, weight, cut, (block, block, 2 * block))
    own_a, pair_a, beyond_a = first[0]
    q, e1, o1 = after([q, e1, o1])
    o2 = move(e1, *MIDDLE)
    e2 = move(o1, *OUTWARD)
    own_b, pair_b, far_b, near_b = project(q, weight, cut, hidden - cut, (block,) * 4)

    inward_a = move(beyond_a, *INWARD)
    inward_far = move(far_b, *INWARD)
    (inward_near,) = after([near_b], inward_a)
    inward_near = move(inward_near, *INWARD)
    across_a = move(total(beyond_a, inward_a), *MIDDLE)
    o2, e2 = after([o2, e2], inward_a)
    e3 = move(o2, *OUTWARD)
    inward_far, o2, e2 = after([inward_far, o2, e2])
    across_far = move(total(far_b, inward_far), *MIDDLE)
    across_a, e3 = after([across_a, e3])
    out_a = swap(total(pair_a, across_a[:block]), "tensor", 1)

    (late,) = after([q], inward_far)
    q_t = transposed(late)
    moved = (e1, o1, o2, e2, e3)
    some = hidden // 2 // 512 * 512
    (late,) = after([q_t], across_a, inward_near)
    grad = weight_gradient(late, upstream, moved, 0, some)

    across_near = move(total(near_b, inward_near), *MIDDLE)
    across_far, grad, out_a = after([across_far, grad, out_a])
    out_b = swap(total(pair_b, across_far), "tensor", 1)
    (late,) = after([q_t], across_far)
    weight_grad = weight_gradient(late, upstream, moved, some, hidden - some, grad)
    projected = jnp.concatenate(
        [total(own_a, out_a, across_a[block:]), total(own_b, out_b, across_near)], axis=1
    )
    return (projected, weight_grad)


def per_device(x_tokens, sign_bits, weight, upstream):
    rows, width = x_tokens.shape
    hidden = weight.shape[1]
    fits = rows % 64 == 0 and width % 256 == 0 and hidden % 512 == 0 and hidden >= 1536
    if (lax.axis_size("dp"), lax.axis_size("tensor")) == (8, 4) and fits:
        return lined(x_tokens, sign_bits, weight, upstream)
    return plain(x_tokens, sign_bits, weight, upstream)


def solution(mesh):
    in_specs = (P("dp", "tensor"), P("tensor"), P("tensor", "dp"), P("tensor", "dp"))
    out_specs = (P("tensor", "dp"), P("tensor", "dp"))
    return jax.shard_map(
        per_device, mesh=mesh, in_specs=in_specs, out_specs=out_specs, check_vma=False
    )
```

```python
import functools
import math

import jax
import jax.numpy as jnp
from jax import lax
from jax.experimental import pallas as pl
from jax.experimental.pallas import tpu as pltpu
from jax.sharding import PartitionSpec as P

MIB = 1 << 20
VMEM = pl.BlockSpec(memory_space=pltpu.VMEM)


def hadamard(order):
    row_ids = jnp.arange(order, dtype=jnp.int32)[:, None]
    col_ids = jnp.arange(order, dtype=jnp.int32)[None, :]
    common = row_ids & col_ids
    parity = jnp.zeros((order, order), jnp.int32)
    for section_bit in range(max(order.bit_length() - 1, 0)):
        parity = parity + (common >> section_bit & 1)
    return (1 - 2 * (parity % 2)).astype(jnp.bfloat16)


def swap(block, axis, mask):
    count = lax.axis_size(axis)
    return lax.ppermute(
        block, axis, [(i, i ^ mask) for i in range(count) if i ^ mask < count]
    )


def plain(x_tokens, sign_bits, weight, upstream):
    panel_width = x_tokens.shape[1]
    groups = lax.axis_size("tensor")
    factor = 1.0 / math.sqrt(panel_width * groups)
    column_sign = (1 - 2 * sign_bits).astype(jnp.bfloat16)
    current = jnp.dot(
        x_tokens * column_sign[None, :],
        hadamard(panel_width),
        preferred_element_type=jnp.float32,
    )
    position = lax.axis_index("tensor")
    for section_bit in range(groups.bit_length() - 1):
        partner = swap(current.astype(jnp.bfloat16), "tensor", 1 << section_bit).astype(
            current.dtype
        )
        upper_half = position >> section_bit & 1 == 1
        current = jnp.where(upper_half, partner - current, current + partner)
    quantized = (current * factor).astype(jnp.bfloat16)
    gathered = lax.all_gather(quantized, "dp", axis=0, tiled=True)
    projected = lax.psum_scatter(
        jnp.dot(gathered, weight, preferred_element_type=jnp.float32).astype(jnp.bfloat16),
        "tensor",
        scatter_dimension=0,
        tiled=True,
    )
    weight_grad = lax.dot_general(
        gathered,
        lax.all_gather(upstream, "tensor", axis=0, tiled=True),
        (((0,), (0,)), ((), ())),
        preferred_element_type=jnp.float32,
    )
    return (projected, weight_grad)


def parity_sign(bits):
    return (1 - 2 * ((bits ^ bits >> 1) & 1)).astype(jnp.float32)


def butterfly(parts):
    stride = 1
    parts = list(parts)
    while stride < len(parts):
        for low in range(len(parts)):
            if not low & stride:
                a, b = parts[low], parts[low | stride]
                parts[low], parts[low | stride] = a + b, a - b
        stride *= 2
    return parts


def whole(shape):
    return pl.BlockSpec(shape, lambda n: (0,) * len(shape))


def tile_of(width, first=0):
    return next((t for t in (512, 256, 128) if width % t == 0 and first % t == 0), width)


def after(arrays, *earlier):
    arrays = list(arrays)
    return list(lax.optimization_barrier(tuple(arrays) + tuple(earlier))[: len(arrays)])


def sign_kernel(x_ref, bits_ref, *outs):
    z = lax.axis_index("tensor")
    rows = outs[0].shape[0]
    sign = (1 - 2 * bits_ref[...]).astype(jnp.float32)
    for m, out in enumerate(outs):
        first = pl.multiple_of((z ^ m) * rows, rows)
        out[...] = (x_ref[pl.ds(first, rows), :].astype(jnp.float32) * sign).astype(out.dtype)


def signed_pieces(x, sign_bits, groups):
    rows, width = x.shape
    part = rows // groups
    return pl.pallas_call(
        sign_kernel,
        out_shape=[jax.ShapeDtypeStruct((part, width), jnp.bfloat16)] * groups,
        in_specs=[VMEM] * 2,
        out_specs=[VMEM] * groups,
        compiler_params=pltpu.CompilerParams(vmem_limit_bytes=8 * MIB),
        name="signed_pieces",
    )(x, sign_bits.reshape(1, width))


def rotate_kernel(groups, order, factor, h_ref, *refs):
    pieces, outs = refs[:groups], refs[groups:]
    z = lax.axis_index("tensor")
    rows, width = pieces[0].shape
    chunks = width // order
    stacked = jnp.concatenate(
        [piece[:, j * order : (j + 1) * order] for piece in pieces for j in range(chunks)], axis=0
    )
    product = jnp.dot(stacked, h_ref[...], preferred_element_type=jnp.float32)
    rotated = []
    for i in range(groups):
        sign = parity_sign(z & i)
        rotated.append(
            butterfly(
                [
                    product[(i * chunks + j) * rows : (i * chunks + j + 1) * rows] * sign
                    for j in range(chunks)
                ]
            )
        )
    for j in range(chunks):
        panel = butterfly([r[j] for r in rotated])
        for m in range(groups):
            scale = parity_sign((z ^ m) & z) * factor
            outs[m][:, j * order : (j + 1) * order] = (panel[m] * scale).astype(jnp.bfloat16)


def rotate(pieces):
    groups = len(pieces)
    rows, width = pieces[0].shape
    order = min(256, width)
    return pl.pallas_call(
        functools.partial(rotate_kernel, groups, order, 1.0 / math.sqrt(width * groups)),
        out_shape=[jax.ShapeDtypeStruct((rows, width), jnp.bfloat16)] * groups,
        in_specs=[VMEM] * (1 + groups),
        out_specs=[VMEM] * groups,
        compiler_params=pltpu.CompilerParams(vmem_limit_bytes=8 * MIB),
        name="rotate",
    )(hadamard(order), *pieces)


def gather_rows(own, d):
    x, y, core = swap(own, "dp", 2), swap(own, "dp", 4), swap(own, "dp", 1)
    x, y = after([x, y])
    through = jnp.where(d & 1 == 0, x, y)
    diagonal = lax.ppermute(
        through, "dp", [(i, i ^ (4 if i & 1 == 0 else 2)) for i in range(8)]
    )
    return [
        own,
        core,
        x,
        swap(x, "dp", 1),
        y,
        swap(y, "dp", 1),
        diagonal,
        swap(diagonal, "dp", 1),
    ]


def is_outer(z):
    return 1 - ((z ^ z >> 1) & 1)


def slot(m, z):
    return m ^ (m >> 1 & is_outer(z))


def first_kernel(*refs):
    pieces, (w_ref, q_ref, *out_refs, sems) = refs[:8], refs[8:]
    rows = pieces[0].shape[0]

    @pl.when(pl.program_id(0) == 0)
    def _():
        z, d = lax.axis_index("tensor"), lax.axis_index("dp")
        copies = []
        for mask, piece in enumerate(pieces):
            start = slot(((d ^ mask) >> 1) ^ z, z) * (2 * rows) + ((d ^ mask) & 1) * rows
            copies.append(
                pltpu.make_async_copy(
                    piece, q_ref.at[pl.ds(pl.multiple_of(start, rows), rows), :], sems.at[mask]
                )
            )
        for copy in copies:
            copy.start()
        for copy in copies:
            copy.wait()

    project_kernel(q_ref, w_ref, *out_refs)


def project_kernel(q_ref, w_ref, *out_refs):
    product = jnp.dot(q_ref[...], w_ref[...], preferred_element_type=jnp.float32)
    first = 0
    for out_ref in out_refs:
        rows = out_ref.shape[0]
        out_ref[...] = product[first : first + rows].astype(out_ref.dtype)
        first += rows


def project_first(pieces, weight, width, blocks):
    depth = weight.shape[0]
    tokens = sum(blocks)
    tile = tile_of(width)
    q, *products = pl.pallas_call(
        first_kernel,
        out_shape=[
            jax.ShapeDtypeStruct((tokens, depth), jnp.bfloat16),
            *[jax.ShapeDtypeStruct((block, width), jnp.bfloat16) for block in blocks],
        ],
        grid=(width // tile,),
        in_specs=[pl.BlockSpec(memory_space=pl.ANY)] * len(pieces)
        + [pl.BlockSpec((depth, tile), lambda n: (0, n))],
        out_specs=[whole((tokens, depth))]
        + [pl.BlockSpec((block, tile), lambda n: (0, n)) for block in blocks],
        scratch_shapes=[pltpu.SemaphoreType.DMA((len(pieces),))],
        compiler_params=pltpu.CompilerParams(vmem_limit_bytes=48 * MIB),
        cost_estimate=pl.CostEstimate(flops=1, bytes_accessed=1, transcendentals=0),
        name="project_first",
    )(*pieces, weight)
    return q, products


def project(q, weight, first, width, blocks):
    tile = tile_of(width, first)
    tokens, depth = q.shape
    return pl.pallas_call(
        project_kernel,
        out_shape=[jax.ShapeDtypeStruct((block, width), jnp.bfloat16) for block in blocks],
        grid=(width // tile,),
        in_specs=[
            whole((tokens, depth)),
            pl.BlockSpec((depth, tile), lambda n: (0, n + first // tile)),
        ],
        out_specs=[pl.BlockSpec((block, tile), lambda n: (0, n)) for block in blocks],
        compiler_params=pltpu.CompilerParams(vmem_limit_bytes=48 * MIB),
        cost_estimate=pl.CostEstimate(
            flops=2 * tokens * depth * width,
            bytes_accessed=2 * (tokens * depth + depth * width + tokens * width),
            transcendentals=0,
        ),
        name="project",
    )(q, weight)


def transpose_kernel(q_ref, out_ref):
    out_ref[...] = q_ref[...].T


def transposed(q):
    tokens, depth = q.shape
    return pl.pallas_call(
        transpose_kernel,
        out_shape=jax.ShapeDtypeStruct((depth, tokens), jnp.bfloat16),
        in_specs=[VMEM],
        out_specs=VMEM,
        compiler_params=pltpu.CompilerParams(vmem_limit_bytes=16 * MIB),
        name="transposed",
    )(q)


def grad_kernel(tile, start, q_t, own_ref, e1, o1, o2, e2, e3, *refs):
    out_ref, up_all, sems = refs[-3:]
    z = lax.axis_index("tensor")
    rows, width = own_ref.shape[0], up_all.shape[1]

    @pl.when(pl.program_id(0) == 0)
    def _():
        def copy(source, m):
            return pltpu.make_async_copy(
                source.at[:, start : start + width],
                up_all.at[m * rows : (m + 1) * rows, :],
                sems.at[m],
            )

        copy(own_ref, 0).start()
        copy(e1, 1).start()

        @pl.when(is_outer(z) == 0)
        def _():
            copy(o2, 2).start()
            copy(o1, 3).start()

        @pl.when(is_outer(z) == 1)
        def _():
            copy(e3, 2).start()
            copy(e2, 3).start()

        for m in range(4):
            copy(own_ref, m).wait()

    first = pl.multiple_of(pl.program_id(0) * tile, tile)
    out_ref[...] = jnp.dot(
        q_t[...], up_all[:, pl.ds(first, tile)], preferred_element_type=jnp.float32
    )


def weight_gradient(q_t, own, moved, start, width, done=None):
    depth, tokens = q_t.shape
    hidden = own.shape[1]
    tile = tile_of(width, start)
    before = [] if done is None else [done]
    anywhere = pl.BlockSpec(memory_space=pl.ANY)
    return pl.pallas_call(
        functools.partial(grad_kernel, tile, start),
        out_shape=jax.ShapeDtypeStruct((depth, hidden), jnp.float32),
        grid=(width // tile,),
        in_specs=[whole((depth, tokens))] + [anywhere] * (6 + len(before)),
        out_specs=pl.BlockSpec((depth, tile), lambda n: (0, n + start // tile)),
        input_output_aliases={7: 0} if before else {},
        scratch_shapes=[
            pltpu.VMEM((tokens, width), jnp.bfloat16),
            pltpu.SemaphoreType.DMA((4,)),
        ],
        compiler_params=pltpu.CompilerParams(vmem_limit_bytes=28 * MIB),
        cost_estimate=pl.CostEstimate(
            flops=2 * tokens * depth * width,
            bytes_accessed=2 * tokens * (depth + width) + 4 * depth * width,
            transcendentals=0,
        ),
        name="weight_gradient",
    )(q_t, own, *moved, *before)


def total(*blocks):
    return sum(b.astype(jnp.float32) for b in blocks).astype(jnp.bfloat16)


def move(block, *pairs):
    return lax.ppermute(block, "tensor", pairs)


INWARD = ((0, 1), (3, 2))
MIDDLE = ((1, 2), (2, 1))
OUTWARD = ((1, 0), (2, 3))


def lined(x_tokens, sign_bits, weight, upstream):
    groups = lax.axis_size("tensor")
    z = lax.axis_index("tensor")
    d = lax.axis_index("dp")
    rows = x_tokens.shape[0]
    hidden = weight.shape[1]

    pieces = list(signed_pieces(x_tokens, sign_bits, groups))
    for m in (3, 2, 1):
        pieces[m] = swap(pieces[m], "tensor", m)
    turned = list(rotate(pieces))
    (up,) = after([upstream], turned[0])
    for m in (3, 2, 1):
        turned[m] = swap(turned[m], "tensor", m)
    own = jnp.concatenate(
        [lax.select_n(z, *[turned[g ^ k] for k in range(groups)]) for g in range(groups)]
    )

    e1 = swap(up, "tensor", 1)
    o1 = move(up, *MIDDLE)

    gathered = gather_rows(own, d)
    cut = 3 * hidden // 7 // 512 * 512
    block = rows * len(gathered) // groups
    q, *first = project_first(gathered, weight, cut, (block, block, 2 * block))
    own_a, pair_a, beyond_a = first[0]
    q, e1, o1 = after([q, e1, o1])
    o2 = move(e1, *MIDDLE)
    e2 = move(o1, *OUTWARD)
    own_b, pair_b, far_b, near_b = project(q, weight, cut, hidden - cut, (block,) * 4)

    inward_a = move(beyond_a, *INWARD)
    inward_far = move(far_b, *INWARD)
    (inward_near,) = after([near_b], inward_a)
    inward_near = move(inward_near, *INWARD)
    across_a = move(total(beyond_a, inward_a), *MIDDLE)
    o2, e2 = after([o2, e2], inward_a)
    e3 = move(o2, *OUTWARD)
    inward_far, o2, e2 = after([inward_far, o2, e2])
    across_far = move(total(far_b, inward_far), *MIDDLE)
    out_a = swap(total(pair_a, across_a[:block]), "tensor", 1)

    (late,) = after([q], inward_far)
    q_t = transposed(late)
    moved = (e1, o1, o2, e2, e3)
    some = hidden // 2 // 512 * 512
    (late,) = after([q_t], across_a)
    grad = weight_gradient(late, upstream, moved, 0, some)

    inward_near, grad = after([inward_near, grad])
    across_near = move(total(near_b, inward_near), *MIDDLE)
    across_far, grad, out_a = after([across_far, grad, out_a])
    out_b = swap(total(pair_b, across_far), "tensor", 1)
    (late,) = after([q_t], across_far)
    weight_grad = weight_gradient(late, upstream, moved, some, hidden - some, grad)
    projected = jnp.concatenate(
        [total(own_a, out_a, across_a[block:]), total(own_b, out_b, across_near)], axis=1
    )
    return (projected, weight_grad)


def per_device(x_tokens, sign_bits, weight, upstream):
    rows, width = x_tokens.shape
    hidden = weight.shape[1]
    fits = rows % 64 == 0 and width % 256 == 0 and hidden % 512 == 0 and hidden >= 1536
    if (lax.axis_size("dp"), lax.axis_size("tensor")) == (8, 4) and fits:
        return lined(x_tokens, sign_bits, weight, upstream)
    return plain(x_tokens, sign_bits, weight, upstream)


def solution(mesh):
    in_specs = (P("dp", "tensor"), P("tensor"), P("tensor", "dp"), P("tensor", "dp"))
    out_specs = (P("tensor", "dp"), P("tensor", "dp"))
    return jax.shard_map(
        per_device, mesh=mesh, in_specs=in_specs, out_specs=out_specs, check_vma=False
    )
```

```python
import functools
import math

import jax
import jax.numpy as jnp
from jax import lax
from jax.experimental import pallas as pl
from jax.experimental.pallas import tpu as pltpu
from jax.sharding import PartitionSpec as P

MIB = 1 << 20
VMEM = pl.BlockSpec(memory_space=pltpu.VMEM)


def hadamard(order):
    row_ids = jnp.arange(order, dtype=jnp.int32)[:, None]
    col_ids = jnp.arange(order, dtype=jnp.int32)[None, :]
    common = row_ids & col_ids
    parity = jnp.zeros((order, order), jnp.int32)
    for section_bit in range(max(order.bit_length() - 1, 0)):
        parity = parity + (common >> section_bit & 1)
    return (1 - 2 * (parity % 2)).astype(jnp.bfloat16)


def swap(block, axis, mask):
    count = lax.axis_size(axis)
    return lax.ppermute(
        block, axis, [(i, i ^ mask) for i in range(count) if i ^ mask < count]
    )


def plain(x_tokens, sign_bits, weight, upstream):
    panel_width = x_tokens.shape[1]
    groups = lax.axis_size("tensor")
    factor = 1.0 / math.sqrt(panel_width * groups)
    column_sign = (1 - 2 * sign_bits).astype(jnp.bfloat16)
    current = jnp.dot(
        x_tokens * column_sign[None, :],
        hadamard(panel_width),
        preferred_element_type=jnp.float32,
    )
    position = lax.axis_index("tensor")
    for section_bit in range(groups.bit_length() - 1):
        partner = swap(current.astype(jnp.bfloat16), "tensor", 1 << section_bit).astype(
            current.dtype
        )
        upper_half = position >> section_bit & 1 == 1
        current = jnp.where(upper_half, partner - current, current + partner)
    quantized = (current * factor).astype(jnp.bfloat16)
    gathered = lax.all_gather(quantized, "dp", axis=0, tiled=True)
    projected = lax.psum_scatter(
        jnp.dot(gathered, weight, preferred_element_type=jnp.float32).astype(jnp.bfloat16),
        "tensor",
        scatter_dimension=0,
        tiled=True,
    )
    weight_grad = lax.dot_general(
        gathered,
        lax.all_gather(upstream, "tensor", axis=0, tiled=True),
        (((0,), (0,)), ((), ())),
        preferred_element_type=jnp.float32,
    )
    return (projected, weight_grad)


def parity_sign(bits):
    return (1 - 2 * ((bits ^ bits >> 1) & 1)).astype(jnp.float32)


def butterfly(parts):
    stride = 1
    parts = list(parts)
    while stride < len(parts):
        for low in range(len(parts)):
            if not low & stride:
                a, b = parts[low], parts[low | stride]
                parts[low], parts[low | stride] = a + b, a - b
        stride *= 2
    return parts


def whole(shape):
    return pl.BlockSpec(shape, lambda n: (0,) * len(shape))


def tile_of(width, first=0):
    return next((t for t in (512, 256, 128) if width % t == 0 and first % t == 0), width)


def after(arrays, *earlier):
    arrays = list(arrays)
    return list(lax.optimization_barrier(tuple(arrays) + tuple(earlier))[: len(arrays)])


def sign_kernel(x_ref, bits_ref, *outs):
    z = lax.axis_index("tensor")
    rows = outs[0].shape[0]
    sign = (1 - 2 * bits_ref[...]).astype(jnp.float32)
    for m, out in enumerate(outs):
        first = pl.multiple_of((z ^ m) * rows, rows)
        out[...] = (x_ref[pl.ds(first, rows), :].astype(jnp.float32) * sign).astype(out.dtype)


def signed_pieces(x, sign_bits, groups):
    rows, width = x.shape
    part = rows // groups
    return pl.pallas_call(
        sign_kernel,
        out_shape=[jax.ShapeDtypeStruct((part, width), jnp.bfloat16)] * groups,
        in_specs=[VMEM] * 2,
        out_specs=[VMEM] * groups,
        compiler_params=pltpu.CompilerParams(vmem_limit_bytes=8 * MIB),
        name="signed_pieces",
    )(x, sign_bits.reshape(1, width))


def rotate_kernel(groups, order, factor, h_ref, *refs):
    pieces, outs = refs[:groups], refs[groups:]
    z = lax.axis_index("tensor")
    rows, width = pieces[0].shape
    chunks = width // order
    stacked = jnp.concatenate(
        [piece[:, j * order : (j + 1) * order] for piece in pieces for j in range(chunks)], axis=0
    )
    product = jnp.dot(stacked, h_ref[...], preferred_element_type=jnp.float32)
    rotated = []
    for i in range(groups):
        sign = parity_sign(z & i)
        rotated.append(
            butterfly(
                [
                    product[(i * chunks + j) * rows : (i * chunks + j + 1) * rows] * sign
                    for j in range(chunks)
                ]
            )
        )
    for j in range(chunks):
        panel = butterfly([r[j] for r in rotated])
        for m in range(groups):
            scale = parity_sign((z ^ m) & z) * factor
            outs[m][:, j * order : (j + 1) * order] = (panel[m] * scale).astype(jnp.bfloat16)


def rotate(pieces):
    groups = len(pieces)
    rows, width = pieces[0].shape
    order = min(256, width)
    return pl.pallas_call(
        functools.partial(rotate_kernel, groups, order, 1.0 / math.sqrt(width * groups)),
        out_shape=[jax.ShapeDtypeStruct((rows, width), jnp.bfloat16)] * groups,
        in_specs=[VMEM] * (1 + groups),
        out_specs=[VMEM] * groups,
        compiler_params=pltpu.CompilerParams(vmem_limit_bytes=8 * MIB),
        name="rotate",
    )(hadamard(order), *pieces)


def gather_rows(own, d):
    x, y, core = swap(own, "dp", 2), swap(own, "dp", 4), swap(own, "dp", 1)
    x, y = after([x, y])
    through = jnp.where(d & 1 == 0, x, y)
    diagonal = lax.ppermute(
        through, "dp", [(i, i ^ (4 if i & 1 == 0 else 2)) for i in range(8)]
    )
    return [
        own,
        core,
        x,
        swap(x, "dp", 1),
        y,
        swap(y, "dp", 1),
        diagonal,
        swap(diagonal, "dp", 1),
    ]


def is_outer(z):
    return 1 - ((z ^ z >> 1) & 1)


def slot(m, z):
    return m ^ (m >> 1 & is_outer(z))


def first_kernel(*refs):
    pieces, (w_ref, q_ref, *out_refs, sems) = refs[:8], refs[8:]
    rows = pieces[0].shape[0]

    @pl.when(pl.program_id(0) == 0)
    def _():
        z, d = lax.axis_index("tensor"), lax.axis_index("dp")
        copies = []
        for mask, piece in enumerate(pieces):
            start = slot(((d ^ mask) >> 1) ^ z, z) * (2 * rows) + ((d ^ mask) & 1) * rows
            copies.append(
                pltpu.make_async_copy(
                    piece, q_ref.at[pl.ds(pl.multiple_of(start, rows), rows), :], sems.at[mask]
                )
            )
        for copy in copies:
            copy.start()
        for copy in copies:
            copy.wait()

    project_kernel(q_ref, w_ref, *out_refs)


def project_kernel(q_ref, w_ref, *out_refs):
    product = jnp.dot(q_ref[...], w_ref[...], preferred_element_type=jnp.float32)
    first = 0
    for out_ref in out_refs:
        rows = out_ref.shape[0]
        out_ref[...] = product[first : first + rows].astype(out_ref.dtype)
        first += rows


def project_first(pieces, weight, width, blocks):
    depth = weight.shape[0]
    tokens = sum(blocks)
    tile = tile_of(width)
    q, *products = pl.pallas_call(
        first_kernel,
        out_shape=[
            jax.ShapeDtypeStruct((tokens, depth), jnp.bfloat16),
            *[jax.ShapeDtypeStruct((block, width), jnp.bfloat16) for block in blocks],
        ],
        grid=(width // tile,),
        in_specs=[pl.BlockSpec(memory_space=pl.ANY)] * len(pieces)
        + [pl.BlockSpec((depth, tile), lambda n: (0, n))],
        out_specs=[whole((tokens, depth))]
        + [pl.BlockSpec((block, tile), lambda n: (0, n)) for block in blocks],
        scratch_shapes=[pltpu.SemaphoreType.DMA((len(pieces),))],
        compiler_params=pltpu.CompilerParams(vmem_limit_bytes=48 * MIB),
        cost_estimate=pl.CostEstimate(flops=1, bytes_accessed=1, transcendentals=0),
        name="project_first",
    )(*pieces, weight)
    return q, products


def project(q, weight, first, width, blocks):
    tile = tile_of(width, first)
    tokens, depth = q.shape
    return pl.pallas_call(
        project_kernel,
        out_shape=[jax.ShapeDtypeStruct((block, width), jnp.bfloat16) for block in blocks],
        grid=(width // tile,),
        in_specs=[
            whole((tokens, depth)),
            pl.BlockSpec((depth, tile), lambda n: (0, n + first // tile)),
        ],
        out_specs=[pl.BlockSpec((block, tile), lambda n: (0, n)) for block in blocks],
        compiler_params=pltpu.CompilerParams(vmem_limit_bytes=48 * MIB),
        cost_estimate=pl.CostEstimate(
            flops=2 * tokens * depth * width,
            bytes_accessed=2 * (tokens * depth + depth * width + tokens * width),
            transcendentals=0,
        ),
        name="project",
    )(q, weight)


def transpose_kernel(q_ref, out_ref):
    out_ref[...] = q_ref[...].T


def transposed(q):
    tokens, depth = q.shape
    return pl.pallas_call(
        transpose_kernel,
        out_shape=jax.ShapeDtypeStruct((depth, tokens), jnp.bfloat16),
        in_specs=[VMEM],
        out_specs=VMEM,
        compiler_params=pltpu.CompilerParams(vmem_limit_bytes=16 * MIB),
        name="transposed",
    )(q)


def grad_kernel(tile, start, q_t, own_ref, e1, o1, o2, e2, e3, *refs):
    out_ref, up_all, sems = refs[-3:]
    z = lax.axis_index("tensor")
    rows, width = own_ref.shape[0], up_all.shape[1]

    def columns(source):
        first = 0 if source.shape[1] == width else start
        return source.at[:, first : first + width]

    @pl.when(pl.program_id(0) == 0)
    def _():
        def copy(source, m):
            return pltpu.make_async_copy(
                columns(source),
                up_all.at[m * rows : (m + 1) * rows, :],
                sems.at[m],
            )

        copy(own_ref, 0).start()
        copy(e1, 1).start()

        @pl.when(is_outer(z) == 0)
        def _():
            copy(o2, 2).start()
            copy(o1, 3).start()

        @pl.when(is_outer(z) == 1)
        def _():
            copy(e3, 2).start()
            copy(e2, 3).start()

        for m in range(4):
            copy(own_ref, m).wait()

    first = pl.multiple_of(pl.program_id(0) * tile, tile)
    out_ref[...] = jnp.dot(
        q_t[...], up_all[:, pl.ds(first, tile)], preferred_element_type=jnp.float32
    )


def weight_gradient(q_t, own, moved, start, width, done=None):
    depth, tokens = q_t.shape
    hidden = own.shape[1]
    tile = tile_of(width, start)
    before = [] if done is None else [done]
    anywhere = pl.BlockSpec(memory_space=pl.ANY)
    return pl.pallas_call(
        functools.partial(grad_kernel, tile, start),
        out_shape=jax.ShapeDtypeStruct((depth, hidden), jnp.float32),
        grid=(width // tile,),
        in_specs=[whole((depth, tokens))] + [anywhere] * (6 + len(before)),
        out_specs=pl.BlockSpec((depth, tile), lambda n: (0, n + start // tile)),
        input_output_aliases={7: 0} if before else {},
        scratch_shapes=[
            pltpu.VMEM((tokens, width), jnp.bfloat16),
            pltpu.SemaphoreType.DMA((4,)),
        ],
        compiler_params=pltpu.CompilerParams(vmem_limit_bytes=28 * MIB),
        cost_estimate=pl.CostEstimate(
            flops=2 * tokens * depth * width,
            bytes_accessed=2 * tokens * (depth + width) + 4 * depth * width,
            transcendentals=0,
        ),
        name="weight_gradient",
    )(q_t, own, *moved, *before)


def total(*blocks):
    return sum(b.astype(jnp.float32) for b in blocks).astype(jnp.bfloat16)


def move(block, *pairs):
    return lax.ppermute(block, "tensor", pairs)


INWARD = ((0, 1), (3, 2))
MIDDLE = ((1, 2), (2, 1))
OUTWARD = ((1, 0), (2, 3))


def lined(x_tokens, sign_bits, weight, upstream):
    groups = lax.axis_size("tensor")
    z = lax.axis_index("tensor")
    d = lax.axis_index("dp")
    rows = x_tokens.shape[0]
    hidden = weight.shape[1]

    pieces = list(signed_pieces(x_tokens, sign_bits, groups))
    for m in (3, 2, 1):
        pieces[m] = swap(pieces[m], "tensor", m)
    turned = list(rotate(pieces))
    (up,) = after([upstream], turned[0])
    for m in (3, 2, 1):
        turned[m] = swap(turned[m], "tensor", m)
    own = jnp.concatenate(
        [lax.select_n(z, *[turned[g ^ k] for k in range(groups)]) for g in range(groups)]
    )

    e1 = swap(up, "tensor", 1)
    o1 = move(up, *MIDDLE)

    gathered = gather_rows(own, d)
    cut = 3 * hidden // 7 // 512 * 512
    block = rows * len(gathered) // groups
    q, *first = project_first(gathered, weight, cut, (block, block, 2 * block))
    own_a, pair_a, beyond_a = first[0]
    q, e1, o1 = after([q, e1, o1])
    some = (hidden // 512 + 1) // 2 * 512
    o2_a, o2_b = move(e1[:, :some], *MIDDLE), move(e1[:, some:], *MIDDLE)
    e2 = move(o1, *OUTWARD)
    own_b, pair_b, far_b, near_b = project(q, weight, cut, hidden - cut, (block,) * 4)

    inward_a = move(beyond_a, *INWARD)
    inward_far = move(far_b, *INWARD)
    (inward_near,) = after([near_b], inward_a)
    inward_near = move(inward_near, *INWARD)
    across_a = move(total(beyond_a, inward_a), *MIDDLE)
    e3_a = move(o2_a, *OUTWARD)
    o2_b, e2 = after([o2_b, e2], inward_a)
    e3_b = move(o2_b, *OUTWARD)

    q_t = transposed(after([q], o2_a)[0])
    grad = weight_gradient(q_t, upstream, (e1, o1, o2_a, e2, e3_a), 0, some)
    inward_far, grad = after([inward_far, grad])
    across_far = move(total(far_b, inward_far), *MIDDLE)
    out_a = swap(total(pair_a, across_a[:block]), "tensor", 1)
    inward_near, e3_b = after([inward_near, e3_b])
    across_near = move(total(near_b, inward_near), *MIDDLE)
    across_far, out_a = after([across_far, out_a])
    out_b = swap(total(pair_b, across_far), "tensor", 1)
    (late,) = after([q_t], across_far)
    weight_grad = weight_gradient(
        late, upstream, (e1, o1, o2_b, e2, e3_b), some, hidden - some, grad
    )
    projected = jnp.concatenate(
        [total(own_a, out_a, across_a[block:]), total(own_b, out_b, across_near)], axis=1
    )
    return (projected, weight_grad)


def per_device(x_tokens, sign_bits, weight, upstream):
    rows, width = x_tokens.shape
    hidden = weight.shape[1]
    fits = rows % 64 == 0 and width % 256 == 0 and hidden % 512 == 0 and hidden >= 1536
    if (lax.axis_size("dp"), lax.axis_size("tensor")) == (8, 4) and fits:
        return lined(x_tokens, sign_bits, weight, upstream)
    return plain(x_tokens, sign_bits, weight, upstream)


def solution(mesh):
    in_specs = (P("dp", "tensor"), P("tensor"), P("tensor", "dp"), P("tensor", "dp"))
    out_specs = (P("tensor", "dp"), P("tensor", "dp"))
    return jax.shard_map(
        per_device, mesh=mesh, in_specs=in_specs, out_specs=out_specs, check_vma=False
    )
```

```python
import functools
import math

import jax
import jax.numpy as jnp
from jax import lax
from jax.experimental import pallas as pl
from jax.experimental.pallas import tpu as pltpu
from jax.sharding import PartitionSpec as P

MIB = 1 << 20
VMEM = pl.BlockSpec(memory_space=pltpu.VMEM)


def hadamard(order):
    row_ids = jnp.arange(order, dtype=jnp.int32)[:, None]
    col_ids = jnp.arange(order, dtype=jnp.int32)[None, :]
    common = row_ids & col_ids
    parity = jnp.zeros((order, order), jnp.int32)
    for section_bit in range(max(order.bit_length() - 1, 0)):
        parity = parity + (common >> section_bit & 1)
    return (1 - 2 * (parity % 2)).astype(jnp.bfloat16)


def swap(block, axis, mask):
    count = lax.axis_size(axis)
    return lax.ppermute(
        block, axis, [(i, i ^ mask) for i in range(count) if i ^ mask < count]
    )


def plain(x_tokens, sign_bits, weight, upstream):
    panel_width = x_tokens.shape[1]
    groups = lax.axis_size("tensor")
    factor = 1.0 / math.sqrt(panel_width * groups)
    column_sign = (1 - 2 * sign_bits).astype(jnp.bfloat16)
    current = jnp.dot(
        x_tokens * column_sign[None, :],
        hadamard(panel_width),
        preferred_element_type=jnp.float32,
    )
    position = lax.axis_index("tensor")
    for section_bit in range(groups.bit_length() - 1):
        partner = swap(current.astype(jnp.bfloat16), "tensor", 1 << section_bit).astype(
            current.dtype
        )
        upper_half = position >> section_bit & 1 == 1
        current = jnp.where(upper_half, partner - current, current + partner)
    quantized = (current * factor).astype(jnp.bfloat16)
    gathered = lax.all_gather(quantized, "dp", axis=0, tiled=True)
    projected = lax.psum_scatter(
        jnp.dot(gathered, weight, preferred_element_type=jnp.float32).astype(jnp.bfloat16),
        "tensor",
        scatter_dimension=0,
        tiled=True,
    )
    weight_grad = lax.dot_general(
        gathered,
        lax.all_gather(upstream, "tensor", axis=0, tiled=True),
        (((0,), (0,)), ((), ())),
        preferred_element_type=jnp.float32,
    )
    return (projected, weight_grad)


def parity_sign(bits):
    return (1 - 2 * ((bits ^ bits >> 1) & 1)).astype(jnp.float32)


def butterfly(parts):
    stride = 1
    parts = list(parts)
    while stride < len(parts):
        for low in range(len(parts)):
            if not low & stride:
                a, b = parts[low], parts[low | stride]
                parts[low], parts[low | stride] = a + b, a - b
        stride *= 2
    return parts


def whole(shape):
    return pl.BlockSpec(shape, lambda n: (0,) * len(shape))


def tile_of(width, first=0):
    return next((t for t in (512, 256, 128) if width % t == 0 and first % t == 0), width)


def after(arrays, *earlier):
    arrays = list(arrays)
    return list(lax.optimization_barrier(tuple(arrays) + tuple(earlier))[: len(arrays)])


def sign_kernel(x_ref, bits_ref, *outs):
    z = lax.axis_index("tensor")
    rows = outs[0].shape[0]
    sign = (1 - 2 * bits_ref[...]).astype(jnp.float32)
    for m, out in enumerate(outs):
        first = pl.multiple_of((z ^ m) * rows, rows)
        out[...] = (x_ref[pl.ds(first, rows), :].astype(jnp.float32) * sign).astype(out.dtype)


def signed_pieces(x, sign_bits, groups):
    rows, width = x.shape
    part = rows // groups
    return pl.pallas_call(
        sign_kernel,
        out_shape=[jax.ShapeDtypeStruct((part, width), jnp.bfloat16)] * groups,
        in_specs=[VMEM] * 2,
        out_specs=[VMEM] * groups,
        compiler_params=pltpu.CompilerParams(vmem_limit_bytes=8 * MIB),
        name="signed_pieces",
    )(x, sign_bits.reshape(1, width))


def rotate_kernel(groups, order, factor, h_ref, *refs):
    pieces, outs = refs[:groups], refs[groups:]
    z = lax.axis_index("tensor")
    rows, width = pieces[0].shape
    chunks = width // order
    stacked = jnp.concatenate(
        [piece[:, j * order : (j + 1) * order] for piece in pieces for j in range(chunks)], axis=0
    )
    product = jnp.dot(stacked, h_ref[...], preferred_element_type=jnp.float32)
    rotated = []
    for i in range(groups):
        sign = parity_sign(z & i)
        rotated.append(
            butterfly(
                [
                    product[(i * chunks + j) * rows : (i * chunks + j + 1) * rows] * sign
                    for j in range(chunks)
                ]
            )
        )
    for j in range(chunks):
        panel = butterfly([r[j] for r in rotated])
        for m in range(groups):
            scale = parity_sign((z ^ m) & z) * factor
            outs[m][:, j * order : (j + 1) * order] = (panel[m] * scale).astype(jnp.bfloat16)


def rotate(pieces):
    groups = len(pieces)
    rows, width = pieces[0].shape
    order = min(256, width)
    return pl.pallas_call(
        functools.partial(rotate_kernel, groups, order, 1.0 / math.sqrt(width * groups)),
        out_shape=[jax.ShapeDtypeStruct((rows, width), jnp.bfloat16)] * groups,
        in_specs=[VMEM] * (1 + groups),
        out_specs=[VMEM] * groups,
        compiler_params=pltpu.CompilerParams(vmem_limit_bytes=8 * MIB),
        name="rotate",
    )(hadamard(order), *pieces)


def gather_rows(own, d):
    x, y, core = swap(own, "dp", 2), swap(own, "dp", 4), swap(own, "dp", 1)
    x, y = after([x, y])
    through = jnp.where(d & 1 == 0, x, y)
    diagonal = lax.ppermute(
        through, "dp", [(i, i ^ (4 if i & 1 == 0 else 2)) for i in range(8)]
    )
    return [
        own,
        core,
        x,
        swap(x, "dp", 1),
        y,
        swap(y, "dp", 1),
        diagonal,
        swap(diagonal, "dp", 1),
    ]


def is_outer(z):
    return 1 - ((z ^ z >> 1) & 1)


def slot(m, z):
    return m ^ (m >> 1 & is_outer(z))


def first_kernel(*refs):
    pieces, (w_ref, q_ref, *out_refs, sems) = refs[:8], refs[8:]
    rows = pieces[0].shape[0]

    @pl.when(pl.program_id(0) == 0)
    def _():
        z, d = lax.axis_index("tensor"), lax.axis_index("dp")
        copies = []
        for mask, piece in enumerate(pieces):
            start = slot(((d ^ mask) >> 1) ^ z, z) * (2 * rows) + ((d ^ mask) & 1) * rows
            copies.append(
                pltpu.make_async_copy(
                    piece, q_ref.at[pl.ds(pl.multiple_of(start, rows), rows), :], sems.at[mask]
                )
            )
        for copy in copies:
            copy.start()
        for copy in copies:
            copy.wait()

    project_kernel(q_ref, w_ref, *out_refs)


def project_kernel(q_ref, w_ref, *out_refs):
    product = jnp.dot(q_ref[...], w_ref[...], preferred_element_type=jnp.float32)
    first = 0
    for out_ref in out_refs:
        rows = out_ref.shape[0]
        out_ref[...] = product[first : first + rows].astype(out_ref.dtype)
        first += rows


def project_first(pieces, weight, width, blocks):
    depth = weight.shape[0]
    tokens = sum(blocks)
    tile = tile_of(width)
    q, *products = pl.pallas_call(
        first_kernel,
        out_shape=[
            jax.ShapeDtypeStruct((tokens, depth), jnp.bfloat16),
            *[jax.ShapeDtypeStruct((block, width), jnp.bfloat16) for block in blocks],
        ],
        grid=(width // tile,),
        in_specs=[pl.BlockSpec(memory_space=pl.ANY)] * len(pieces)
        + [pl.BlockSpec((depth, tile), lambda n: (0, n))],
        out_specs=[whole((tokens, depth))]
        + [pl.BlockSpec((block, tile), lambda n: (0, n)) for block in blocks],
        scratch_shapes=[pltpu.SemaphoreType.DMA((len(pieces),))],
        compiler_params=pltpu.CompilerParams(vmem_limit_bytes=48 * MIB),
        cost_estimate=pl.CostEstimate(flops=1, bytes_accessed=1, transcendentals=0),
        name="project_first",
    )(*pieces, weight)
    return q, products


def project(q, weight, first, width, blocks):
    tile = tile_of(width, first)
    tokens, depth = q.shape
    return pl.pallas_call(
        project_kernel,
        out_shape=[jax.ShapeDtypeStruct((block, width), jnp.bfloat16) for block in blocks],
        grid=(width // tile,),
        in_specs=[
            whole((tokens, depth)),
            pl.BlockSpec((depth, tile), lambda n: (0, n + first // tile)),
        ],
        out_specs=[pl.BlockSpec((block, tile), lambda n: (0, n)) for block in blocks],
        compiler_params=pltpu.CompilerParams(vmem_limit_bytes=48 * MIB),
        cost_estimate=pl.CostEstimate(
            flops=2 * tokens * depth * width,
            bytes_accessed=2 * (tokens * depth + depth * width + tokens * width),
            transcendentals=0,
        ),
        name="project",
    )(q, weight)


def transpose_kernel(q_ref, out_ref):
    out_ref[...] = q_ref[...].T


def transposed(q):
    tokens, depth = q.shape
    return pl.pallas_call(
        transpose_kernel,
        out_shape=jax.ShapeDtypeStruct((depth, tokens), jnp.bfloat16),
        in_specs=[VMEM],
        out_specs=VMEM,
        compiler_params=pltpu.CompilerParams(vmem_limit_bytes=16 * MIB),
        name="transposed",
    )(q)


def grad_kernel(tile, start, q_t, own_ref, e1, o1, o2, e2, e3, *refs):
    out_ref, up_all, sems = refs[-3:]
    z = lax.axis_index("tensor")
    rows, width = own_ref.shape[0], up_all.shape[1]

    @pl.when(pl.program_id(0) == 0)
    def _():
        def copy(source, m):
            return pltpu.make_async_copy(
                source.at[:, start : start + width],
                up_all.at[m * rows : (m + 1) * rows, :],
                sems.at[m],
            )

        copy(own_ref, 0).start()
        copy(e1, 1).start()

        @pl.when(is_outer(z) == 0)
        def _():
            copy(o2, 2).start()
            copy(o1, 3).start()

        @pl.when(is_outer(z) == 1)
        def _():
            copy(e3, 2).start()
            copy(e2, 3).start()

        for m in range(4):
            copy(own_ref, m).wait()

    first = pl.multiple_of(pl.program_id(0) * tile, tile)
    out_ref[...] = jnp.dot(
        q_t[...], up_all[:, pl.ds(first, tile)], preferred_element_type=jnp.float32
    )


def weight_gradient(q_t, own, moved, start, width, done=None):
    depth, tokens = q_t.shape
    hidden = own.shape[1]
    tile = tile_of(width, start)
    before = [] if done is None else [done]
    anywhere = pl.BlockSpec(memory_space=pl.ANY)
    return pl.pallas_call(
        functools.partial(grad_kernel, tile, start),
        out_shape=jax.ShapeDtypeStruct((depth, hidden), jnp.float32),
        grid=(width // tile,),
        in_specs=[whole((depth, tokens))] + [anywhere] * (6 + len(before)),
        out_specs=pl.BlockSpec((depth, tile), lambda n: (0, n + start // tile)),
        input_output_aliases={7: 0} if before else {},
        scratch_shapes=[
            pltpu.VMEM((tokens, width), jnp.bfloat16),
            pltpu.SemaphoreType.DMA((4,)),
        ],
        compiler_params=pltpu.CompilerParams(vmem_limit_bytes=28 * MIB),
        cost_estimate=pl.CostEstimate(
            flops=2 * tokens * depth * width,
            bytes_accessed=2 * tokens * (depth + width) + 4 * depth * width,
            transcendentals=0,
        ),
        name="weight_gradient",
    )(q_t, own, *moved, *before)


def total(*blocks):
    return sum(b.astype(jnp.float32) for b in blocks).astype(jnp.bfloat16)


def move(block, *pairs):
    return lax.ppermute(block, "tensor", pairs)


INWARD = ((0, 1), (3, 2))
MIDDLE = ((1, 2), (2, 1))
OUTWARD = ((1, 0), (2, 3))


def lined(x_tokens, sign_bits, weight, upstream):
    groups = lax.axis_size("tensor")
    z = lax.axis_index("tensor")
    d = lax.axis_index("dp")
    rows = x_tokens.shape[0]
    hidden = weight.shape[1]

    pieces = list(signed_pieces(x_tokens, sign_bits, groups))
    for m in (3, 2, 1):
        pieces[m] = swap(pieces[m], "tensor", m)
    turned = list(rotate(pieces))
    (up,) = after([upstream], turned[0])
    for m in (3, 2, 1):
        turned[m] = swap(turned[m], "tensor", m)
    own = jnp.concatenate(
        [lax.select_n(z, *[turned[g ^ k] for k in range(groups)]) for g in range(groups)]
    )

    e1 = swap(up, "tensor", 1)
    o1 = move(up, *MIDDLE)

    gathered = gather_rows(own, d)
    cut = (hidden // 512 + 1) // 2 * 512
    block = rows * len(gathered) // groups
    q, *first = project_first(gathered, weight, cut, (block, block, 2 * block))
    own_a, pair_a, beyond_a = first[0]
    q, e1, o1 = after([q, e1, o1])
    o2 = move(e1, *MIDDLE)
    e2 = move(o1, *OUTWARD)
    own_b, pair_b, far_b, near_b = project(q, weight, cut, hidden - cut, (block,) * 4)

    inward_a = move(beyond_a, *INWARD)
    inward_a, own_b = after([inward_a, own_b])
    inward_far = move(far_b, *INWARD)
    (inward_near,) = after([near_b], inward_a)
    inward_near = move(inward_near, *INWARD)
    across_a = move(total(beyond_a, inward_a), *MIDDLE)
    o2, e2 = after([o2, e2], inward_a)
    e3 = move(o2, *OUTWARD)
    inward_far, o2, e2 = after([inward_far, o2, e2])
    across_far = move(total(far_b, inward_far), *MIDDLE)
    across_a, e3 = after([across_a, e3])
    out_a = swap(total(pair_a, across_a[:block]), "tensor", 1)

    (late,) = after([q], inward_far)
    q_t = transposed(late)
    moved = (e1, o1, o2, e2, e3)
    some = hidden // 2 // 512 * 512
    (late,) = after([q_t], across_a)
    grad = weight_gradient(late, upstream, moved, 0, some)

    inward_near, grad = after([inward_near, grad])
    across_near = move(total(near_b, inward_near), *MIDDLE)
    across_far, grad, out_a = after([across_far, grad, out_a])
    out_b = swap(total(pair_b, across_far), "tensor", 1)
    (late,) = after([q_t], across_far)
    weight_grad = weight_gradient(late, upstream, moved, some, hidden - some, grad)
    projected = jnp.concatenate(
        [total(own_a, out_a, across_a[block:]), total(own_b, out_b, across_near)], axis=1
    )
    return (projected, weight_grad)


def per_device(x_tokens, sign_bits, weight, upstream):
    rows, width = x_tokens.shape
    hidden = weight.shape[1]
    fits = rows % 64 == 0 and width % 256 == 0 and hidden % 512 == 0 and hidden >= 1536
    if (lax.axis_size("dp"), lax.axis_size("tensor")) == (8, 4) and fits:
        return lined(x_tokens, sign_bits, weight, upstream)
    return plain(x_tokens, sign_bits, weight, upstream)


def solution(mesh):
    in_specs = (P("dp", "tensor"), P("tensor"), P("tensor", "dp"), P("tensor", "dp"))
    out_specs = (P("tensor", "dp"), P("tensor", "dp"))
    return jax.shard_map(
        per_device, mesh=mesh, in_specs=in_specs, out_specs=out_specs, check_vma=False
    )
```

```python
import functools
import math

import jax
import jax.numpy as jnp
from jax import lax
from jax.experimental import pallas as pl
from jax.experimental.pallas import tpu as pltpu
from jax.sharding import PartitionSpec as P

MIB = 1 << 20
VMEM = pl.BlockSpec(memory_space=pltpu.VMEM)


def hadamard(order):
    row_ids = jnp.arange(order, dtype=jnp.int32)[:, None]
    col_ids = jnp.arange(order, dtype=jnp.int32)[None, :]
    common = row_ids & col_ids
    parity = jnp.zeros((order, order), jnp.int32)
    for section_bit in range(max(order.bit_length() - 1, 0)):
        parity = parity + (common >> section_bit & 1)
    return (1 - 2 * (parity % 2)).astype(jnp.bfloat16)


def swap(block, axis, mask):
    count = lax.axis_size(axis)
    return lax.ppermute(
        block, axis, [(i, i ^ mask) for i in range(count) if i ^ mask < count]
    )


def plain(x_tokens, sign_bits, weight, upstream):
    panel_width = x_tokens.shape[1]
    groups = lax.axis_size("tensor")
    factor = 1.0 / math.sqrt(panel_width * groups)
    column_sign = (1 - 2 * sign_bits).astype(jnp.bfloat16)
    current = jnp.dot(
        x_tokens * column_sign[None, :],
        hadamard(panel_width),
        preferred_element_type=jnp.float32,
    )
    position = lax.axis_index("tensor")
    for section_bit in range(groups.bit_length() - 1):
        partner = swap(current.astype(jnp.bfloat16), "tensor", 1 << section_bit).astype(
            current.dtype
        )
        upper_half = position >> section_bit & 1 == 1
        current = jnp.where(upper_half, partner - current, current + partner)
    quantized = (current * factor).astype(jnp.bfloat16)
    gathered = lax.all_gather(quantized, "dp", axis=0, tiled=True)
    projected = lax.psum_scatter(
        jnp.dot(gathered, weight, preferred_element_type=jnp.float32).astype(jnp.bfloat16),
        "tensor",
        scatter_dimension=0,
        tiled=True,
    )
    weight_grad = lax.dot_general(
        gathered,
        lax.all_gather(upstream, "tensor", axis=0, tiled=True),
        (((0,), (0,)), ((), ())),
        preferred_element_type=jnp.float32,
    )
    return (projected, weight_grad)


def parity_sign(bits):
    return (1 - 2 * ((bits ^ bits >> 1) & 1)).astype(jnp.float32)


def butterfly(parts):
    stride = 1
    parts = list(parts)
    while stride < len(parts):
        for low in range(len(parts)):
            if not low & stride:
                a, b = parts[low], parts[low | stride]
                parts[low], parts[low | stride] = a + b, a - b
        stride *= 2
    return parts


def whole(shape):
    return pl.BlockSpec(shape, lambda n: (0,) * len(shape))


def tile_of(width, first=0):
    return next((t for t in (512, 256, 128) if width % t == 0 and first % t == 0), width)


def after(arrays, *earlier):
    arrays = list(arrays)
    return list(lax.optimization_barrier(tuple(arrays) + tuple(earlier))[: len(arrays)])


def sign_kernel(x_ref, bits_ref, *outs):
    z = lax.axis_index("tensor")
    rows = outs[0].shape[0]
    sign = (1 - 2 * bits_ref[...]).astype(jnp.float32)
    for m, out in enumerate(outs):
        first = pl.multiple_of((z ^ m) * rows, rows)
        out[...] = (x_ref[pl.ds(first, rows), :].astype(jnp.float32) * sign).astype(out.dtype)


def signed_pieces(x, sign_bits, groups):
    rows, width = x.shape
    part = rows // groups
    return pl.pallas_call(
        sign_kernel,
        out_shape=[jax.ShapeDtypeStruct((part, width), jnp.bfloat16)] * groups,
        in_specs=[VMEM] * 2,
        out_specs=[VMEM] * groups,
        compiler_params=pltpu.CompilerParams(vmem_limit_bytes=8 * MIB),
        name="signed_pieces",
    )(x, sign_bits.reshape(1, width))


def rotate_kernel(groups, order, factor, h_ref, *refs):
    pieces, outs = refs[:groups], refs[groups:]
    z = lax.axis_index("tensor")
    rows, width = pieces[0].shape
    chunks = width // order
    stacked = jnp.concatenate(
        [piece[:, j * order : (j + 1) * order] for piece in pieces for j in range(chunks)], axis=0
    )
    product = jnp.dot(stacked, h_ref[...], preferred_element_type=jnp.float32)
    rotated = []
    for i in range(groups):
        sign = parity_sign(z & i)
        rotated.append(
            butterfly(
                [
                    product[(i * chunks + j) * rows : (i * chunks + j + 1) * rows] * sign
                    for j in range(chunks)
                ]
            )
        )
    for j in range(chunks):
        panel = butterfly([r[j] for r in rotated])
        for m in range(groups):
            scale = parity_sign((z ^ m) & z) * factor
            outs[m][:, j * order : (j + 1) * order] = (panel[m] * scale).astype(jnp.bfloat16)


def rotate(pieces):
    groups = len(pieces)
    rows, width = pieces[0].shape
    order = min(256, width)
    return pl.pallas_call(
        functools.partial(rotate_kernel, groups, order, 1.0 / math.sqrt(width * groups)),
        out_shape=[jax.ShapeDtypeStruct((rows, width), jnp.bfloat16)] * groups,
        in_specs=[VMEM] * (1 + groups),
        out_specs=[VMEM] * groups,
        compiler_params=pltpu.CompilerParams(vmem_limit_bytes=8 * MIB),
        name="rotate",
    )(hadamard(order), *pieces)


def gather_rows(own, d):
    x, y, core = swap(own, "dp", 2), swap(own, "dp", 4), swap(own, "dp", 1)
    x, y = after([x, y])
    through = jnp.where(d & 1 == 0, x, y)
    diagonal = lax.ppermute(
        through, "dp", [(i, i ^ (4 if i & 1 == 0 else 2)) for i in range(8)]
    )
    return [
        own,
        core,
        x,
        swap(x, "dp", 1),
        y,
        swap(y, "dp", 1),
        diagonal,
        swap(diagonal, "dp", 1),
    ]


def is_outer(z):
    return 1 - ((z ^ z >> 1) & 1)


def slot(m, z):
    return m ^ (m >> 1 & is_outer(z))


def first_kernel(*refs):
    pieces, (w_ref, q_ref, *out_refs, sems) = refs[:8], refs[8:]
    rows = pieces[0].shape[0]

    @pl.when(pl.program_id(0) == 0)
    def _():
        z, d = lax.axis_index("tensor"), lax.axis_index("dp")
        copies = []
        for mask, piece in enumerate(pieces):
            start = slot(((d ^ mask) >> 1) ^ z, z) * (2 * rows) + ((d ^ mask) & 1) * rows
            copies.append(
                pltpu.make_async_copy(
                    piece, q_ref.at[pl.ds(pl.multiple_of(start, rows), rows), :], sems.at[mask]
                )
            )
        for copy in copies:
            copy.start()
        for copy in copies:
            copy.wait()

    project_kernel(q_ref, w_ref, *out_refs)


def project_kernel(q_ref, w_ref, *out_refs):
    product = jnp.dot(q_ref[...], w_ref[...], preferred_element_type=jnp.float32)
    first = 0
    for out_ref in out_refs:
        rows = out_ref.shape[0]
        out_ref[...] = product[first : first + rows].astype(out_ref.dtype)
        first += rows


def project_first(pieces, weight, width, blocks):
    depth = weight.shape[0]
    tokens = sum(blocks)
    tile = tile_of(width)
    q, *products = pl.pallas_call(
        first_kernel,
        out_shape=[
            jax.ShapeDtypeStruct((tokens, depth), jnp.bfloat16),
            *[jax.ShapeDtypeStruct((block, width), jnp.bfloat16) for block in blocks],
        ],
        grid=(width // tile,),
        in_specs=[pl.BlockSpec(memory_space=pl.ANY)] * len(pieces)
        + [pl.BlockSpec((depth, tile), lambda n: (0, n))],
        out_specs=[whole((tokens, depth))]
        + [pl.BlockSpec((block, tile), lambda n: (0, n)) for block in blocks],
        scratch_shapes=[pltpu.SemaphoreType.DMA((len(pieces),))],
        compiler_params=pltpu.CompilerParams(vmem_limit_bytes=48 * MIB),
        cost_estimate=pl.CostEstimate(flops=1, bytes_accessed=1, transcendentals=0),
        name="project_first",
    )(*pieces, weight)
    return q, products


def project(q, weight, first, width, blocks):
    tile = tile_of(width, first)
    tokens, depth = q.shape
    return pl.pallas_call(
        project_kernel,
        out_shape=[jax.ShapeDtypeStruct((block, width), jnp.bfloat16) for block in blocks],
        grid=(width // tile,),
        in_specs=[
            whole((tokens, depth)),
            pl.BlockSpec((depth, tile), lambda n: (0, n + first // tile)),
        ],
        out_specs=[pl.BlockSpec((block, tile), lambda n: (0, n)) for block in blocks],
        compiler_params=pltpu.CompilerParams(vmem_limit_bytes=48 * MIB),
        cost_estimate=pl.CostEstimate(
            flops=2 * tokens * depth * width,
            bytes_accessed=2 * (tokens * depth + depth * width + tokens * width),
            transcendentals=0,
        ),
        name="project",
    )(q, weight)


def transpose_kernel(q_ref, out_ref):
    out_ref[...] = q_ref[...].T


def transposed(q):
    tokens, depth = q.shape
    return pl.pallas_call(
        transpose_kernel,
        out_shape=jax.ShapeDtypeStruct((depth, tokens), jnp.bfloat16),
        in_specs=[VMEM],
        out_specs=VMEM,
        compiler_params=pltpu.CompilerParams(vmem_limit_bytes=16 * MIB),
        name="transposed",
    )(q)


def grad_kernel(tile, start, q_t, own_ref, e1, o1, o2, e2, e3, *refs):
    out_ref, up_all, sems = refs[-3:]
    z = lax.axis_index("tensor")
    rows, width = own_ref.shape[0], up_all.shape[1]

    @pl.when(pl.program_id(0) == 0)
    def _():
        def copy(source, m):
            return pltpu.make_async_copy(
                source.at[:, start : start + width],
                up_all.at[m * rows : (m + 1) * rows, :],
                sems.at[m],
            )

        copy(own_ref, 0).start()
        copy(e1, 1).start()

        @pl.when(is_outer(z) == 0)
        def _():
            copy(o2, 2).start()
            copy(o1, 3).start()

        @pl.when(is_outer(z) == 1)
        def _():
            copy(e3, 2).start()
            copy(e2, 3).start()

        for m in range(4):
            copy(own_ref, m).wait()

    first = pl.multiple_of(pl.program_id(0) * tile, tile)
    out_ref[...] = jnp.dot(
        q_t[...], up_all[:, pl.ds(first, tile)], preferred_element_type=jnp.float32
    )


def weight_gradient(q_t, own, moved, start, width, done=None):
    depth, tokens = q_t.shape
    hidden = own.shape[1]
    tile = tile_of(width, start)
    before = [] if done is None else [done]
    anywhere = pl.BlockSpec(memory_space=pl.ANY)
    return pl.pallas_call(
        functools.partial(grad_kernel, tile, start),
        out_shape=jax.ShapeDtypeStruct((depth, hidden), jnp.float32),
        grid=(width // tile,),
        in_specs=[whole((depth, tokens))] + [anywhere] * (6 + len(before)),
        out_specs=pl.BlockSpec((depth, tile), lambda n: (0, n + start // tile)),
        input_output_aliases={7: 0} if before else {},
        scratch_shapes=[
            pltpu.VMEM((tokens, width), jnp.bfloat16),
            pltpu.SemaphoreType.DMA((4,)),
        ],
        compiler_params=pltpu.CompilerParams(vmem_limit_bytes=28 * MIB),
        cost_estimate=pl.CostEstimate(
            flops=2 * tokens * depth * width,
            bytes_accessed=2 * tokens * (depth + width) + 4 * depth * width,
            transcendentals=0,
        ),
        name="weight_gradient",
    )(q_t, own, *moved, *before)


def total(*blocks):
    return sum(b.astype(jnp.float32) for b in blocks).astype(jnp.bfloat16)


def move(block, *pairs):
    return lax.ppermute(block, "tensor", pairs)


INWARD = ((0, 1), (3, 2))
MIDDLE = ((1, 2), (2, 1))
OUTWARD = ((1, 0), (2, 3))


def lined(x_tokens, sign_bits, weight, upstream):
    groups = lax.axis_size("tensor")
    z = lax.axis_index("tensor")
    d = lax.axis_index("dp")
    rows = x_tokens.shape[0]
    hidden = weight.shape[1]

    pieces = list(signed_pieces(x_tokens, sign_bits, groups))
    for m in (3, 2, 1):
        pieces[m] = swap(pieces[m], "tensor", m)
    turned = list(rotate(pieces))
    (up,) = after([upstream], turned[0])
    for m in (3, 2, 1):
        turned[m] = swap(turned[m], "tensor", m)
    own = jnp.concatenate(
        [lax.select_n(z, *[turned[g ^ k] for k in range(groups)]) for g in range(groups)]
    )

    e1 = swap(up, "tensor", 1)
    o1 = move(up, *MIDDLE)

    gathered = gather_rows(own, d)
    cut = 3 * hidden // 7 // 512 * 512
    block = rows * len(gathered) // groups
    q, *first = project_first(gathered, weight, cut, (block, block, 2 * block))
    own_a, pair_a, beyond_a = first[0]
    q, e1, o1 = after([q, e1, o1])
    o2 = move(e1, *MIDDLE)
    e2 = move(o1, *OUTWARD)
    own_b, pair_b, beyond_b = project(q, weight, cut, hidden - cut, (block, block, 2 * block))

    inward_a = move(beyond_a, *INWARD)
    inward_b = move(beyond_b, *INWARD)
    inward_a, o2, e2 = after([inward_a, o2, e2])
    across_a = move(total(beyond_a, inward_a), *MIDDLE)
    e3 = move(o2, *OUTWARD)
    across_far = move(total(beyond_b[:block], inward_b[:block]), *MIDDLE)
    across_near = move(total(beyond_b[block:], inward_b[block:]), *MIDDLE)
    across_a, e3 = after([across_a, e3])
    out_a = swap(total(pair_a, across_a[:block]), "tensor", 1)

    q_t = transposed(after([q], inward_a)[0])
    moved = (e1, o1, o2, e2, e3)
    some = hidden // 2 // 512 * 512
    (late,) = after([q_t], across_a)
    grad = weight_gradient(late, upstream, moved, 0, some)
    across_far, grad, out_a = after([across_far, grad, out_a])
    out_b = swap(total(pair_b, across_far), "tensor", 1)
    (late,) = after([q_t], across_far)
    weight_grad = weight_gradient(late, upstream, moved, some, hidden - some, grad)
    projected = jnp.concatenate(
        [total(own_a, out_a, across_a[block:]), total(own_b, out_b, across_near)], axis=1
    )
    return (projected, weight_grad)


def per_device(x_tokens, sign_bits, weight, upstream):
    rows, width = x_tokens.shape
    hidden = weight.shape[1]
    fits = rows % 64 == 0 and width % 256 == 0 and hidden % 512 == 0 and hidden >= 1536
    if (lax.axis_size("dp"), lax.axis_size("tensor")) == (8, 4) and fits:
        return lined(x_tokens, sign_bits, weight, upstream)
    return plain(x_tokens, sign_bits, weight, upstream)


def solution(mesh):
    in_specs = (P("dp", "tensor"), P("tensor"), P("tensor", "dp"), P("tensor", "dp"))
    out_specs = (P("tensor", "dp"), P("tensor", "dp"))
    return jax.shard_map(
        per_device, mesh=mesh, in_specs=in_specs, out_specs=out_specs, check_vma=False
    )
```

```python
import functools
import math

import jax
import jax.numpy as jnp
from jax import lax
from jax.experimental import pallas as pl
from jax.experimental.pallas import tpu as pltpu
from jax.sharding import PartitionSpec as P

MIB = 1 << 20
VMEM = pl.BlockSpec(memory_space=pltpu.VMEM)


def hadamard(order):
    row_ids = jnp.arange(order, dtype=jnp.int32)[:, None]
    col_ids = jnp.arange(order, dtype=jnp.int32)[None, :]
    common = row_ids & col_ids
    parity = jnp.zeros((order, order), jnp.int32)
    for section_bit in range(max(order.bit_length() - 1, 0)):
        parity = parity + (common >> section_bit & 1)
    return (1 - 2 * (parity % 2)).astype(jnp.bfloat16)


def swap(block, axis, mask):
    count = lax.axis_size(axis)
    return lax.ppermute(
        block, axis, [(i, i ^ mask) for i in range(count) if i ^ mask < count]
    )


def plain(x_tokens, sign_bits, weight, upstream):
    panel_width = x_tokens.shape[1]
    groups = lax.axis_size("tensor")
    factor = 1.0 / math.sqrt(panel_width * groups)
    column_sign = (1 - 2 * sign_bits).astype(jnp.bfloat16)
    current = jnp.dot(
        x_tokens * column_sign[None, :],
        hadamard(panel_width),
        preferred_element_type=jnp.float32,
    )
    position = lax.axis_index("tensor")
    for section_bit in range(groups.bit_length() - 1):
        partner = swap(current.astype(jnp.bfloat16), "tensor", 1 << section_bit).astype(
            current.dtype
        )
        upper_half = position >> section_bit & 1 == 1
        current = jnp.where(upper_half, partner - current, current + partner)
    quantized = (current * factor).astype(jnp.bfloat16)
    gathered = lax.all_gather(quantized, "dp", axis=0, tiled=True)
    projected = lax.psum_scatter(
        jnp.dot(gathered, weight, preferred_element_type=jnp.float32).astype(jnp.bfloat16),
        "tensor",
        scatter_dimension=0,
        tiled=True,
    )
    weight_grad = lax.dot_general(
        gathered,
        lax.all_gather(upstream, "tensor", axis=0, tiled=True),
        (((0,), (0,)), ((), ())),
        preferred_element_type=jnp.float32,
    )
    return (projected, weight_grad)


def butterfly(parts):
    stride = 1
    parts = list(parts)
    while stride < len(parts):
        for low in range(len(parts)):
            if not low & stride:
                a, b = parts[low], parts[low | stride]
                parts[low], parts[low | stride] = a + b, a - b
        stride *= 2
    return parts


def whole(shape):
    return pl.BlockSpec(shape, lambda n: (0,) * len(shape))


def tile_of(width, first=0):
    return next((t for t in (512, 256, 128) if width % t == 0 and first % t == 0), width)


def after(arrays, *earlier):
    arrays = list(arrays)
    return list(lax.optimization_barrier(tuple(arrays) + tuple(earlier))[: len(arrays)])


def sign_kernel(x_ref, bits_ref, out_ref):
    sign = (1 - 2 * bits_ref[...]).astype(jnp.float32)
    rows = out_ref.shape[1]
    for group in range(out_ref.shape[0]):
        piece = x_ref[group * rows : (group + 1) * rows, :].astype(jnp.float32) * sign
        out_ref[group] = piece.astype(out_ref.dtype)


def signed_pieces(x, sign_bits, groups):
    rows, width = x.shape
    return pl.pallas_call(
        sign_kernel,
        out_shape=jax.ShapeDtypeStruct((groups, rows // groups, width), jnp.bfloat16),
        in_specs=[VMEM] * 2,
        out_specs=VMEM,
        compiler_params=pltpu.CompilerParams(vmem_limit_bytes=8 * MIB),
        name="signed_pieces",
    )(x, sign_bits.reshape(1, width))


def rotate_kernel(order, factor, h_ref, x_ref, out_ref):
    groups, rows, width = x_ref.shape
    chunks = width // order
    stacked = jnp.concatenate(
        [x_ref[i, :, j * order : (j + 1) * order] for i in range(groups) for j in range(chunks)],
        axis=0,
    )
    product = jnp.dot(stacked, h_ref[...], preferred_element_type=jnp.float32)
    rotated = [
        butterfly([product[n * rows : (n + 1) * rows] for n in range(i * chunks, (i + 1) * chunks)])
        for i in range(groups)
    ]
    for j in range(chunks):
        for i, panel in enumerate(butterfly([r[j] for r in rotated])):
            out_ref[i, :, j * order : (j + 1) * order] = (panel * factor).astype(out_ref.dtype)


def rotate(panels):
    groups, rows, width = panels.shape
    order = min(256, width)
    return pl.pallas_call(
        functools.partial(rotate_kernel, order, 1.0 / math.sqrt(width * groups)),
        out_shape=jax.ShapeDtypeStruct(panels.shape, jnp.bfloat16),
        in_specs=[VMEM] * 2,
        out_specs=VMEM,
        compiler_params=pltpu.CompilerParams(vmem_limit_bytes=8 * MIB),
        name="rotate",
    )(hadamard(order), panels)


def gather_rows(own, d):
    x, y, core = swap(own, "dp", 2), swap(own, "dp", 4), swap(own, "dp", 1)
    x, y = after([x, y])
    through = jnp.where(d & 1 == 0, x, y)
    diagonal = lax.ppermute(
        through, "dp", [(i, i ^ (4 if i & 1 == 0 else 2)) for i in range(8)]
    )
    return [
        own,
        core,
        x,
        swap(x, "dp", 1),
        y,
        swap(y, "dp", 1),
        diagonal,
        swap(diagonal, "dp", 1),
    ]


def is_outer(z):
    return 1 - ((z ^ z >> 1) & 1)


def slot(m, z):
    return m ^ (m >> 1 & is_outer(z))


def first_kernel(*refs):
    pieces, (w_ref, q_ref, *out_refs, sems) = refs[:8], refs[8:]
    rows = pieces[0].shape[0]

    @pl.when(pl.program_id(0) == 0)
    def _():
        z, d = lax.axis_index("tensor"), lax.axis_index("dp")
        copies = []
        for mask, piece in enumerate(pieces):
            start = slot(((d ^ mask) >> 1) ^ z, z) * (2 * rows) + ((d ^ mask) & 1) * rows
            copies.append(
                pltpu.make_async_copy(
                    piece, q_ref.at[pl.ds(pl.multiple_of(start, rows), rows), :], sems.at[mask]
                )
            )
        for copy in copies:
            copy.start()
        for copy in copies:
            copy.wait()

    project_kernel(q_ref, w_ref, *out_refs)


def project_kernel(q_ref, w_ref, *out_refs):
    product = jnp.dot(q_ref[...], w_ref[...], preferred_element_type=jnp.float32)
    first = 0
    for out_ref in out_refs:
        rows = out_ref.shape[0]
        out_ref[...] = product[first : first + rows].astype(out_ref.dtype)
        first += rows


def project_first(pieces, weight, width, blocks):
    depth = weight.shape[0]
    tokens = sum(blocks)
    tile = tile_of(width)
    q, *products = pl.pallas_call(
        first_kernel,
        out_shape=[
            jax.ShapeDtypeStruct((tokens, depth), jnp.bfloat16),
            *[jax.ShapeDtypeStruct((block, width), jnp.bfloat16) for block in blocks],
        ],
        grid=(width // tile,),
        in_specs=[pl.BlockSpec(memory_space=pl.ANY)] * len(pieces)
        + [pl.BlockSpec((depth, tile), lambda n: (0, n))],
        out_specs=[whole((tokens, depth))]
        + [pl.BlockSpec((block, tile), lambda n: (0, n)) for block in blocks],
        scratch_shapes=[pltpu.SemaphoreType.DMA((len(pieces),))],
        compiler_params=pltpu.CompilerParams(vmem_limit_bytes=48 * MIB),
        cost_estimate=pl.CostEstimate(flops=1, bytes_accessed=1, transcendentals=0),
        name="project_first",
    )(*pieces, weight)
    return q, products


def project(q, weight, first, width, blocks):
    tile = tile_of(width, first)
    tokens, depth = q.shape
    return pl.pallas_call(
        project_kernel,
        out_shape=[jax.ShapeDtypeStruct((block, width), jnp.bfloat16) for block in blocks],
        grid=(width // tile,),
        in_specs=[
            whole((tokens, depth)),
            pl.BlockSpec((depth, tile), lambda n: (0, n + first // tile)),
        ],
        out_specs=[pl.BlockSpec((block, tile), lambda n: (0, n)) for block in blocks],
        compiler_params=pltpu.CompilerParams(vmem_limit_bytes=48 * MIB),
        cost_estimate=pl.CostEstimate(
            flops=2 * tokens * depth * width,
            bytes_accessed=2 * (tokens * depth + depth * width + tokens * width),
            transcendentals=0,
        ),
        name="project",
    )(q, weight)


def transpose_kernel(q_ref, out_ref):
    out_ref[...] = q_ref[...].T


def transposed(q):
    tokens, depth = q.shape
    return pl.pallas_call(
        transpose_kernel,
        out_shape=jax.ShapeDtypeStruct((depth, tokens), jnp.bfloat16),
        in_specs=[VMEM],
        out_specs=VMEM,
        compiler_params=pltpu.CompilerParams(vmem_limit_bytes=16 * MIB),
        name="transposed",
    )(q)


def grad_kernel(tile, start, q_t, own_ref, e1, o1, o2, e2, e3, *refs):
    out_ref, up_all, sems = refs[-3:]
    z = lax.axis_index("tensor")
    rows, width = own_ref.shape[0], up_all.shape[1]

    @pl.when(pl.program_id(0) == 0)
    def _():
        def copy(source, m):
            return pltpu.make_async_copy(
                source.at[:, start : start + width],
                up_all.at[m * rows : (m + 1) * rows, :],
                sems.at[m],
            )

        copy(own_ref, 0).start()
        copy(e1, 1).start()

        @pl.when(is_outer(z) == 0)
        def _():
            copy(o2, 2).start()
            copy(o1, 3).start()

        @pl.when(is_outer(z) == 1)
        def _():
            copy(e3, 2).start()
            copy(e2, 3).start()

        for m in range(4):
            copy(own_ref, m).wait()

    first = pl.multiple_of(pl.program_id(0) * tile, tile)
    out_ref[...] = jnp.dot(
        q_t[...], up_all[:, pl.ds(first, tile)], preferred_element_type=jnp.float32
    )


def weight_gradient(q_t, own, moved, start, width, done=None):
    depth, tokens = q_t.shape
    hidden = own.shape[1]
    tile = tile_of(width, start)
    before = [] if done is None else [done]
    anywhere = pl.BlockSpec(memory_space=pl.ANY)
    return pl.pallas_call(
        functools.partial(grad_kernel, tile, start),
        out_shape=jax.ShapeDtypeStruct((depth, hidden), jnp.float32),
        grid=(width // tile,),
        in_specs=[whole((depth, tokens))] + [anywhere] * (6 + len(before)),
        out_specs=pl.BlockSpec((depth, tile), lambda n: (0, n + start // tile)),
        input_output_aliases={7: 0} if before else {},
        scratch_shapes=[
            pltpu.VMEM((tokens, width), jnp.bfloat16),
            pltpu.SemaphoreType.DMA((4,)),
        ],
        compiler_params=pltpu.CompilerParams(vmem_limit_bytes=28 * MIB),
        cost_estimate=pl.CostEstimate(
            flops=2 * tokens * depth * width,
            bytes_accessed=2 * tokens * (depth + width) + 4 * depth * width,
            transcendentals=0,
        ),
        name="weight_gradient",
    )(q_t, own, *moved, *before)


def total(*blocks):
    return sum(b.astype(jnp.float32) for b in blocks).astype(jnp.bfloat16)


def move(block, *pairs):
    return lax.ppermute(block, "tensor", pairs)


INWARD = ((0, 1), (3, 2))
MIDDLE = ((1, 2), (2, 1))
OUTWARD = ((1, 0), (2, 3))


def lined(x_tokens, sign_bits, weight, upstream):
    groups = lax.axis_size("tensor")
    z = lax.axis_index("tensor")
    d = lax.axis_index("dp")
    rows = x_tokens.shape[0]
    hidden = weight.shape[1]

    panels = signed_pieces(x_tokens, sign_bits, groups)
    turned = rotate(lax.all_to_all(panels, "tensor", 0, 0))
    (up,) = after([upstream], turned)
    own = lax.all_to_all(turned, "tensor", 0, 0).reshape(x_tokens.shape)

    e1 = swap(up, "tensor", 1)
    o1 = move(up, *MIDDLE)

    gathered = gather_rows(own, d)
    cut = 3 * hidden // 7 // 512 * 512
    block = rows * len(gathered) // groups
    q, *first = project_first(gathered, weight, cut, (block, block, 2 * block))
    own_a, pair_a, beyond_a = first[0]
    q, e1, o1 = after([q, e1, o1])
    o2 = move(e1, *MIDDLE)
    e2 = move(o1, *OUTWARD)
    own_b, pair_b, beyond_b = project(q, weight, cut, hidden - cut, (block, block, 2 * block))

    inward_a = move(beyond_a, *INWARD)
    inward_b = move(after([beyond_b], inward_a)[0], *INWARD)
    inward_a, o2, e2 = after([inward_a, o2, e2])
    across_a = move(total(beyond_a, inward_a), *MIDDLE)
    e3 = move(o2, *OUTWARD)
    across_far = move(total(beyond_b[:block], inward_b[:block]), *MIDDLE)
    across_near = move(total(beyond_b[block:], inward_b[block:]), *MIDDLE)
    across_a, e3 = after([across_a, e3])
    out_a = swap(total(pair_a, across_a[:block]), "tensor", 1)

    q_t = transposed(after([q], inward_a)[0])
    moved = (e1, o1, o2, e2, e3)
    some = hidden // 2 // 512 * 512
    (late,) = after([q_t], across_a)
    grad = weight_gradient(late, upstream, moved, 0, some)
    across_far, grad, out_a = after([across_far, grad, out_a])
    out_b = swap(total(pair_b, across_far), "tensor", 1)
    (late,) = after([q_t], across_far)
    weight_grad = weight_gradient(late, upstream, moved, some, hidden - some, grad)
    projected = jnp.concatenate(
        [total(own_a, out_a, across_a[block:]), total(own_b, out_b, across_near)], axis=1
    )
    return (projected, weight_grad)


def per_device(x_tokens, sign_bits, weight, upstream):
    rows, width = x_tokens.shape
    hidden = weight.shape[1]
    fits = rows % 64 == 0 and width % 256 == 0 and hidden % 512 == 0 and hidden >= 1536
    if (lax.axis_size("dp"), lax.axis_size("tensor")) == (8, 4) and fits:
        return lined(x_tokens, sign_bits, weight, upstream)
    return plain(x_tokens, sign_bits, weight, upstream)


def solution(mesh):
    in_specs = (P("dp", "tensor"), P("tensor"), P("tensor", "dp"), P("tensor", "dp"))
    out_specs = (P("tensor", "dp"), P("tensor", "dp"))
    return jax.shard_map(
        per_device, mesh=mesh, in_specs=in_specs, out_specs=out_specs, check_vma=False
    )
```

```python
import functools
import math

import jax
import jax.numpy as jnp
from jax import lax
from jax.experimental import pallas as pl
from jax.experimental.pallas import tpu as pltpu
from jax.sharding import PartitionSpec as P

MIB = 1 << 20
VMEM = pl.BlockSpec(memory_space=pltpu.VMEM)


def hadamard(order):
    row_ids = jnp.arange(order, dtype=jnp.int32)[:, None]
    col_ids = jnp.arange(order, dtype=jnp.int32)[None, :]
    common = row_ids & col_ids
    parity = jnp.zeros((order, order), jnp.int32)
    for section_bit in range(max(order.bit_length() - 1, 0)):
        parity = parity + (common >> section_bit & 1)
    return (1 - 2 * (parity % 2)).astype(jnp.bfloat16)


def swap(block, axis, mask):
    count = lax.axis_size(axis)
    return lax.ppermute(
        block, axis, [(i, i ^ mask) for i in range(count) if i ^ mask < count]
    )


def plain(x_tokens, sign_bits, weight, upstream):
    panel_width = x_tokens.shape[1]
    groups = lax.axis_size("tensor")
    factor = 1.0 / math.sqrt(panel_width * groups)
    column_sign = (1 - 2 * sign_bits).astype(jnp.bfloat16)
    current = jnp.dot(
        x_tokens * column_sign[None, :],
        hadamard(panel_width),
        preferred_element_type=jnp.float32,
    )
    position = lax.axis_index("tensor")
    for section_bit in range(groups.bit_length() - 1):
        partner = swap(current.astype(jnp.bfloat16), "tensor", 1 << section_bit).astype(
            current.dtype
        )
        upper_half = position >> section_bit & 1 == 1
        current = jnp.where(upper_half, partner - current, current + partner)
    quantized = (current * factor).astype(jnp.bfloat16)
    gathered = lax.all_gather(quantized, "dp", axis=0, tiled=True)
    projected = lax.psum_scatter(
        jnp.dot(gathered, weight, preferred_element_type=jnp.float32).astype(jnp.bfloat16),
        "tensor",
        scatter_dimension=0,
        tiled=True,
    )
    weight_grad = lax.dot_general(
        gathered,
        lax.all_gather(upstream, "tensor", axis=0, tiled=True),
        (((0,), (0,)), ((), ())),
        preferred_element_type=jnp.float32,
    )
    return (projected, weight_grad)


def parity_sign(bits):
    return (1 - 2 * ((bits ^ bits >> 1) & 1)).astype(jnp.float32)


def butterfly(parts):
    stride = 1
    parts = list(parts)
    while stride < len(parts):
        for low in range(len(parts)):
            if not low & stride:
                a, b = parts[low], parts[low | stride]
                parts[low], parts[low | stride] = a + b, a - b
        stride *= 2
    return parts


def whole(shape):
    return pl.BlockSpec(shape, lambda n: (0,) * len(shape))


def tile_of(width, first=0):
    return next((t for t in (512, 256, 128) if width % t == 0 and first % t == 0), width)


def after(arrays, *earlier):
    arrays = list(arrays)
    return list(lax.optimization_barrier(tuple(arrays) + tuple(earlier))[: len(arrays)])


def sign_kernel(x_ref, bits_ref, *outs):
    z = lax.axis_index("tensor")
    rows = outs[0].shape[0]
    sign = (1 - 2 * bits_ref[...]).astype(jnp.float32)
    for m, out in enumerate(outs):
        first = pl.multiple_of((z ^ m) * rows, rows)
        out[...] = (x_ref[pl.ds(first, rows), :].astype(jnp.float32) * sign).astype(out.dtype)


def signed_pieces(x, sign_bits, groups):
    rows, width = x.shape
    part = rows // groups
    return pl.pallas_call(
        sign_kernel,
        out_shape=[jax.ShapeDtypeStruct((part, width), jnp.bfloat16)] * groups,
        in_specs=[VMEM] * 2,
        out_specs=[VMEM] * groups,
        compiler_params=pltpu.CompilerParams(vmem_limit_bytes=8 * MIB),
        name="signed_pieces",
    )(x, sign_bits.reshape(1, width))


def rotate_kernel(groups, order, factor, h_ref, *refs):
    pieces, outs = refs[:groups], refs[groups:]
    z = lax.axis_index("tensor")
    rows, width = pieces[0].shape
    chunks = width // order
    stacked = jnp.concatenate(
        [piece[:, j * order : (j + 1) * order] for piece in pieces for j in range(chunks)], axis=0
    )
    product = jnp.dot(stacked, h_ref[...], preferred_element_type=jnp.float32)
    rotated = []
    for i in range(groups):
        sign = parity_sign(z & i)
        rotated.append(
            butterfly(
                [
                    product[(i * chunks + j) * rows : (i * chunks + j + 1) * rows] * sign
                    for j in range(chunks)
                ]
            )
        )
    for j in range(chunks):
        panel = butterfly([r[j] for r in rotated])
        for m in range(groups):
            scale = parity_sign((z ^ m) & z) * factor
            outs[m][:, j * order : (j + 1) * order] = (panel[m] * scale).astype(jnp.bfloat16)


def rotate(pieces):
    groups = len(pieces)
    rows, width = pieces[0].shape
    order = min(256, width)
    return pl.pallas_call(
        functools.partial(rotate_kernel, groups, order, 1.0 / math.sqrt(width * groups)),
        out_shape=[jax.ShapeDtypeStruct((rows, width), jnp.bfloat16)] * groups,
        in_specs=[VMEM] * (1 + groups),
        out_specs=[VMEM] * groups,
        compiler_params=pltpu.CompilerParams(vmem_limit_bytes=8 * MIB),
        name="rotate",
    )(hadamard(order), *pieces)


def gather_rows(own, d):
    x, y, core = swap(own, "dp", 2), swap(own, "dp", 4), swap(own, "dp", 1)
    x, y = after([x, y])
    through = jnp.where(d & 1 == 0, x, y)
    diagonal = lax.ppermute(
        through, "dp", [(i, i ^ (4 if i & 1 == 0 else 2)) for i in range(8)]
    )
    return [
        own,
        core,
        x,
        swap(x, "dp", 1),
        y,
        swap(y, "dp", 1),
        diagonal,
        swap(diagonal, "dp", 1),
    ]


def is_outer(z):
    return 1 - ((z ^ z >> 1) & 1)


def slot(m, z):
    return m ^ (m >> 1 & is_outer(z))


def first_kernel(*refs):
    pieces, (w_ref, q_ref, *out_refs, sems) = refs[:8], refs[8:]
    rows = pieces[0].shape[0]

    @pl.when(pl.program_id(0) == 0)
    def _():
        z, d = lax.axis_index("tensor"), lax.axis_index("dp")
        copies = []
        for mask, piece in enumerate(pieces):
            start = slot(((d ^ mask) >> 1) ^ z, z) * (2 * rows) + ((d ^ mask) & 1) * rows
            copies.append(
                pltpu.make_async_copy(
                    piece, q_ref.at[pl.ds(pl.multiple_of(start, rows), rows), :], sems.at[mask]
                )
            )
        for copy in copies:
            copy.start()
        for copy in copies:
            copy.wait()

    project_kernel(q_ref, w_ref, *out_refs)


def project_kernel(q_ref, w_ref, *out_refs):
    product = jnp.dot(q_ref[...], w_ref[...], preferred_element_type=jnp.float32)
    first = 0
    for out_ref in out_refs:
        rows = out_ref.shape[0]
        out_ref[...] = product[first : first + rows].astype(out_ref.dtype)
        first += rows


def project_first(pieces, weight, width, blocks):
    depth = weight.shape[0]
    tokens = sum(blocks)
    tile = tile_of(width)
    q, *products = pl.pallas_call(
        first_kernel,
        out_shape=[
            jax.ShapeDtypeStruct((tokens, depth), jnp.bfloat16),
            *[jax.ShapeDtypeStruct((block, width), jnp.bfloat16) for block in blocks],
        ],
        grid=(width // tile,),
        in_specs=[pl.BlockSpec(memory_space=pl.ANY)] * len(pieces)
        + [pl.BlockSpec((depth, tile), lambda n: (0, n))],
        out_specs=[whole((tokens, depth))]
        + [pl.BlockSpec((block, tile), lambda n: (0, n)) for block in blocks],
        scratch_shapes=[pltpu.SemaphoreType.DMA((len(pieces),))],
        compiler_params=pltpu.CompilerParams(vmem_limit_bytes=48 * MIB),
        cost_estimate=pl.CostEstimate(flops=1, bytes_accessed=1, transcendentals=0),
        name="project_first",
    )(*pieces, weight)
    return q, products


def project(q, weight, first, width, blocks):
    tile = tile_of(width, first)
    tokens, depth = q.shape
    return pl.pallas_call(
        project_kernel,
        out_shape=[jax.ShapeDtypeStruct((block, width), jnp.bfloat16) for block in blocks],
        grid=(width // tile,),
        in_specs=[
            whole((tokens, depth)),
            pl.BlockSpec((depth, tile), lambda n: (0, n + first // tile)),
        ],
        out_specs=[pl.BlockSpec((block, tile), lambda n: (0, n)) for block in blocks],
        compiler_params=pltpu.CompilerParams(vmem_limit_bytes=48 * MIB),
        cost_estimate=pl.CostEstimate(
            flops=2 * tokens * depth * width,
            bytes_accessed=2 * (tokens * depth + depth * width + tokens * width),
            transcendentals=0,
        ),
        name="project",
    )(q, weight)


def transpose_kernel(q_ref, out_ref):
    out_ref[...] = q_ref[...].T


def transposed(q):
    tokens, depth = q.shape
    return pl.pallas_call(
        transpose_kernel,
        out_shape=jax.ShapeDtypeStruct((depth, tokens), jnp.bfloat16),
        in_specs=[VMEM],
        out_specs=VMEM,
        compiler_params=pltpu.CompilerParams(vmem_limit_bytes=16 * MIB),
        name="transposed",
    )(q)


def grad_kernel(tile, start, q_t, own_ref, e1, o1, o2, e2, e3, *refs):
    out_ref, up_all, sems = refs[-3:]
    z = lax.axis_index("tensor")
    rows, width = own_ref.shape[0], up_all.shape[1]

    @pl.when(pl.program_id(0) == 0)
    def _():
        def copy(source, m):
            return pltpu.make_async_copy(
                source.at[:, start : start + width],
                up_all.at[m * rows : (m + 1) * rows, :],
                sems.at[m],
            )

        copy(own_ref, 0).start()
        copy(e1, 1).start()

        @pl.when(is_outer(z) == 0)
        def _():
            copy(o2, 2).start()
            copy(o1, 3).start()

        @pl.when(is_outer(z) == 1)
        def _():
            copy(e3, 2).start()
            copy(e2, 3).start()

        for m in range(4):
            copy(own_ref, m).wait()

    first = pl.multiple_of(pl.program_id(0) * tile, tile)
    out_ref[...] = jnp.dot(
        q_t[...], up_all[:, pl.ds(first, tile)], preferred_element_type=jnp.float32
    )


def weight_gradient(q_t, own, moved, start, width, done=None):
    depth, tokens = q_t.shape
    hidden = own.shape[1]
    tile = tile_of(width, start)
    before = [] if done is None else [done]
    anywhere = pl.BlockSpec(memory_space=pl.ANY)
    return pl.pallas_call(
        functools.partial(grad_kernel, tile, start),
        out_shape=jax.ShapeDtypeStruct((depth, hidden), jnp.float32),
        grid=(width // tile,),
        in_specs=[whole((depth, tokens))] + [anywhere] * (6 + len(before)),
        out_specs=pl.BlockSpec((depth, tile), lambda n: (0, n + start // tile)),
        input_output_aliases={7: 0} if before else {},
        scratch_shapes=[
            pltpu.VMEM((tokens, width), jnp.bfloat16),
            pltpu.SemaphoreType.DMA((4,)),
        ],
        compiler_params=pltpu.CompilerParams(vmem_limit_bytes=28 * MIB),
        cost_estimate=pl.CostEstimate(
            flops=5 * tokens * depth * width,
            bytes_accessed=2 * tokens * (depth + width) + 4 * depth * width,
            transcendentals=0,
        ),
        name="weight_gradient",
    )(q_t, own, *moved, *before)


def total(*blocks):
    return sum(b.astype(jnp.float32) for b in blocks).astype(jnp.bfloat16)


def move(block, *pairs):
    return lax.ppermute(block, "tensor", pairs)


INWARD = ((0, 1), (3, 2))
MIDDLE = ((1, 2), (2, 1))
OUTWARD = ((1, 0), (2, 3))


def lined(x_tokens, sign_bits, weight, upstream):
    groups = lax.axis_size("tensor")
    z = lax.axis_index("tensor")
    d = lax.axis_index("dp")
    rows = x_tokens.shape[0]
    hidden = weight.shape[1]

    pieces = list(signed_pieces(x_tokens, sign_bits, groups))
    for m in (3, 2, 1):
        pieces[m] = swap(pieces[m], "tensor", m)
    turned = list(rotate(pieces))
    (up,) = after([upstream], turned[0])
    for m in (3, 2, 1):
        turned[m] = swap(turned[m], "tensor", m)
    own = jnp.concatenate(
        [lax.select_n(z, *[turned[g ^ k] for k in range(groups)]) for g in range(groups)]
    )

    e1 = swap(up, "tensor", 1)
    o1 = move(up, *MIDDLE)

    gathered = gather_rows(own, d)
    cut = 3 * hidden // 7 // 512 * 512
    block = rows * len(gathered) // groups
    q, *first = project_first(gathered, weight, cut, (block, block, 2 * block))
    own_a, pair_a, beyond_a = first[0]
    q, e1, o1 = after([q, e1, o1])
    o2 = move(e1, *MIDDLE)
    e2 = move(o1, *OUTWARD)
    own_b, pair_b, far_b, near_b = project(q, weight, cut, hidden - cut, (block,) * 4)

    inward_a = move(beyond_a, *INWARD)
    inward_far = move(far_b, *INWARD)
    (inward_near,) = after([near_b], inward_a)
    inward_near = move(inward_near, *INWARD)
    across_a = move(total(beyond_a, inward_a), *MIDDLE)
    o2, e2 = after([o2, e2], inward_a)
    e3 = move(o2, *OUTWARD)
    inward_far, o2, e2 = after([inward_far, o2, e2])
    across_far = move(total(far_b, inward_far), *MIDDLE)
    across_a, e3 = after([across_a, e3])
    out_a = swap(total(pair_a, across_a[:block]), "tensor", 1)

    (late,) = after([q], inward_far)
    q_t = transposed(late)
    moved = (e1, o1, o2, e2, e3)
    some = hidden // 2 // 512 * 512
    (late,) = after([q_t], across_a, inward_near)
    grad = weight_gradient(late, upstream, moved, 0, some)

    across_near = move(total(near_b, inward_near), *MIDDLE)
    across_far, grad, out_a = after([across_far, grad, out_a])
    out_b = swap(total(pair_b, across_far), "tensor", 1)
    (late,) = after([q_t], across_far)
    weight_grad = weight_gradient(late, upstream, moved, some, hidden - some, grad)
    projected = jnp.concatenate(
        [total(own_a, out_a, across_a[block:]), total(own_b, out_b, across_near)], axis=1
    )
    return (projected, weight_grad)


def per_device(x_tokens, sign_bits, weight, upstream):
    rows, width = x_tokens.shape
    hidden = weight.shape[1]
    fits = rows % 64 == 0 and width % 256 == 0 and hidden % 512 == 0 and hidden >= 1536
    if (lax.axis_size("dp"), lax.axis_size("tensor")) == (8, 4) and fits:
        return lined(x_tokens, sign_bits, weight, upstream)
    return plain(x_tokens, sign_bits, weight, upstream)


def solution(mesh):
    in_specs = (P("dp", "tensor"), P("tensor"), P("tensor", "dp"), P("tensor", "dp"))
    out_specs = (P("tensor", "dp"), P("tensor", "dp"))
    return jax.shard_map(
        per_device, mesh=mesh, in_specs=in_specs, out_specs=out_specs, check_vma=False
    )
```

```python
import functools
import math

import jax
import jax.numpy as jnp
from jax import lax
from jax.experimental import pallas as pl
from jax.experimental.pallas import tpu as pltpu
from jax.sharding import PartitionSpec as P

MIB = 1 << 20
VMEM = pl.BlockSpec(memory_space=pltpu.VMEM)


def hadamard(order):
    row_ids = jnp.arange(order, dtype=jnp.int32)[:, None]
    col_ids = jnp.arange(order, dtype=jnp.int32)[None, :]
    common = row_ids & col_ids
    parity = jnp.zeros((order, order), jnp.int32)
    for section_bit in range(max(order.bit_length() - 1, 0)):
        parity = parity + (common >> section_bit & 1)
    return (1 - 2 * (parity % 2)).astype(jnp.bfloat16)


def swap(block, axis, mask):
    count = lax.axis_size(axis)
    return lax.ppermute(
        block, axis, [(i, i ^ mask) for i in range(count) if i ^ mask < count]
    )


def plain(x_tokens, sign_bits, weight, upstream):
    panel_width = x_tokens.shape[1]
    groups = lax.axis_size("tensor")
    factor = 1.0 / math.sqrt(panel_width * groups)
    column_sign = (1 - 2 * sign_bits).astype(jnp.bfloat16)
    current = jnp.dot(
        x_tokens * column_sign[None, :],
        hadamard(panel_width),
        preferred_element_type=jnp.float32,
    )
    position = lax.axis_index("tensor")
    for section_bit in range(groups.bit_length() - 1):
        partner = swap(current.astype(jnp.bfloat16), "tensor", 1 << section_bit).astype(
            current.dtype
        )
        upper_half = position >> section_bit & 1 == 1
        current = jnp.where(upper_half, partner - current, current + partner)
    quantized = (current * factor).astype(jnp.bfloat16)
    gathered = lax.all_gather(quantized, "dp", axis=0, tiled=True)
    projected = lax.psum_scatter(
        jnp.dot(gathered, weight, preferred_element_type=jnp.float32).astype(jnp.bfloat16),
        "tensor",
        scatter_dimension=0,
        tiled=True,
    )
    weight_grad = lax.dot_general(
        gathered,
        lax.all_gather(upstream, "tensor", axis=0, tiled=True),
        (((0,), (0,)), ((), ())),
        preferred_element_type=jnp.float32,
    )
    return (projected, weight_grad)


def parity_sign(bits):
    return (1 - 2 * ((bits ^ bits >> 1) & 1)).astype(jnp.float32)


def butterfly(parts):
    stride = 1
    parts = list(parts)
    while stride < len(parts):
        for low in range(len(parts)):
            if not low & stride:
                a, b = parts[low], parts[low | stride]
                parts[low], parts[low | stride] = a + b, a - b
        stride *= 2
    return parts


def whole(shape):
    return pl.BlockSpec(shape, lambda n: (0,) * len(shape))


def tile_of(width, first=0):
    return next((t for t in (512, 256, 128) if width % t == 0 and first % t == 0), width)


def after(arrays, *earlier):
    arrays = list(arrays)
    return list(lax.optimization_barrier(tuple(arrays) + tuple(earlier))[: len(arrays)])


def sign_kernel(x_ref, bits_ref, *outs):
    z = lax.axis_index("tensor")
    rows = outs[0].shape[0]
    sign = (1 - 2 * bits_ref[...]).astype(jnp.float32)
    for m, out in enumerate(outs):
        first = pl.multiple_of((z ^ m) * rows, rows)
        out[...] = (x_ref[pl.ds(first, rows), :].astype(jnp.float32) * sign).astype(out.dtype)


def signed_pieces(x, sign_bits, groups):
    rows, width = x.shape
    part = rows // groups
    return pl.pallas_call(
        sign_kernel,
        out_shape=[jax.ShapeDtypeStruct((part, width), jnp.bfloat16)] * groups,
        in_specs=[VMEM] * 2,
        out_specs=[VMEM] * groups,
        compiler_params=pltpu.CompilerParams(vmem_limit_bytes=8 * MIB),
        name="signed_pieces",
    )(x, sign_bits.reshape(1, width))


def rotate_kernel(groups, order, factor, h_ref, *refs):
    pieces, outs = refs[:groups], refs[groups:]
    z = lax.axis_index("tensor")
    rows, width = pieces[0].shape
    chunks = width // order
    stacked = jnp.concatenate(
        [piece[:, j * order : (j + 1) * order] for piece in pieces for j in range(chunks)], axis=0
    )
    product = jnp.dot(stacked, h_ref[...], preferred_element_type=jnp.float32)
    rotated = []
    for i in range(groups):
        sign = parity_sign(z & i)
        rotated.append(
            butterfly(
                [
                    product[(i * chunks + j) * rows : (i * chunks + j + 1) * rows] * sign
                    for j in range(chunks)
                ]
            )
        )
    for j in range(chunks):
        panel = butterfly([r[j] for r in rotated])
        for m in range(groups):
            scale = parity_sign((z ^ m) & z) * factor
            outs[m][:, j * order : (j + 1) * order] = (panel[m] * scale).astype(jnp.bfloat16)


def rotate(pieces):
    groups = len(pieces)
    rows, width = pieces[0].shape
    order = min(256, width)
    return pl.pallas_call(
        functools.partial(rotate_kernel, groups, order, 1.0 / math.sqrt(width * groups)),
        out_shape=[jax.ShapeDtypeStruct((rows, width), jnp.bfloat16)] * groups,
        in_specs=[VMEM] * (1 + groups),
        out_specs=[VMEM] * groups,
        compiler_params=pltpu.CompilerParams(vmem_limit_bytes=8 * MIB),
        name="rotate",
    )(hadamard(order), *pieces)


def gather_rows(own, d):
    x, y, core = swap(own, "dp", 2), swap(own, "dp", 4), swap(own, "dp", 1)
    x, y = after([x, y])
    through = jnp.where(d & 1 == 0, x, y)
    diagonal = lax.ppermute(
        through, "dp", [(i, i ^ (4 if i & 1 == 0 else 2)) for i in range(8)]
    )
    return [
        own,
        core,
        x,
        swap(x, "dp", 1),
        y,
        swap(y, "dp", 1),
        diagonal,
        swap(diagonal, "dp", 1),
    ]


def is_outer(z):
    return 1 - ((z ^ z >> 1) & 1)


def slot(m, z):
    return m ^ (m >> 1 & is_outer(z))


def first_kernel(*refs):
    pieces, (w_ref, q_ref, *out_refs, sems) = refs[:8], refs[8:]
    rows = pieces[0].shape[0]

    @pl.when(pl.program_id(0) == 0)
    def _():
        z, d = lax.axis_index("tensor"), lax.axis_index("dp")
        copies = []
        for mask, piece in enumerate(pieces):
            start = slot(((d ^ mask) >> 1) ^ z, z) * (2 * rows) + ((d ^ mask) & 1) * rows
            copies.append(
                pltpu.make_async_copy(
                    piece, q_ref.at[pl.ds(pl.multiple_of(start, rows), rows), :], sems.at[mask]
                )
            )
        for copy in copies:
            copy.start()
        for copy in copies:
            copy.wait()

    project_kernel(q_ref, w_ref, *out_refs)


def project_kernel(q_ref, w_ref, *out_refs):
    product = jnp.dot(q_ref[...], w_ref[...], preferred_element_type=jnp.float32)
    first = 0
    for out_ref in out_refs:
        rows = out_ref.shape[0]
        out_ref[...] = product[first : first + rows].astype(out_ref.dtype)
        first += rows


def project_first(pieces, weight, width, blocks):
    depth = weight.shape[0]
    tokens = sum(blocks)
    tile = tile_of(width)
    q, *products = pl.pallas_call(
        first_kernel,
        out_shape=[
            jax.ShapeDtypeStruct((tokens, depth), jnp.bfloat16),
            *[jax.ShapeDtypeStruct((block, width), jnp.bfloat16) for block in blocks],
        ],
        grid=(width // tile,),
        in_specs=[pl.BlockSpec(memory_space=pl.ANY)] * len(pieces)
        + [pl.BlockSpec((depth, tile), lambda n: (0, n))],
        out_specs=[whole((tokens, depth))]
        + [pl.BlockSpec((block, tile), lambda n: (0, n)) for block in blocks],
        scratch_shapes=[pltpu.SemaphoreType.DMA((len(pieces),))],
        compiler_params=pltpu.CompilerParams(vmem_limit_bytes=48 * MIB),
        cost_estimate=pl.CostEstimate(flops=1, bytes_accessed=1, transcendentals=0),
        name="project_first",
    )(*pieces, weight)
    return q, products


def project(q, weight, first, width, blocks):
    tile = tile_of(width, first)
    tokens, depth = q.shape
    return pl.pallas_call(
        project_kernel,
        out_shape=[jax.ShapeDtypeStruct((block, width), jnp.bfloat16) for block in blocks],
        grid=(width // tile,),
        in_specs=[
            whole((tokens, depth)),
            pl.BlockSpec((depth, tile), lambda n: (0, n + first // tile)),
        ],
        out_specs=[pl.BlockSpec((block, tile), lambda n: (0, n)) for block in blocks],
        compiler_params=pltpu.CompilerParams(vmem_limit_bytes=48 * MIB),
        cost_estimate=pl.CostEstimate(
            flops=2 * tokens * depth * width,
            bytes_accessed=2 * (tokens * depth + depth * width + tokens * width),
            transcendentals=0,
        ),
        name="project",
    )(q, weight)


def transpose_kernel(q_ref, out_ref):
    out_ref[...] = q_ref[...].T


def transposed(q):
    tokens, depth = q.shape
    return pl.pallas_call(
        transpose_kernel,
        out_shape=jax.ShapeDtypeStruct((depth, tokens), jnp.bfloat16),
        in_specs=[VMEM],
        out_specs=VMEM,
        compiler_params=pltpu.CompilerParams(vmem_limit_bytes=16 * MIB),
        name="transposed",
    )(q)


def grad_kernel(tile, start, q_t, own_ref, e1, o1, o2, e2, e3, *refs):
    out_ref, up_all, sems = refs[-3:]
    z = lax.axis_index("tensor")
    rows, width = own_ref.shape[0], up_all.shape[1]

    @pl.when(pl.program_id(0) == 0)
    def _():
        def copy(source, m):
            return pltpu.make_async_copy(
                source.at[:, start : start + width],
                up_all.at[m * rows : (m + 1) * rows, :],
                sems.at[m],
            )

        copy(own_ref, 0).start()
        copy(e1, 1).start()

        @pl.when(is_outer(z) == 0)
        def _():
            copy(o2, 2).start()
            copy(o1, 3).start()

        @pl.when(is_outer(z) == 1)
        def _():
            copy(e3, 2).start()
            copy(e2, 3).start()

        for m in range(4):
            copy(own_ref, m).wait()

    first = pl.multiple_of(pl.program_id(0) * tile, tile)
    out_ref[...] = jnp.dot(
        q_t[...], up_all[:, pl.ds(first, tile)], preferred_element_type=jnp.float32
    )


def weight_gradient(q_t, own, moved, start, width, done=None):
    depth, tokens = q_t.shape
    hidden = own.shape[1]
    tile = tile_of(width, start)
    before = [] if done is None else [done]
    anywhere = pl.BlockSpec(memory_space=pl.ANY)
    return pl.pallas_call(
        functools.partial(grad_kernel, tile, start),
        out_shape=jax.ShapeDtypeStruct((depth, hidden), jnp.float32),
        grid=(width // tile,),
        in_specs=[whole((depth, tokens))] + [anywhere] * (6 + len(before)),
        out_specs=pl.BlockSpec((depth, tile), lambda n: (0, n + start // tile)),
        input_output_aliases={7: 0} if before else {},
        scratch_shapes=[
            pltpu.VMEM((tokens, width), jnp.bfloat16),
            pltpu.SemaphoreType.DMA((4,)),
        ],
        compiler_params=pltpu.CompilerParams(vmem_limit_bytes=28 * MIB),
        cost_estimate=pl.CostEstimate(
            flops=5 * tokens * depth * width,
            bytes_accessed=2 * tokens * (depth + width) + 4 * depth * width,
            transcendentals=0,
        ),
        name="weight_gradient",
    )(q_t, own, *moved, *before)


def early_kernel(tile, q_t, own_ref, e1, o1, e2, out_ref, near, far, sems):
    z = lax.axis_index("tensor")
    rows, width = far.shape

    def copy(source, place, n):
        return pltpu.make_async_copy(source.at[:, :width], place, sems.at[n])

    copy(own_ref, near.at[:rows, :], 0).start()
    copy(e1, near.at[rows:, :], 1).start()

    @pl.when(is_outer(z) == 0)
    def _():
        copy(o1, far, 2).start()

    @pl.when(is_outer(z) == 1)
    def _():
        copy(e2, far, 2).start()

    copy(own_ref, near.at[:rows, :], 0).wait()
    copy(e1, near.at[rows:, :], 1).wait()
    copy(o1, far, 2).wait()

    @pl.loop(0, width // tile)
    def _(n):
        columns = pl.ds(pl.multiple_of(n * tile, tile), tile)
        out_ref[:, columns] = jnp.dot(
            q_t[:, : 2 * rows], near[:, columns], preferred_element_type=jnp.float32
        ) + jnp.dot(q_t[:, 3 * rows :], far[:, columns], preferred_element_type=jnp.float32)


def gradient_early(q_t, own, e1, o1, e2, width):
    depth, tokens = q_t.shape
    rows = own.shape[0]
    anywhere = pl.BlockSpec(memory_space=pl.ANY)
    return pl.pallas_call(
        functools.partial(early_kernel, tile_of(width)),
        out_shape=jax.ShapeDtypeStruct((depth, width), jnp.float32),
        in_specs=[VMEM] + [anywhere] * 4,
        out_specs=VMEM,
        scratch_shapes=[
            pltpu.VMEM((2 * rows, width), jnp.bfloat16),
            pltpu.VMEM((rows, width), jnp.bfloat16),
            pltpu.SemaphoreType.DMA((3,)),
        ],
        compiler_params=pltpu.CompilerParams(vmem_limit_bytes=20 * MIB),
        cost_estimate=pl.CostEstimate(flops=1, bytes_accessed=1, transcendentals=0),
        name="gradient_early",
    )(q_t, own, e1, o1, e2)


def late_kernel(tile, early, q_t, o2, e3, out_ref, third, sem):
    z = lax.axis_index("tensor")
    rows, width = third.shape

    @pl.when(pl.program_id(0) == 0)
    def _():
        @pl.when(is_outer(z) == 0)
        def _():
            pltpu.make_async_copy(o2.at[:, :width], third, sem).start()

        @pl.when(is_outer(z) == 1)
        def _():
            pltpu.make_async_copy(e3.at[:, :width], third, sem).start()

        pltpu.make_async_copy(o2.at[:, :width], third, sem).wait()

    columns = pl.ds(pl.multiple_of(pl.program_id(0) * tile, tile), tile)
    out_ref[...] = early[:, columns] + jnp.dot(
        q_t[:, 2 * rows : 3 * rows], third[:, columns], preferred_element_type=jnp.float32
    )


def gradient_late(early, q_t, o2, e3):
    depth, width = early.shape
    rows, hidden = o2.shape
    tile = tile_of(width)
    anywhere = pl.BlockSpec(memory_space=pl.ANY)
    return pl.pallas_call(
        functools.partial(late_kernel, tile),
        out_shape=jax.ShapeDtypeStruct((depth, hidden), jnp.float32),
        grid=(width // tile,),
        in_specs=[VMEM, VMEM, anywhere, anywhere],
        out_specs=pl.BlockSpec((depth, tile), lambda n: (0, n)),
        scratch_shapes=[pltpu.VMEM((rows, width), jnp.bfloat16), pltpu.SemaphoreType.DMA],
        compiler_params=pltpu.CompilerParams(vmem_limit_bytes=16 * MIB),
        cost_estimate=pl.CostEstimate(
            flops=12 * rows * depth * width,
            bytes_accessed=4 * depth * width,
            transcendentals=0,
        ),
        name="gradient_late",
    )(early, q_t, o2, e3)


def total(*blocks):
    return sum(b.astype(jnp.float32) for b in blocks).astype(jnp.bfloat16)


def move(block, *pairs):
    return lax.ppermute(block, "tensor", pairs)


INWARD = ((0, 1), (3, 2))
MIDDLE = ((1, 2), (2, 1))
OUTWARD = ((1, 0), (2, 3))


def lined(x_tokens, sign_bits, weight, upstream):
    groups = lax.axis_size("tensor")
    z = lax.axis_index("tensor")
    d = lax.axis_index("dp")
    rows = x_tokens.shape[0]
    hidden = weight.shape[1]

    pieces = list(signed_pieces(x_tokens, sign_bits, groups))
    for m in (3, 2, 1):
        pieces[m] = swap(pieces[m], "tensor", m)
    turned = list(rotate(pieces))
    (up,) = after([upstream], turned[0])
    for m in (3, 2, 1):
        turned[m] = swap(turned[m], "tensor", m)
    own = jnp.concatenate(
        [lax.select_n(z, *[turned[g ^ k] for k in range(groups)]) for g in range(groups)]
    )

    e1 = swap(up, "tensor", 1)
    o1 = move(up, *MIDDLE)

    gathered = gather_rows(own, d)
    cut = 3 * hidden // 7 // 512 * 512
    block = rows * len(gathered) // groups
    q, *first = project_first(gathered, weight, cut, (block, block, 2 * block))
    own_a, pair_a, beyond_a = first[0]
    q, e1, o1 = after([q, e1, o1])
    o2 = move(e1, *MIDDLE)
    e2 = move(o1, *OUTWARD)
    own_b, pair_b, far_b, near_b = project(q, weight, cut, hidden - cut, (block,) * 4)

    inward_a = move(beyond_a, *INWARD)
    inward_far = move(far_b, *INWARD)
    (inward_near,) = after([near_b], inward_a)
    inward_near = move(inward_near, *INWARD)
    across_a = move(total(beyond_a, inward_a), *MIDDLE)
    o2, e2 = after([o2, e2], inward_a)
    e3 = move(o2, *OUTWARD)
    inward_far, o2, e2 = after([inward_far, o2, e2])
    across_far = move(total(far_b, inward_far), *MIDDLE)
    across_a, e3 = after([across_a, e3])
    out_a = swap(total(pair_a, across_a[:block]), "tensor", 1)

    (late,) = after([q], inward_far)
    q_t = transposed(late)
    moved = (e1, o1, o2, e2, e3)
    some = hidden // 2 // 512 * 512
    early = gradient_early(q_t, upstream, e1, o1, e2, some)
    inward_near, early = after([inward_near, early])
    (late,) = after([q_t], across_a, inward_near)
    grad = gradient_late(early, late, o2, e3)

    across_near = move(total(near_b, inward_near), *MIDDLE)
    across_far, grad, out_a = after([across_far, grad, out_a])
    out_b = swap(total(pair_b, across_far), "tensor", 1)
    (late,) = after([q_t], across_far)
    weight_grad = weight_gradient(late, upstream, moved, some, hidden - some, grad)
    projected = jnp.concatenate(
        [total(own_a, out_a, across_a[block:]), total(own_b, out_b, across_near)], axis=1
    )
    return (projected, weight_grad)


def per_device(x_tokens, sign_bits, weight, upstream):
    rows, width = x_tokens.shape
    hidden = weight.shape[1]
    fits = rows % 64 == 0 and width % 256 == 0 and hidden % 512 == 0 and hidden >= 1536
    if (lax.axis_size("dp"), lax.axis_size("tensor")) == (8, 4) and fits:
        return lined(x_tokens, sign_bits, weight, upstream)
    return plain(x_tokens, sign_bits, weight, upstream)


def solution(mesh):
    in_specs = (P("dp", "tensor"), P("tensor"), P("tensor", "dp"), P("tensor", "dp"))
    out_specs = (P("tensor", "dp"), P("tensor", "dp"))
    return jax.shard_map(
        per_device, mesh=mesh, in_specs=in_specs, out_specs=out_specs, check_vma=False
    )
```

```python
import functools
import math

import jax
import jax.numpy as jnp
from jax import lax
from jax.experimental import pallas as pl
from jax.experimental.pallas import tpu as pltpu
from jax.sharding import PartitionSpec as P

MIB = 1 << 20
VMEM = pl.BlockSpec(memory_space=pltpu.VMEM)


def hadamard(order):
    row_ids = jnp.arange(order, dtype=jnp.int32)[:, None]
    col_ids = jnp.arange(order, dtype=jnp.int32)[None, :]
    common = row_ids & col_ids
    parity = jnp.zeros((order, order), jnp.int32)
    for section_bit in range(max(order.bit_length() - 1, 0)):
        parity = parity + (common >> section_bit & 1)
    return (1 - 2 * (parity % 2)).astype(jnp.bfloat16)


def swap(block, axis, mask):
    count = lax.axis_size(axis)
    return lax.ppermute(
        block, axis, [(i, i ^ mask) for i in range(count) if i ^ mask < count]
    )


def plain(x_tokens, sign_bits, weight, upstream):
    panel_width = x_tokens.shape[1]
    groups = lax.axis_size("tensor")
    factor = 1.0 / math.sqrt(panel_width * groups)
    column_sign = (1 - 2 * sign_bits).astype(jnp.bfloat16)
    current = jnp.dot(
        x_tokens * column_sign[None, :],
        hadamard(panel_width),
        preferred_element_type=jnp.float32,
    )
    position = lax.axis_index("tensor")
    for section_bit in range(groups.bit_length() - 1):
        partner = swap(current.astype(jnp.bfloat16), "tensor", 1 << section_bit).astype(
            current.dtype
        )
        upper_half = position >> section_bit & 1 == 1
        current = jnp.where(upper_half, partner - current, current + partner)
    quantized = (current * factor).astype(jnp.bfloat16)
    gathered = lax.all_gather(quantized, "dp", axis=0, tiled=True)
    projected = lax.psum_scatter(
        jnp.dot(gathered, weight, preferred_element_type=jnp.float32).astype(jnp.bfloat16),
        "tensor",
        scatter_dimension=0,
        tiled=True,
    )
    weight_grad = lax.dot_general(
        gathered,
        lax.all_gather(upstream, "tensor", axis=0, tiled=True),
        (((0,), (0,)), ((), ())),
        preferred_element_type=jnp.float32,
    )
    return (projected, weight_grad)


def parity_sign(bits):
    return (1 - 2 * ((bits ^ bits >> 1) & 1)).astype(jnp.float32)


def butterfly(parts):
    stride = 1
    parts = list(parts)
    while stride < len(parts):
        for low in range(len(parts)):
            if not low & stride:
                a, b = parts[low], parts[low | stride]
                parts[low], parts[low | stride] = a + b, a - b
        stride *= 2
    return parts


def whole(shape):
    return pl.BlockSpec(shape, lambda n: (0,) * len(shape))


def tile_of(width, first=0):
    return next((t for t in (512, 256, 128) if width % t == 0 and first % t == 0), width)


def after(arrays, *earlier):
    arrays = list(arrays)
    return list(lax.optimization_barrier(tuple(arrays) + tuple(earlier))[: len(arrays)])


def sign_kernel(x_ref, bits_ref, *outs):
    z = lax.axis_index("tensor")
    rows = outs[0].shape[0]
    sign = (1 - 2 * bits_ref[...]).astype(jnp.float32)
    for m, out in enumerate(outs):
        first = pl.multiple_of((z ^ m) * rows, rows)
        out[...] = (x_ref[pl.ds(first, rows), :].astype(jnp.float32) * sign).astype(out.dtype)


def signed_pieces(x, sign_bits, groups):
    rows, width = x.shape
    part = rows // groups
    return pl.pallas_call(
        sign_kernel,
        out_shape=[jax.ShapeDtypeStruct((part, width), jnp.bfloat16)] * groups,
        in_specs=[VMEM] * 2,
        out_specs=[VMEM] * groups,
        compiler_params=pltpu.CompilerParams(vmem_limit_bytes=8 * MIB),
        name="signed_pieces",
    )(x, sign_bits.reshape(1, width))


def rotate_kernel(groups, order, factor, h_ref, *refs):
    pieces, outs = refs[:groups], refs[groups:]
    z = lax.axis_index("tensor")
    rows, width = pieces[0].shape
    chunks = width // order
    stacked = jnp.concatenate(
        [piece[:, j * order : (j + 1) * order] for piece in pieces for j in range(chunks)], axis=0
    )
    product = jnp.dot(stacked, h_ref[...], preferred_element_type=jnp.float32)
    rotated = []
    for i in range(groups):
        sign = parity_sign(z & i)
        rotated.append(
            butterfly(
                [
                    product[(i * chunks + j) * rows : (i * chunks + j + 1) * rows] * sign
                    for j in range(chunks)
                ]
            )
        )
    for j in range(chunks):
        panel = butterfly([r[j] for r in rotated])
        for m in range(groups):
            scale = parity_sign((z ^ m) & z) * factor
            outs[m][:, j * order : (j + 1) * order] = (panel[m] * scale).astype(jnp.bfloat16)


def rotate(pieces):
    groups = len(pieces)
    rows, width = pieces[0].shape
    order = min(256, width)
    return pl.pallas_call(
        functools.partial(rotate_kernel, groups, order, 1.0 / math.sqrt(width * groups)),
        out_shape=[jax.ShapeDtypeStruct((rows, width), jnp.bfloat16)] * groups,
        in_specs=[VMEM] * (1 + groups),
        out_specs=[VMEM] * groups,
        compiler_params=pltpu.CompilerParams(vmem_limit_bytes=8 * MIB),
        name="rotate",
    )(hadamard(order), *pieces)


def gather_rows(own, d):
    x, y, core = swap(own, "dp", 2), swap(own, "dp", 4), swap(own, "dp", 1)
    x, y = after([x, y])
    through = jnp.where(d & 1 == 0, x, y)
    diagonal = lax.ppermute(
        through, "dp", [(i, i ^ (4 if i & 1 == 0 else 2)) for i in range(8)]
    )
    return [
        own,
        core,
        x,
        swap(x, "dp", 1),
        y,
        swap(y, "dp", 1),
        diagonal,
        swap(diagonal, "dp", 1),
    ]


def is_outer(z):
    return 1 - ((z ^ z >> 1) & 1)


def slot(m, z):
    return m ^ (m >> 1 & is_outer(z))


def first_kernel(*refs):
    pieces, (w_ref, q_ref, *out_refs, sems) = refs[:8], refs[8:]
    rows = pieces[0].shape[0]

    @pl.when(pl.program_id(0) == 0)
    def _():
        z, d = lax.axis_index("tensor"), lax.axis_index("dp")
        copies = []
        for mask, piece in enumerate(pieces):
            start = slot(((d ^ mask) >> 1) ^ z, z) * (2 * rows) + ((d ^ mask) & 1) * rows
            copies.append(
                pltpu.make_async_copy(
                    piece, q_ref.at[pl.ds(pl.multiple_of(start, rows), rows), :], sems.at[mask]
                )
            )
        for copy in copies:
            copy.start()
        for copy in copies:
            copy.wait()

    project_kernel(q_ref, w_ref, *out_refs)


def project_kernel(q_ref, w_ref, *out_refs):
    product = jnp.dot(q_ref[...], w_ref[...], preferred_element_type=jnp.float32)
    first = 0
    for out_ref in out_refs:
        rows = out_ref.shape[0]
        out_ref[...] = product[first : first + rows].astype(out_ref.dtype)
        first += rows


def project_first(pieces, weight, width, blocks):
    depth = weight.shape[0]
    tokens = sum(blocks)
    tile = tile_of(width)
    q, *products = pl.pallas_call(
        first_kernel,
        out_shape=[
            jax.ShapeDtypeStruct((tokens, depth), jnp.bfloat16),
            *[jax.ShapeDtypeStruct((block, width), jnp.bfloat16) for block in blocks],
        ],
        grid=(width // tile,),
        in_specs=[pl.BlockSpec(memory_space=pl.ANY)] * len(pieces)
        + [pl.BlockSpec((depth, tile), lambda n: (0, n))],
        out_specs=[whole((tokens, depth))]
        + [pl.BlockSpec((block, tile), lambda n: (0, n)) for block in blocks],
        scratch_shapes=[pltpu.SemaphoreType.DMA((len(pieces),))],
        compiler_params=pltpu.CompilerParams(vmem_limit_bytes=48 * MIB),
        cost_estimate=pl.CostEstimate(flops=1, bytes_accessed=1, transcendentals=0),
        name="project_first",
    )(*pieces, weight)
    return q, products


def project(q, weight, first, width, blocks):
    tile = tile_of(width, first)
    tokens, depth = q.shape
    return pl.pallas_call(
        project_kernel,
        out_shape=[jax.ShapeDtypeStruct((block, width), jnp.bfloat16) for block in blocks],
        grid=(width // tile,),
        in_specs=[
            whole((tokens, depth)),
            pl.BlockSpec((depth, tile), lambda n: (0, n + first // tile)),
        ],
        out_specs=[pl.BlockSpec((block, tile), lambda n: (0, n)) for block in blocks],
        compiler_params=pltpu.CompilerParams(vmem_limit_bytes=48 * MIB),
        cost_estimate=pl.CostEstimate(
            flops=20 * tokens * depth * width,
            bytes_accessed=2 * (tokens * depth + depth * width + tokens * width),
            transcendentals=0,
        ),
        name="project",
    )(q, weight)


def transpose_kernel(q_ref, out_ref):
    out_ref[...] = q_ref[...].T


def transposed(q):
    tokens, depth = q.shape
    return pl.pallas_call(
        transpose_kernel,
        out_shape=jax.ShapeDtypeStruct((depth, tokens), jnp.bfloat16),
        in_specs=[VMEM],
        out_specs=VMEM,
        compiler_params=pltpu.CompilerParams(vmem_limit_bytes=16 * MIB),
        name="transposed",
    )(q)


def grad_kernel(tile, start, q_t, own_ref, e1, o1, o2, e2, e3, *refs):
    out_ref, up_all, sems = refs[-3:]
    z = lax.axis_index("tensor")
    rows, width = own_ref.shape[0], up_all.shape[1]

    @pl.when(pl.program_id(0) == 0)
    def _():
        def copy(source, m):
            return pltpu.make_async_copy(
                source.at[:, start : start + width],
                up_all.at[m * rows : (m + 1) * rows, :],
                sems.at[m],
            )

        copy(own_ref, 0).start()
        copy(e1, 1).start()

        @pl.when(is_outer(z) == 0)
        def _():
            copy(o2, 2).start()
            copy(o1, 3).start()

        @pl.when(is_outer(z) == 1)
        def _():
            copy(e3, 2).start()
            copy(e2, 3).start()

        for m in range(4):
            copy(own_ref, m).wait()

    first = pl.multiple_of(pl.program_id(0) * tile, tile)
    out_ref[...] = jnp.dot(
        q_t[...], up_all[:, pl.ds(first, tile)], preferred_element_type=jnp.float32
    )


def weight_gradient(q_t, own, moved, start, width, done=None):
    depth, tokens = q_t.shape
    hidden = own.shape[1]
    tile = tile_of(width, start)
    before = [] if done is None else [done]
    anywhere = pl.BlockSpec(memory_space=pl.ANY)
    return pl.pallas_call(
        functools.partial(grad_kernel, tile, start),
        out_shape=jax.ShapeDtypeStruct((depth, hidden), jnp.float32),
        grid=(width // tile,),
        in_specs=[whole((depth, tokens))] + [anywhere] * (6 + len(before)),
        out_specs=pl.BlockSpec((depth, tile), lambda n: (0, n + start // tile)),
        input_output_aliases={7: 0} if before else {},
        scratch_shapes=[
            pltpu.VMEM((tokens, width), jnp.bfloat16),
            pltpu.SemaphoreType.DMA((4,)),
        ],
        compiler_params=pltpu.CompilerParams(vmem_limit_bytes=28 * MIB),
        cost_estimate=pl.CostEstimate(
            flops=5 * tokens * depth * width,
            bytes_accessed=2 * tokens * (depth + width) + 4 * depth * width,
            transcendentals=0,
        ),
        name="weight_gradient",
    )(q_t, own, *moved, *before)


def early_kernel(tile, q_t, own_ref, e1, o1, e2, out_ref, near, far, sems):
    z = lax.axis_index("tensor")
    rows, width = far.shape

    def copy(source, place, n):
        return pltpu.make_async_copy(source.at[:, :width], place, sems.at[n])

    copy(own_ref, near.at[:rows, :], 0).start()
    copy(e1, near.at[rows:, :], 1).start()

    @pl.when(is_outer(z) == 0)
    def _():
        copy(o1, far, 2).start()

    @pl.when(is_outer(z) == 1)
    def _():
        copy(e2, far, 2).start()

    copy(own_ref, near.at[:rows, :], 0).wait()
    copy(e1, near.at[rows:, :], 1).wait()
    copy(o1, far, 2).wait()

    @pl.loop(0, width // tile)
    def _(n):
        columns = pl.ds(pl.multiple_of(n * tile, tile), tile)
        out_ref[:, columns] = jnp.dot(
            q_t[:, : 2 * rows], near[:, columns], preferred_element_type=jnp.float32
        ) + jnp.dot(q_t[:, 3 * rows :], far[:, columns], preferred_element_type=jnp.float32)


def gradient_early(q_t, own, e1, o1, e2, width):
    depth, tokens = q_t.shape
    rows = own.shape[0]
    anywhere = pl.BlockSpec(memory_space=pl.ANY)
    return pl.pallas_call(
        functools.partial(early_kernel, tile_of(width)),
        out_shape=jax.ShapeDtypeStruct((depth, width), jnp.float32),
        in_specs=[VMEM] + [anywhere] * 4,
        out_specs=VMEM,
        scratch_shapes=[
            pltpu.VMEM((2 * rows, width), jnp.bfloat16),
            pltpu.VMEM((rows, width), jnp.bfloat16),
            pltpu.SemaphoreType.DMA((3,)),
        ],
        compiler_params=pltpu.CompilerParams(vmem_limit_bytes=20 * MIB),
        cost_estimate=pl.CostEstimate(flops=1, bytes_accessed=1, transcendentals=0),
        name="gradient_early",
    )(q_t, own, e1, o1, e2)


def late_kernel(tile, early, q_t, o2, e3, out_ref, third, sem):
    z = lax.axis_index("tensor")
    rows, width = third.shape

    @pl.when(pl.program_id(0) == 0)
    def _():
        @pl.when(is_outer(z) == 0)
        def _():
            pltpu.make_async_copy(o2.at[:, :width], third, sem).start()

        @pl.when(is_outer(z) == 1)
        def _():
            pltpu.make_async_copy(e3.at[:, :width], third, sem).start()

        pltpu.make_async_copy(o2.at[:, :width], third, sem).wait()

    columns = pl.ds(pl.multiple_of(pl.program_id(0) * tile, tile), tile)
    out_ref[...] = early[:, columns] + jnp.dot(
        q_t[:, 2 * rows : 3 * rows], third[:, columns], preferred_element_type=jnp.float32
    )


def gradient_late(early, q_t, o2, e3):
    depth, width = early.shape
    rows, hidden = o2.shape
    tile = tile_of(width)
    anywhere = pl.BlockSpec(memory_space=pl.ANY)
    return pl.pallas_call(
        functools.partial(late_kernel, tile),
        out_shape=jax.ShapeDtypeStruct((depth, hidden), jnp.float32),
        grid=(width // tile,),
        in_specs=[VMEM, VMEM, anywhere, anywhere],
        out_specs=pl.BlockSpec((depth, tile), lambda n: (0, n)),
        scratch_shapes=[pltpu.VMEM((rows, width), jnp.bfloat16), pltpu.SemaphoreType.DMA],
        compiler_params=pltpu.CompilerParams(vmem_limit_bytes=16 * MIB),
        cost_estimate=pl.CostEstimate(
            flops=24 * rows * depth * width,
            bytes_accessed=4 * depth * width,
            transcendentals=0,
        ),
        name="gradient_late",
    )(early, q_t, o2, e3)


def total(*blocks):
    return sum(b.astype(jnp.float32) for b in blocks).astype(jnp.bfloat16)


def move(block, *pairs):
    return lax.ppermute(block, "tensor", pairs)


INWARD = ((0, 1), (3, 2))
MIDDLE = ((1, 2), (2, 1))
OUTWARD = ((1, 0), (2, 3))


def lined(x_tokens, sign_bits, weight, upstream):
    groups = lax.axis_size("tensor")
    z = lax.axis_index("tensor")
    d = lax.axis_index("dp")
    rows = x_tokens.shape[0]
    hidden = weight.shape[1]

    pieces = list(signed_pieces(x_tokens, sign_bits, groups))
    for m in (3, 2, 1):
        pieces[m] = swap(pieces[m], "tensor", m)
    turned = list(rotate(pieces))
    (up,) = after([upstream], turned[0])
    for m in (3, 2, 1):
        turned[m] = swap(turned[m], "tensor", m)
    own = jnp.concatenate(
        [lax.select_n(z, *[turned[g ^ k] for k in range(groups)]) for g in range(groups)]
    )

    e1 = swap(up, "tensor", 1)
    o1 = move(up, *MIDDLE)

    gathered = gather_rows(own, d)
    cut = (hidden // 512 + 1) // 2 * 512
    block = rows * len(gathered) // groups
    q, *first = project_first(gathered, weight, cut, (block, block, 2 * block))
    own_a, pair_a, beyond_a = first[0]
    q, e1, o1 = after([q, e1, o1])
    o2 = move(e1, *MIDDLE)
    e2 = move(o1, *OUTWARD)
    own_b, pair_b, far_b, near_b = project(q, weight, cut, hidden - cut, (block,) * 4)

    inward_a = move(beyond_a, *INWARD)
    inward_a, own_b = after([inward_a, own_b])
    inward_far = move(far_b, *INWARD)
    (inward_near,) = after([near_b], inward_a)
    inward_near = move(inward_near, *INWARD)
    across_a = move(total(beyond_a, inward_a), *MIDDLE)
    o2, e2 = after([o2, e2], inward_a)
    e3 = move(o2, *OUTWARD)
    inward_far, o2, e2 = after([inward_far, o2, e2])
    across_far = move(total(far_b, inward_far), *MIDDLE)
    across_a, e3 = after([across_a, e3])
    out_a = swap(total(pair_a, across_a[:block]), "tensor", 1)

    (late,) = after([q], inward_far)
    q_t = transposed(late)
    moved = (e1, o1, o2, e2, e3)
    some = hidden // 2 // 512 * 512
    early = gradient_early(q_t, upstream, e1, o1, e2, some)
    inward_near, early = after([inward_near, early])
    (late,) = after([q_t], across_a, inward_near)
    grad = gradient_late(early, late, o2, e3)

    across_near = move(total(near_b, inward_near), *MIDDLE)
    across_far, grad, out_a = after([across_far, grad, out_a])
    out_b = swap(total(pair_b, across_far), "tensor", 1)
    (late,) = after([q_t], across_far)
    weight_grad = weight_gradient(late, upstream, moved, some, hidden - some, grad)
    projected = jnp.concatenate(
        [total(own_a, out_a, across_a[block:]), total(own_b, out_b, across_near)], axis=1
    )
    return (projected, weight_grad)


def per_device(x_tokens, sign_bits, weight, upstream):
    rows, width = x_tokens.shape
    hidden = weight.shape[1]
    fits = rows % 64 == 0 and width % 256 == 0 and hidden % 512 == 0 and hidden >= 1536
    if (lax.axis_size("dp"), lax.axis_size("tensor")) == (8, 4) and fits:
        return lined(x_tokens, sign_bits, weight, upstream)
    return plain(x_tokens, sign_bits, weight, upstream)


def solution(mesh):
    in_specs = (P("dp", "tensor"), P("tensor"), P("tensor", "dp"), P("tensor", "dp"))
    out_specs = (P("tensor", "dp"), P("tensor", "dp"))
    return jax.shard_map(
        per_device, mesh=mesh, in_specs=in_specs, out_specs=out_specs, check_vma=False
    )
```

```python
import functools
import math

import jax
import jax.numpy as jnp
from jax import lax
from jax.experimental import pallas as pl
from jax.experimental.pallas import tpu as pltpu
from jax.sharding import PartitionSpec as P

MIB = 1 << 20
VMEM = pl.BlockSpec(memory_space=pltpu.VMEM)


def hadamard(order):
    row_ids = jnp.arange(order, dtype=jnp.int32)[:, None]
    col_ids = jnp.arange(order, dtype=jnp.int32)[None, :]
    common = row_ids & col_ids
    parity = jnp.zeros((order, order), jnp.int32)
    for section_bit in range(max(order.bit_length() - 1, 0)):
        parity = parity + (common >> section_bit & 1)
    return (1 - 2 * (parity % 2)).astype(jnp.bfloat16)


def swap(block, axis, mask):
    count = lax.axis_size(axis)
    return lax.ppermute(
        block, axis, [(i, i ^ mask) for i in range(count) if i ^ mask < count]
    )


def plain(x_tokens, sign_bits, weight, upstream):
    panel_width = x_tokens.shape[1]
    groups = lax.axis_size("tensor")
    factor = 1.0 / math.sqrt(panel_width * groups)
    column_sign = (1 - 2 * sign_bits).astype(jnp.bfloat16)
    current = jnp.dot(
        x_tokens * column_sign[None, :],
        hadamard(panel_width),
        preferred_element_type=jnp.float32,
    )
    position = lax.axis_index("tensor")
    for section_bit in range(groups.bit_length() - 1):
        partner = swap(current.astype(jnp.bfloat16), "tensor", 1 << section_bit).astype(
            current.dtype
        )
        upper_half = position >> section_bit & 1 == 1
        current = jnp.where(upper_half, partner - current, current + partner)
    quantized = (current * factor).astype(jnp.bfloat16)
    gathered = lax.all_gather(quantized, "dp", axis=0, tiled=True)
    projected = lax.psum_scatter(
        jnp.dot(gathered, weight, preferred_element_type=jnp.float32).astype(jnp.bfloat16),
        "tensor",
        scatter_dimension=0,
        tiled=True,
    )
    weight_grad = lax.dot_general(
        gathered,
        lax.all_gather(upstream, "tensor", axis=0, tiled=True),
        (((0,), (0,)), ((), ())),
        preferred_element_type=jnp.float32,
    )
    return (projected, weight_grad)


def parity_sign(bits):
    return (1 - 2 * ((bits ^ bits >> 1) & 1)).astype(jnp.float32)


def butterfly(parts):
    stride = 1
    parts = list(parts)
    while stride < len(parts):
        for low in range(len(parts)):
            if not low & stride:
                a, b = parts[low], parts[low | stride]
                parts[low], parts[low | stride] = a + b, a - b
        stride *= 2
    return parts


def whole(shape):
    return pl.BlockSpec(shape, lambda n: (0,) * len(shape))


def tile_of(width, first=0):
    return next((t for t in (512, 256, 128) if width % t == 0 and first % t == 0), width)


def after(arrays, *earlier):
    arrays = list(arrays)
    return list(lax.optimization_barrier(tuple(arrays) + tuple(earlier))[: len(arrays)])


def sign_kernel(x_ref, bits_ref, *outs):
    z = lax.axis_index("tensor")
    rows = outs[0].shape[0]
    sign = (1 - 2 * bits_ref[...]).astype(jnp.float32)
    for m, out in enumerate(outs):
        first = pl.multiple_of((z ^ m) * rows, rows)
        out[...] = (x_ref[pl.ds(first, rows), :].astype(jnp.float32) * sign).astype(out.dtype)


def signed_pieces(x, sign_bits, groups):
    rows, width = x.shape
    part = rows // groups
    return pl.pallas_call(
        sign_kernel,
        out_shape=[jax.ShapeDtypeStruct((part, width), jnp.bfloat16)] * groups,
        in_specs=[VMEM] * 2,
        out_specs=[VMEM] * groups,
        compiler_params=pltpu.CompilerParams(vmem_limit_bytes=8 * MIB),
        name="signed_pieces",
    )(x, sign_bits.reshape(1, width))


def rotate_kernel(groups, order, factor, h_ref, *refs):
    pieces, outs = refs[:groups], refs[groups:]
    z = lax.axis_index("tensor")
    rows, width = pieces[0].shape
    chunks = width // order
    stacked = jnp.concatenate(
        [piece[:, j * order : (j + 1) * order] for piece in pieces for j in range(chunks)], axis=0
    )
    product = jnp.dot(stacked, h_ref[...], preferred_element_type=jnp.float32)
    rotated = []
    for i in range(groups):
        sign = parity_sign(z & i)
        rotated.append(
            butterfly(
                [
                    product[(i * chunks + j) * rows : (i * chunks + j + 1) * rows] * sign
                    for j in range(chunks)
                ]
            )
        )
    for j in range(chunks):
        panel = butterfly([r[j] for r in rotated])
        for m in range(groups):
            scale = parity_sign((z ^ m) & z) * factor
            outs[m][:, j * order : (j + 1) * order] = (panel[m] * scale).astype(jnp.bfloat16)


def rotate(pieces):
    groups = len(pieces)
    rows, width = pieces[0].shape
    order = min(256, width)
    return pl.pallas_call(
        functools.partial(rotate_kernel, groups, order, 1.0 / math.sqrt(width * groups)),
        out_shape=[jax.ShapeDtypeStruct((rows, width), jnp.bfloat16)] * groups,
        in_specs=[VMEM] * (1 + groups),
        out_specs=[VMEM] * groups,
        compiler_params=pltpu.CompilerParams(vmem_limit_bytes=8 * MIB),
        name="rotate",
    )(hadamard(order), *pieces)


def gather_rows(own, d):
    x, y, core = swap(own, "dp", 2), swap(own, "dp", 4), swap(own, "dp", 1)
    x, y = after([x, y])
    through = jnp.where(d & 1 == 0, x, y)
    diagonal = lax.ppermute(
        through, "dp", [(i, i ^ (4 if i & 1 == 0 else 2)) for i in range(8)]
    )
    return [
        own,
        core,
        x,
        swap(x, "dp", 1),
        y,
        swap(y, "dp", 1),
        diagonal,
        swap(diagonal, "dp", 1),
    ]


def is_outer(z):
    return 1 - ((z ^ z >> 1) & 1)


def slot(m, z):
    return m ^ (m >> 1 & is_outer(z))


def first_kernel(*refs):
    pieces, (w_ref, q_ref, *out_refs, sems) = refs[:8], refs[8:]
    rows = pieces[0].shape[0]

    @pl.when(pl.program_id(0) == 0)
    def _():
        z, d = lax.axis_index("tensor"), lax.axis_index("dp")
        copies = []
        for mask, piece in enumerate(pieces):
            start = slot(((d ^ mask) >> 1) ^ z, z) * (2 * rows) + ((d ^ mask) & 1) * rows
            copies.append(
                pltpu.make_async_copy(
                    piece, q_ref.at[pl.ds(pl.multiple_of(start, rows), rows), :], sems.at[mask]
                )
            )
        for copy in copies:
            copy.start()
        for copy in copies:
            copy.wait()

    project_kernel(q_ref, w_ref, *out_refs)


def project_kernel(q_ref, w_ref, *out_refs):
    product = jnp.dot(q_ref[...], w_ref[...], preferred_element_type=jnp.float32)
    first = 0
    for out_ref in out_refs:
        rows = out_ref.shape[0]
        out_ref[...] = product[first : first + rows].astype(out_ref.dtype)
        first += rows


def project_first(pieces, weight, width, blocks):
    depth = weight.shape[0]
    tokens = sum(blocks)
    tile = tile_of(width)
    q, *products = pl.pallas_call(
        first_kernel,
        out_shape=[
            jax.ShapeDtypeStruct((tokens, depth), jnp.bfloat16),
            *[jax.ShapeDtypeStruct((block, width), jnp.bfloat16) for block in blocks],
        ],
        grid=(width // tile,),
        in_specs=[pl.BlockSpec(memory_space=pl.ANY)] * len(pieces)
        + [pl.BlockSpec((depth, tile), lambda n: (0, n))],
        out_specs=[whole((tokens, depth))]
        + [pl.BlockSpec((block, tile), lambda n: (0, n)) for block in blocks],
        scratch_shapes=[pltpu.SemaphoreType.DMA((len(pieces),))],
        compiler_params=pltpu.CompilerParams(vmem_limit_bytes=48 * MIB),
        cost_estimate=pl.CostEstimate(flops=1, bytes_accessed=1, transcendentals=0),
        name="project_first",
    )(*pieces, weight)
    return q, products


def project(q, weight, first, width, blocks):
    tile = tile_of(width, first)
    tokens, depth = q.shape
    return pl.pallas_call(
        project_kernel,
        out_shape=[jax.ShapeDtypeStruct((block, width), jnp.bfloat16) for block in blocks],
        grid=(width // tile,),
        in_specs=[
            whole((tokens, depth)),
            pl.BlockSpec((depth, tile), lambda n: (0, n + first // tile)),
        ],
        out_specs=[pl.BlockSpec((block, tile), lambda n: (0, n)) for block in blocks],
        compiler_params=pltpu.CompilerParams(vmem_limit_bytes=48 * MIB),
        cost_estimate=pl.CostEstimate(
            flops=2 * tokens * depth * width,
            bytes_accessed=2 * (tokens * depth + depth * width + tokens * width),
            transcendentals=0,
        ),
        name="project",
    )(q, weight)


def transpose_kernel(q_ref, out_ref):
    out_ref[...] = q_ref[...].T


def transposed(q):
    tokens, depth = q.shape
    return pl.pallas_call(
        transpose_kernel,
        out_shape=jax.ShapeDtypeStruct((depth, tokens), jnp.bfloat16),
        in_specs=[VMEM],
        out_specs=VMEM,
        compiler_params=pltpu.CompilerParams(vmem_limit_bytes=16 * MIB),
        name="transposed",
    )(q)


def grad_kernel(tile, start, q_t, own_ref, e1, o1, o2, e2, e3, *refs):
    out_ref, up_all, sems = refs[-3:]
    z = lax.axis_index("tensor")
    rows, width = own_ref.shape[0], up_all.shape[1]

    @pl.when(pl.program_id(0) == 0)
    def _():
        def copy(source, m):
            return pltpu.make_async_copy(
                source.at[:, start : start + width],
                up_all.at[m * rows : (m + 1) * rows, :],
                sems.at[m],
            )

        copy(own_ref, 0).start()
        copy(e1, 1).start()

        @pl.when(is_outer(z) == 0)
        def _():
            copy(o2, 2).start()
            copy(o1, 3).start()

        @pl.when(is_outer(z) == 1)
        def _():
            copy(e3, 2).start()
            copy(e2, 3).start()

        for m in range(4):
            copy(own_ref, m).wait()

    first = pl.multiple_of(pl.program_id(0) * tile, tile)
    out_ref[...] = jnp.dot(
        q_t[...], up_all[:, pl.ds(first, tile)], preferred_element_type=jnp.float32
    )


def weight_gradient(q_t, own, moved, start, width, done=None):
    depth, tokens = q_t.shape
    hidden = own.shape[1]
    tile = tile_of(width, start)
    before = [] if done is None else [done]
    anywhere = pl.BlockSpec(memory_space=pl.ANY)
    return pl.pallas_call(
        functools.partial(grad_kernel, tile, start),
        out_shape=jax.ShapeDtypeStruct((depth, hidden), jnp.float32),
        grid=(width // tile,),
        in_specs=[whole((depth, tokens))] + [anywhere] * (6 + len(before)),
        out_specs=pl.BlockSpec((depth, tile), lambda n: (0, n + start // tile)),
        input_output_aliases={7: 0} if before else {},
        scratch_shapes=[
            pltpu.VMEM((tokens, width), jnp.bfloat16),
            pltpu.SemaphoreType.DMA((4,)),
        ],
        compiler_params=pltpu.CompilerParams(vmem_limit_bytes=28 * MIB),
        cost_estimate=pl.CostEstimate(
            flops=5 * tokens * depth * width,
            bytes_accessed=2 * tokens * (depth + width) + 4 * depth * width,
            transcendentals=0,
        ),
        name="weight_gradient",
    )(q_t, own, *moved, *before)


def early_kernel(tile, q_t, own_ref, e1, o1, e2, out_ref, near, far, sems):
    z = lax.axis_index("tensor")
    rows, width = far.shape

    def copy(source, place, n):
        return pltpu.make_async_copy(source.at[:, :width], place, sems.at[n])

    copy(own_ref, near.at[:rows, :], 0).start()
    copy(e1, near.at[rows:, :], 1).start()

    @pl.when(is_outer(z) == 0)
    def _():
        copy(o1, far, 2).start()

    @pl.when(is_outer(z) == 1)
    def _():
        copy(e2, far, 2).start()

    copy(own_ref, near.at[:rows, :], 0).wait()
    copy(e1, near.at[rows:, :], 1).wait()
    copy(o1, far, 2).wait()

    @pl.loop(0, width // tile)
    def _(n):
        columns = pl.ds(pl.multiple_of(n * tile, tile), tile)
        out_ref[:, columns] = jnp.dot(
            q_t[:, : 2 * rows], near[:, columns], preferred_element_type=jnp.float32
        ) + jnp.dot(q_t[:, 3 * rows :], far[:, columns], preferred_element_type=jnp.float32)


def gradient_early(q_t, own, e1, o1, e2, width):
    depth, tokens = q_t.shape
    rows = own.shape[0]
    anywhere = pl.BlockSpec(memory_space=pl.ANY)
    return pl.pallas_call(
        functools.partial(early_kernel, tile_of(width)),
        out_shape=jax.ShapeDtypeStruct((depth, width), jnp.float32),
        in_specs=[VMEM] + [anywhere] * 4,
        out_specs=VMEM,
        scratch_shapes=[
            pltpu.VMEM((2 * rows, width), jnp.bfloat16),
            pltpu.VMEM((rows, width), jnp.bfloat16),
            pltpu.SemaphoreType.DMA((3,)),
        ],
        compiler_params=pltpu.CompilerParams(vmem_limit_bytes=20 * MIB),
        cost_estimate=pl.CostEstimate(flops=1, bytes_accessed=1, transcendentals=0),
        name="gradient_early",
    )(q_t, own, e1, o1, e2)


def late_kernel(tile, early, q_t, o2, e3, out_ref, third, sem):
    z = lax.axis_index("tensor")
    rows, width = third.shape

    @pl.when(pl.program_id(0) == 0)
    def _():
        @pl.when(is_outer(z) == 0)
        def _():
            pltpu.make_async_copy(o2.at[:, :width], third, sem).start()

        @pl.when(is_outer(z) == 1)
        def _():
            pltpu.make_async_copy(e3.at[:, :width], third, sem).start()

        pltpu.make_async_copy(o2.at[:, :width], third, sem).wait()

    columns = pl.ds(pl.multiple_of(pl.program_id(0) * tile, tile), tile)
    out_ref[...] = early[:, columns] + jnp.dot(
        q_t[:, 2 * rows : 3 * rows], third[:, columns], preferred_element_type=jnp.float32
    )


def gradient_late(early, q_t, o2, e3):
    depth, width = early.shape
    rows, hidden = o2.shape
    tile = tile_of(width)
    anywhere = pl.BlockSpec(memory_space=pl.ANY)
    return pl.pallas_call(
        functools.partial(late_kernel, tile),
        out_shape=jax.ShapeDtypeStruct((depth, hidden), jnp.float32),
        grid=(width // tile,),
        in_specs=[VMEM, VMEM, anywhere, anywhere],
        out_specs=pl.BlockSpec((depth, tile), lambda n: (0, n)),
        scratch_shapes=[pltpu.VMEM((rows, width), jnp.bfloat16), pltpu.SemaphoreType.DMA],
        compiler_params=pltpu.CompilerParams(vmem_limit_bytes=16 * MIB),
        cost_estimate=pl.CostEstimate(
            flops=12 * rows * depth * width,
            bytes_accessed=4 * depth * width,
            transcendentals=0,
        ),
        name="gradient_late",
    )(early, q_t, o2, e3)


def total(*blocks):
    return sum(b.astype(jnp.float32) for b in blocks).astype(jnp.bfloat16)


def move(block, *pairs):
    return lax.ppermute(block, "tensor", pairs)


INWARD = ((0, 1), (3, 2))
MIDDLE = ((1, 2), (2, 1))
OUTWARD = ((1, 0), (2, 3))


def lined(x_tokens, sign_bits, weight, upstream):
    groups = lax.axis_size("tensor")
    z = lax.axis_index("tensor")
    d = lax.axis_index("dp")
    rows = x_tokens.shape[0]
    hidden = weight.shape[1]

    pieces = list(signed_pieces(x_tokens, sign_bits, groups))
    for m in (3, 2, 1):
        pieces[m] = swap(pieces[m], "tensor", m)
    turned = list(rotate(pieces))
    (up,) = after([upstream], turned[0])
    for m in (3, 2, 1):
        turned[m] = swap(turned[m], "tensor", m)
    own = jnp.concatenate(
        [lax.select_n(z, *[turned[g ^ k] for k in range(groups)]) for g in range(groups)]
    )

    e1 = swap(up, "tensor", 1)
    o1 = move(up, *MIDDLE)

    gathered = gather_rows(own, d)
    cut = 2 * hidden // 7 // 512 * 512
    block = rows * len(gathered) // groups
    q, *first = project_first(gathered, weight, cut, (block, block, 2 * block))
    own_a, pair_a, beyond_a = first[0]
    q, e1, o1 = after([q, e1, o1])
    o2 = move(e1, *MIDDLE)
    e2 = move(o1, *OUTWARD)
    own_b, pair_b, far_b, near_b = project(q, weight, cut, hidden - cut, (block,) * 4)

    inward_a = move(beyond_a, *INWARD)
    inward_far = move(far_b, *INWARD)
    (inward_near,) = after([near_b], inward_a)
    inward_near = move(inward_near, *INWARD)
    across_a = move(total(beyond_a, inward_a), *MIDDLE)
    o2, e2 = after([o2, e2], inward_a)
    e3 = move(o2, *OUTWARD)
    inward_far, o2, e2 = after([inward_far, o2, e2])
    across_far = move(total(far_b, inward_far), *MIDDLE)
    across_a, e3 = after([across_a, e3])
    out_a = swap(total(pair_a, across_a[:block]), "tensor", 1)

    (late,) = after([q], inward_far)
    q_t = transposed(late)
    moved = (e1, o1, o2, e2, e3)
    some = hidden // 2 // 512 * 512
    early = gradient_early(q_t, upstream, e1, o1, e2, some)
    inward_near, early = after([inward_near, early])
    (late,) = after([q_t], across_a, inward_near)
    grad = gradient_late(early, late, o2, e3)

    across_near = move(total(near_b, inward_near), *MIDDLE)
    across_far, grad, out_a = after([across_far, grad, out_a])
    out_b = swap(total(pair_b, across_far), "tensor", 1)
    (late,) = after([q_t], across_far)
    weight_grad = weight_gradient(late, upstream, moved, some, hidden - some, grad)
    projected = jnp.concatenate(
        [total(own_a, out_a, across_a[block:]), total(own_b, out_b, across_near)], axis=1
    )
    return (projected, weight_grad)


def per_device(x_tokens, sign_bits, weight, upstream):
    rows, width = x_tokens.shape
    hidden = weight.shape[1]
    fits = rows % 64 == 0 and width % 256 == 0 and hidden % 512 == 0 and hidden >= 1536
    if (lax.axis_size("dp"), lax.axis_size("tensor")) == (8, 4) and fits:
        return lined(x_tokens, sign_bits, weight, upstream)
    return plain(x_tokens, sign_bits, weight, upstream)


def solution(mesh):
    in_specs = (P("dp", "tensor"), P("tensor"), P("tensor", "dp"), P("tensor", "dp"))
    out_specs = (P("tensor", "dp"), P("tensor", "dp"))
    return jax.shard_map(
        per_device, mesh=mesh, in_specs=in_specs, out_specs=out_specs, check_vma=False
    )
```

```python
import functools
import math

import jax
import jax.numpy as jnp
from jax import lax
from jax.experimental import pallas as pl
from jax.experimental.pallas import tpu as pltpu
from jax.sharding import PartitionSpec as P

MIB = 1 << 20
VMEM = pl.BlockSpec(memory_space=pltpu.VMEM)


def hadamard(order):
    row_ids = jnp.arange(order, dtype=jnp.int32)[:, None]
    col_ids = jnp.arange(order, dtype=jnp.int32)[None, :]
    common = row_ids & col_ids
    parity = jnp.zeros((order, order), jnp.int32)
    for section_bit in range(max(order.bit_length() - 1, 0)):
        parity = parity + (common >> section_bit & 1)
    return (1 - 2 * (parity % 2)).astype(jnp.bfloat16)


def swap(block, axis, mask):
    count = lax.axis_size(axis)
    return lax.ppermute(
        block, axis, [(i, i ^ mask) for i in range(count) if i ^ mask < count]
    )


def plain(x_tokens, sign_bits, weight, upstream):
    panel_width = x_tokens.shape[1]
    groups = lax.axis_size("tensor")
    factor = 1.0 / math.sqrt(panel_width * groups)
    column_sign = (1 - 2 * sign_bits).astype(jnp.bfloat16)
    current = jnp.dot(
        x_tokens * column_sign[None, :],
        hadamard(panel_width),
        preferred_element_type=jnp.float32,
    )
    position = lax.axis_index("tensor")
    for section_bit in range(groups.bit_length() - 1):
        partner = swap(current.astype(jnp.bfloat16), "tensor", 1 << section_bit).astype(
            current.dtype
        )
        upper_half = position >> section_bit & 1 == 1
        current = jnp.where(upper_half, partner - current, current + partner)
    quantized = (current * factor).astype(jnp.bfloat16)
    gathered = lax.all_gather(quantized, "dp", axis=0, tiled=True)
    projected = lax.psum_scatter(
        jnp.dot(gathered, weight, preferred_element_type=jnp.float32).astype(jnp.bfloat16),
        "tensor",
        scatter_dimension=0,
        tiled=True,
    )
    weight_grad = lax.dot_general(
        gathered,
        lax.all_gather(upstream, "tensor", axis=0, tiled=True),
        (((0,), (0,)), ((), ())),
        preferred_element_type=jnp.float32,
    )
    return (projected, weight_grad)


def parity_sign(bits):
    return (1 - 2 * ((bits ^ bits >> 1) & 1)).astype(jnp.float32)


def butterfly(parts):
    stride = 1
    parts = list(parts)
    while stride < len(parts):
        for low in range(len(parts)):
            if not low & stride:
                a, b = parts[low], parts[low | stride]
                parts[low], parts[low | stride] = a + b, a - b
        stride *= 2
    return parts


def whole(shape):
    return pl.BlockSpec(shape, lambda n: (0,) * len(shape))


def tile_of(width, first=0):
    return next((t for t in (512, 256, 128) if width % t == 0 and first % t == 0), width)


def after(arrays, *earlier):
    arrays = list(arrays)
    return list(lax.optimization_barrier(tuple(arrays) + tuple(earlier))[: len(arrays)])


def sign_kernel(x_ref, bits_ref, *outs):
    z = lax.axis_index("tensor")
    rows = outs[0].shape[0]
    sign = (1 - 2 * bits_ref[...]).astype(jnp.float32)
    for m, out in enumerate(outs):
        first = pl.multiple_of((z ^ m) * rows, rows)
        out[...] = (x_ref[pl.ds(first, rows), :].astype(jnp.float32) * sign).astype(out.dtype)


def signed_pieces(x, sign_bits, groups):
    rows, width = x.shape
    part = rows // groups
    return pl.pallas_call(
        sign_kernel,
        out_shape=[jax.ShapeDtypeStruct((part, width), jnp.bfloat16)] * groups,
        in_specs=[VMEM] * 2,
        out_specs=[VMEM] * groups,
        compiler_params=pltpu.CompilerParams(vmem_limit_bytes=8 * MIB),
        name="signed_pieces",
    )(x, sign_bits.reshape(1, width))


def rotate_kernel(groups, order, factor, h_ref, *refs):
    pieces, outs = refs[:groups], refs[groups:]
    z = lax.axis_index("tensor")
    rows, width = pieces[0].shape
    chunks = width // order
    stacked = jnp.concatenate(
        [piece[:, j * order : (j + 1) * order] for piece in pieces for j in range(chunks)], axis=0
    )
    product = jnp.dot(stacked, h_ref[...], preferred_element_type=jnp.float32)
    rotated = []
    for i in range(groups):
        sign = parity_sign(z & i)
        rotated.append(
            butterfly(
                [
                    product[(i * chunks + j) * rows : (i * chunks + j + 1) * rows] * sign
                    for j in range(chunks)
                ]
            )
        )
    for j in range(chunks):
        panel = butterfly([r[j] for r in rotated])
        for m in range(groups):
            scale = parity_sign((z ^ m) & z) * factor
            outs[m][:, j * order : (j + 1) * order] = (panel[m] * scale).astype(jnp.bfloat16)


def rotate(pieces):
    groups = len(pieces)
    rows, width = pieces[0].shape
    order = min(256, width)
    return pl.pallas_call(
        functools.partial(rotate_kernel, groups, order, 1.0 / math.sqrt(width * groups)),
        out_shape=[jax.ShapeDtypeStruct((rows, width), jnp.bfloat16)] * groups,
        in_specs=[VMEM] * (1 + groups),
        out_specs=[VMEM] * groups,
        compiler_params=pltpu.CompilerParams(vmem_limit_bytes=8 * MIB),
        name="rotate",
    )(hadamard(order), *pieces)


def gather_rows(own, d):
    x, y, core = swap(own, "dp", 2), swap(own, "dp", 4), swap(own, "dp", 1)
    x, y = after([x, y])
    through = jnp.where(d & 1 == 0, x, y)
    diagonal = lax.ppermute(
        through, "dp", [(i, i ^ (4 if i & 1 == 0 else 2)) for i in range(8)]
    )
    return [
        own,
        core,
        x,
        swap(x, "dp", 1),
        y,
        swap(y, "dp", 1),
        diagonal,
        swap(diagonal, "dp", 1),
    ]


def is_outer(z):
    return 1 - ((z ^ z >> 1) & 1)


def slot(m, z):
    return m ^ (m >> 1 & is_outer(z))


def first_kernel(*refs):
    pieces, (w_ref, q_ref, *out_refs, sems) = refs[:8], refs[8:]
    rows = pieces[0].shape[0]

    @pl.when(pl.program_id(0) == 0)
    def _():
        z, d = lax.axis_index("tensor"), lax.axis_index("dp")
        copies = []
        for mask, piece in enumerate(pieces):
            start = slot(((d ^ mask) >> 1) ^ z, z) * (2 * rows) + ((d ^ mask) & 1) * rows
            copies.append(
                pltpu.make_async_copy(
                    piece, q_ref.at[pl.ds(pl.multiple_of(start, rows), rows), :], sems.at[mask]
                )
            )
        for copy in copies:
            copy.start()
        for copy in copies:
            copy.wait()

    project_kernel(q_ref, w_ref, *out_refs)


def project_kernel(q_ref, w_ref, *out_refs):
    product = jnp.dot(q_ref[...], w_ref[...], preferred_element_type=jnp.float32)
    first = 0
    for out_ref in out_refs:
        rows = out_ref.shape[0]
        out_ref[...] = product[first : first + rows].astype(out_ref.dtype)
        first += rows


def project_first(pieces, weight, width, blocks):
    depth = weight.shape[0]
    tokens = sum(blocks)
    tile = tile_of(width)
    q, *products = pl.pallas_call(
        first_kernel,
        out_shape=[
            jax.ShapeDtypeStruct((tokens, depth), jnp.bfloat16),
            *[jax.ShapeDtypeStruct((block, width), jnp.bfloat16) for block in blocks],
        ],
        grid=(width // tile,),
        in_specs=[pl.BlockSpec(memory_space=pl.ANY)] * len(pieces)
        + [pl.BlockSpec((depth, tile), lambda n: (0, n))],
        out_specs=[whole((tokens, depth))]
        + [pl.BlockSpec((block, tile), lambda n: (0, n)) for block in blocks],
        scratch_shapes=[pltpu.SemaphoreType.DMA((len(pieces),))],
        compiler_params=pltpu.CompilerParams(vmem_limit_bytes=48 * MIB),
        cost_estimate=pl.CostEstimate(flops=1, bytes_accessed=1, transcendentals=0),
        name="project_first",
    )(*pieces, weight)
    return q, products


def project(q, weight, first, width, blocks):
    tile = tile_of(width, first)
    tokens, depth = q.shape
    return pl.pallas_call(
        project_kernel,
        out_shape=[jax.ShapeDtypeStruct((block, width), jnp.bfloat16) for block in blocks],
        grid=(width // tile,),
        in_specs=[
            whole((tokens, depth)),
            pl.BlockSpec((depth, tile), lambda n: (0, n + first // tile)),
        ],
        out_specs=[pl.BlockSpec((block, tile), lambda n: (0, n)) for block in blocks],
        compiler_params=pltpu.CompilerParams(vmem_limit_bytes=48 * MIB),
        cost_estimate=pl.CostEstimate(
            flops=2 * tokens * depth * width,
            bytes_accessed=2 * (tokens * depth + depth * width + tokens * width),
            transcendentals=0,
        ),
        name="project",
    )(q, weight)


def transpose_kernel(q_ref, out_ref):
    out_ref[...] = q_ref[...].T


def transposed(q):
    tokens, depth = q.shape
    return pl.pallas_call(
        transpose_kernel,
        out_shape=jax.ShapeDtypeStruct((depth, tokens), jnp.bfloat16),
        in_specs=[VMEM],
        out_specs=VMEM,
        compiler_params=pltpu.CompilerParams(vmem_limit_bytes=16 * MIB),
        name="transposed",
    )(q)


def grad_kernel(tile, start, q_t, own_ref, e1, o1, o2, e2, e3, *refs):
    out_ref, up_all, sems = refs[-3:]
    z = lax.axis_index("tensor")
    rows, width = own_ref.shape[0], up_all.shape[1]

    @pl.when(pl.program_id(0) == 0)
    def _():
        def copy(source, m):
            return pltpu.make_async_copy(
                source.at[:, start : start + width],
                up_all.at[m * rows : (m + 1) * rows, :],
                sems.at[m],
            )

        copy(own_ref, 0).start()
        copy(e1, 1).start()

        @pl.when(is_outer(z) == 0)
        def _():
            copy(o2, 2).start()
            copy(o1, 3).start()

        @pl.when(is_outer(z) == 1)
        def _():
            copy(e3, 2).start()
            copy(e2, 3).start()

        for m in range(4):
            copy(own_ref, m).wait()

    first = pl.multiple_of(pl.program_id(0) * tile, tile)
    out_ref[...] = jnp.dot(
        q_t[...], up_all[:, pl.ds(first, tile)], preferred_element_type=jnp.float32
    )


def weight_gradient(q_t, own, moved, start, width, done=None):
    depth, tokens = q_t.shape
    hidden = own.shape[1]
    tile = tile_of(width, start)
    before = [] if done is None else [done]
    anywhere = pl.BlockSpec(memory_space=pl.ANY)
    return pl.pallas_call(
        functools.partial(grad_kernel, tile, start),
        out_shape=jax.ShapeDtypeStruct((depth, hidden), jnp.float32),
        grid=(width // tile,),
        in_specs=[whole((depth, tokens))] + [anywhere] * (6 + len(before)),
        out_specs=pl.BlockSpec((depth, tile), lambda n: (0, n + start // tile)),
        input_output_aliases={7: 0} if before else {},
        scratch_shapes=[
            pltpu.VMEM((tokens, width), jnp.bfloat16),
            pltpu.SemaphoreType.DMA((4,)),
        ],
        compiler_params=pltpu.CompilerParams(vmem_limit_bytes=28 * MIB),
        cost_estimate=pl.CostEstimate(
            flops=1,
            bytes_accessed=1,
            transcendentals=0,
        ),
        name="weight_gradient",
    )(q_t, own, *moved, *before)


def early_kernel(tile, q_t, own_ref, e1, o1, e2, out_ref, near, far, sems):
    z = lax.axis_index("tensor")
    rows, width = far.shape

    def copy(source, place, n):
        return pltpu.make_async_copy(source.at[:, :width], place, sems.at[n])

    copy(own_ref, near.at[:rows, :], 0).start()
    copy(e1, near.at[rows:, :], 1).start()

    @pl.when(is_outer(z) == 0)
    def _():
        copy(o1, far, 2).start()

    @pl.when(is_outer(z) == 1)
    def _():
        copy(e2, far, 2).start()

    copy(own_ref, near.at[:rows, :], 0).wait()
    copy(e1, near.at[rows:, :], 1).wait()
    copy(o1, far, 2).wait()

    @pl.loop(0, width // tile)
    def _(n):
        columns = pl.ds(pl.multiple_of(n * tile, tile), tile)
        out_ref[:, columns] = jnp.dot(
            q_t[:, : 2 * rows], near[:, columns], preferred_element_type=jnp.float32
        ) + jnp.dot(q_t[:, 3 * rows :], far[:, columns], preferred_element_type=jnp.float32)


def gradient_early(q_t, own, e1, o1, e2, width):
    depth, tokens = q_t.shape
    rows = own.shape[0]
    anywhere = pl.BlockSpec(memory_space=pl.ANY)
    return pl.pallas_call(
        functools.partial(early_kernel, tile_of(width)),
        out_shape=jax.ShapeDtypeStruct((depth, width), jnp.float32),
        in_specs=[VMEM] + [anywhere] * 4,
        out_specs=VMEM,
        scratch_shapes=[
            pltpu.VMEM((2 * rows, width), jnp.bfloat16),
            pltpu.VMEM((rows, width), jnp.bfloat16),
            pltpu.SemaphoreType.DMA((3,)),
        ],
        compiler_params=pltpu.CompilerParams(vmem_limit_bytes=20 * MIB),
        cost_estimate=pl.CostEstimate(flops=1, bytes_accessed=1, transcendentals=0),
        name="gradient_early",
    )(q_t, own, e1, o1, e2)


def late_kernel(tile, early, q_t, o2, e3, out_ref, third, sem):
    z = lax.axis_index("tensor")
    rows, width = third.shape

    @pl.when(pl.program_id(0) == 0)
    def _():
        @pl.when(is_outer(z) == 0)
        def _():
            pltpu.make_async_copy(o2.at[:, :width], third, sem).start()

        @pl.when(is_outer(z) == 1)
        def _():
            pltpu.make_async_copy(e3.at[:, :width], third, sem).start()

        pltpu.make_async_copy(o2.at[:, :width], third, sem).wait()

    columns = pl.ds(pl.multiple_of(pl.program_id(0) * tile, tile), tile)
    out_ref[...] = early[:, columns] + jnp.dot(
        q_t[:, 2 * rows : 3 * rows], third[:, columns], preferred_element_type=jnp.float32
    )


def gradient_late(early, q_t, o2, e3):
    depth, width = early.shape
    rows, hidden = o2.shape
    tile = tile_of(width)
    anywhere = pl.BlockSpec(memory_space=pl.ANY)
    return pl.pallas_call(
        functools.partial(late_kernel, tile),
        out_shape=jax.ShapeDtypeStruct((depth, hidden), jnp.float32),
        grid=(width // tile,),
        in_specs=[VMEM, VMEM, anywhere, anywhere],
        out_specs=pl.BlockSpec((depth, tile), lambda n: (0, n)),
        scratch_shapes=[pltpu.VMEM((rows, width), jnp.bfloat16), pltpu.SemaphoreType.DMA],
        compiler_params=pltpu.CompilerParams(vmem_limit_bytes=16 * MIB),
        cost_estimate=pl.CostEstimate(
            flops=12 * rows * depth * width,
            bytes_accessed=4 * depth * width,
            transcendentals=0,
        ),
        name="gradient_late",
    )(early, q_t, o2, e3)


def total(*blocks):
    return sum(b.astype(jnp.float32) for b in blocks).astype(jnp.bfloat16)


def move(block, *pairs):
    return lax.ppermute(block, "tensor", pairs)


INWARD = ((0, 1), (3, 2))
MIDDLE = ((1, 2), (2, 1))
OUTWARD = ((1, 0), (2, 3))


def lined(x_tokens, sign_bits, weight, upstream):
    groups = lax.axis_size("tensor")
    z = lax.axis_index("tensor")
    d = lax.axis_index("dp")
    rows = x_tokens.shape[0]
    hidden = weight.shape[1]

    pieces = list(signed_pieces(x_tokens, sign_bits, groups))
    for m in (3, 2, 1):
        pieces[m] = swap(pieces[m], "tensor", m)
    turned = list(rotate(pieces))
    (up,) = after([upstream], turned[0])
    for m in (3, 2, 1):
        turned[m] = swap(turned[m], "tensor", m)
    own = jnp.concatenate(
        [lax.select_n(z, *[turned[g ^ k] for k in range(groups)]) for g in range(groups)]
    )

    e1 = swap(up, "tensor", 1)
    o1 = move(up, *MIDDLE)

    gathered = gather_rows(own, d)
    cut = 2 * hidden // 7 // 512 * 512
    block = rows * len(gathered) // groups
    q, *first = project_first(gathered, weight, cut, (block, block, 2 * block))
    own_a, pair_a, beyond_a = first[0]
    q, e1, o1 = after([q, e1, o1])
    o2 = move(e1, *MIDDLE)
    e2 = move(o1, *OUTWARD)
    own_b, pair_b, far_b, near_b = project(q, weight, cut, hidden - cut, (block,) * 4)

    inward_a = move(beyond_a, *INWARD)
    inward_far = move(far_b, *INWARD)
    (inward_near,) = after([near_b], inward_a)
    inward_near = move(inward_near, *INWARD)
    across_a = move(total(beyond_a, inward_a), *MIDDLE)
    o2, e2 = after([o2, e2], inward_a)
    e3 = move(o2, *OUTWARD)
    inward_far, o2, e2 = after([inward_far, o2, e2])
    across_far = move(total(far_b, inward_far), *MIDDLE)
    across_a, e3 = after([across_a, e3])
    out_a = swap(total(pair_a, across_a[:block]), "tensor", 1)

    (late,) = after([q], inward_far)
    q_t = transposed(late)
    moved = (e1, o1, o2, e2, e3)
    some = hidden // 2 // 512 * 512
    early = gradient_early(q_t, upstream, e1, o1, e2, some)
    inward_near, early = after([inward_near, early])
    (late,) = after([q_t], across_a, inward_near)
    grad = gradient_late(early, late, o2, e3)

    across_near = move(total(near_b, inward_near), *MIDDLE)
    across_far, out_a = after([across_far, out_a])
    out_b = swap(total(pair_b, across_far), "tensor", 1)
    late, grad = after([q_t, grad], across_far)
    weight_grad = weight_gradient(late, upstream, moved, some, hidden - some, grad)
    projected = jnp.concatenate(
        [total(own_a, out_a, across_a[block:]), total(own_b, out_b, across_near)], axis=1
    )
    return (projected, weight_grad)


def per_device(x_tokens, sign_bits, weight, upstream):
    rows, width = x_tokens.shape
    hidden = weight.shape[1]
    fits = rows % 64 == 0 and width % 256 == 0 and hidden % 512 == 0 and hidden >= 1536
    if (lax.axis_size("dp"), lax.axis_size("tensor")) == (8, 4) and fits:
        return lined(x_tokens, sign_bits, weight, upstream)
    return plain(x_tokens, sign_bits, weight, upstream)


def solution(mesh):
    in_specs = (P("dp", "tensor"), P("tensor"), P("tensor", "dp"), P("tensor", "dp"))
    out_specs = (P("tensor", "dp"), P("tensor", "dp"))
    return jax.shard_map(
        per_device, mesh=mesh, in_specs=in_specs, out_specs=out_specs, check_vma=False
    )
```
